32 devices in a mesh: dp: 2 (over y), ctx: 16 (over z, x, core).
Axes of the slice: x: 2, y: 2, z: 4, core: 2. Of those that a mesh axis runs over, the one named last changes fastest.
Arguments:
- tokens: bfloat16 [8192, 1024], P(('dp', 'ctx')), may hold values from -6 to 6
- seq_lengths: int32 [2, 4], P('dp'), may hold values from 1 to 2048, 4096 in all within a row
- dealing: int32 [2, 64], P('dp'), may hold values from 0 to 63, as said below
- ln1_gain: bfloat16 [1024], P(('dp', 'ctx')), may hold values from 0.5 to 1.5
- ln1_bias: bfloat16 [1024], P(('dp', 'ctx')), may hold values from -1 to 1
- ln2_gain: bfloat16 [1024], P(('dp', 'ctx')), may hold values from 0.5 to 1.5
- ln2_bias: bfloat16 [1024], P(('dp', 'ctx')), may hold values from -1 to 1
- w_qkv: bfloat16 [1024, 3072], P(('dp', 'ctx')), may hold values from -0.25 to 0.25
- b_qkv: bfloat16 [3072], P(('dp', 'ctx')), may hold values from -1 to 1
- w_out: bfloat16 [1024, 1024], P(('dp', 'ctx')), may hold values from -0.75 to 0.75
- w_in: bfloat16 [1024, 4096], P(('dp', 'ctx')), may hold values from -0.1875 to 0.1875
- b_in: bfloat16 [4096], P(('dp', 'ctx')), may hold values from -2.5 to 2.5
- w_fc2: bfloat16 [4096, 1024], P(('dp', 'ctx')), may hold values from -0.09375 to 0.09375
- b_out: bfloat16 [1024], P(('dp', 'ctx')), may hold values from -1 to 1
- cotangent: bfloat16 [8192, 1024], P(('dp', 'ctx')), may hold values from -6 to 6
Outputs:
- mixed: bfloat16 [8192, 1024], P(('dp', 'ctx'))
- grad_tokens: float32 [8192, 1024], P(('dp', 'ctx'))
- grad_ln1_gain: float32 [1024], P(('dp', 'ctx'))
- grad_ln1_bias: float32 [1024], P(('dp', 'ctx'))
- grad_ln2_gain: float32 [1024], P(('dp', 'ctx'))
- grad_ln2_bias: float32 [1024], P(('dp', 'ctx'))
- grad_w_qkv: float32 [1024, 3072], P(('dp', 'ctx'))
- grad_b_qkv: float32 [3072], P(('dp', 'ctx'))
- grad_w_out: float32 [1024, 1024], P(('dp', 'ctx'))
- grad_w_in: float32 [1024, 4096], P(('dp', 'ctx'))
- grad_b_in: float32 [4096], P(('dp', 'ctx'))
- grad_w_fc2: float32 [4096, 1024], P(('dp', 'ctx'))
- grad_b_out: float32 [1024], P(('dp', 'ctx'))
The draws below stay inside these ranges and needn't reach their ends.
Inputs may be any that keep to these rules, and one draw needn't show every extreme that they name: `seq_lengths`: each row gives, in order, the lengths of the sequences packed into the 4096 places of one group; a row sums to 4096; its largest is exactly 2048. `dealing`: each row names every packed block of 64 places once. Slots are ordered by ctx index and then by local block; the slots at one local place b of all ctx indices hold, in some order, one run of consecutive packed blocks that starts at b times the number of ctx devices.
All inputs are finite; a program needn't handle non-finite values.
Results may differ from the reference program's by a relative error of at most 0.012.
The reference program's roundings to bfloat16 on the way count: a program that leaves them out, or rounds other values in their place, can miss the bound.
Values may be sent and summed in bfloat16 or wider, within the bound.
No kernel may reach another device: no remote copies, remote signals or barrier semaphores. Data moves between devices by JAX's collectives and lax.ppermute only.
A program may use at most 320 MiB of HBM per device.

```python
import math
import jax
import jax.numpy as jnp
import numpy as np
from jax import lax

D = 1024
HEADS = 16
HEAD = 64
ROT = 16
FF = 4096
TOK_DEV = 256
LONGEST = 2048
GROUP = 4096
TOKENS = 8192
BLK = 64
NSEQ = 4
N_DP = 2
N_CTX = 16


def draw_dealing(key, part):
    key = jax.random.fold_in(key, 11)
    rounds = TOK_DEV // BLK
    keys_all = jax.random.split(key, N_DP * rounds)
    orders = jax.vmap(lambda single: jax.random.permutation(single, N_CTX))(keys_all)
    orders = orders.reshape(N_DP, rounds, N_CTX).astype(jnp.int32)
    base = (jnp.arange(rounds, dtype=jnp.int32) * N_CTX)[None, :, None]
    placed = base + orders
    return jnp.transpose(placed, (0, 2, 1)).reshape(N_DP, N_CTX * rounds).astype(jnp.int32)


def levels(own_key, extent, cuts, least, top_value):
    factor_of, own = 1.0, jax.random.fold_in(own_key, 6)
    for axis_at, blocks in cuts:
        steps = jnp.exp(jax.random.uniform(jax.random.fold_in(own, axis_at), (blocks,), jnp.float32, least / len(cuts), top_value / len(cuts)))
        factor_of = factor_of * jnp.repeat(steps, extent[axis_at] // blocks).reshape([-1 if axis == axis_at else 1 for axis in range(len(extent))])
    return factor_of


def split_up(amount, total, reach, slope):
    portions = [(1 << 20) // math.isqrt(rank ** slope) + 1 for rank in range(2, amount + 1)]
    spare, holding = total - reach - (amount - 1), [1] * (amount - 1)
    while spare > 0:
        movable = [i for i in range(amount - 1) if holding[i] < reach]
        mass, remaining = sum([portions[i] for i in movable]), spare
        for i in movable:
            more = min(reach - holding[i], max(1, remaining * portions[i] // mass), spare)
            holding[i] = holding[i] + more
            spare = spare - more
    return np.array([reach] + holding)


def ragged_sizes(own_key, count, total, reach, lean):
    if count == 2:
        one = jax.random.randint(own_key, (), max(1, total - reach), min(reach, total - 1) + 1)
        return jnp.stack([one, total - one])
    tallies = jnp.asarray(split_up(count, total, reach, lean), jnp.int32)
    twos = (count - 1) // 2
    giver, receiver = tallies[1:1 + 2 * twos:2], tallies[2:2 + 2 * twos:2]
    margin = jnp.minimum(giver - 1, reach - receiver)
    passed = jax.random.randint(jax.random.fold_in(own_key, 1), (twos,), 0, 1 << 20) % (margin + 1)
    tallies = tallies.at[1:1 + 2 * twos:2].set(giver - passed).at[2:2 + 2 * twos:2].set(receiver + passed)
    return tallies[jax.random.permutation(jax.random.fold_in(own_key, 2), count)]


def bell_draw(key, dims, deviation, limit, cuts=(), held_as=jnp.bfloat16):
    array = deviation * jax.random.normal(key, dims, jnp.float32)
    if cuts:
        array = array * levels(key, dims, cuts, -0.22, 0.18)
    return jnp.clip(array, -limit, limit).astype(held_as)


def setup_inputs(seed: int = 0) -> dict:
    streams_of = jax.random.split(jax.random.key(seed), 16)
    tokens = bell_draw(streams_of[0], (TOKENS, D), 1.0, 6.0, ((0, 32),))
    seq_lengths = jax.vmap(lambda own: ragged_sizes(own, NSEQ, GROUP, LONGEST, 2))(jax.random.split(streams_of[1], N_DP)).reshape((N_DP, NSEQ)).astype(jnp.int32)
    dealing = draw_dealing(jax.random.fold_in(streams_of[15], 71), 0)
    ln1_gain = jnp.clip(1.0 + 0.1 * jax.random.normal(streams_of[3], (D,), jnp.float32), 0.5, 1.5).astype(jnp.bfloat16)
    ln1_bias = bell_draw(streams_of[4], (D,), 0.2, 1.0, ((0, 32),))
    ln2_gain = jnp.clip(1.0 + 0.1 * jax.random.normal(streams_of[5], (D,), jnp.float32), 0.5, 1.5).astype(jnp.bfloat16)
    ln2_bias = bell_draw(streams_of[6], (D,), 0.2, 1.0, ((0, 32),))
    w_qkv = bell_draw(streams_of[7], (D, 3 * D), (D // 2) ** -0.5, 0.25, ((0, 32),))
    b_qkv = bell_draw(streams_of[8], (3 * D,), 0.2, 1.0, ((0, 32),))
    w_out = bell_draw(streams_of[9], (D, D), (D // 16) ** -0.5, 0.75, ((0, 32),))
    w_in = bell_draw(streams_of[10], (D, FF), D ** -0.5, 0.1875, ((0, 32),))
    b_in = bell_draw(streams_of[11], (FF,), 0.5, 2.5, ((0, 32),))
    w_fc2 = bell_draw(streams_of[12], (FF, D), FF ** -0.5, 0.09375, ((0, 32),))
    b_out = bell_draw(streams_of[13], (D,), 0.2, 1.0, ((0, 32),))
    cotangent = bell_draw(streams_of[14], (TOKENS, D), 1.0, 6.0, ((0, 32),))
    return dict(tokens=tokens, seq_lengths=seq_lengths, dealing=dealing, ln1_gain=ln1_gain, ln1_bias=ln1_bias, ln2_gain=ln2_gain, ln2_bias=ln2_bias, w_qkv=w_qkv, b_qkv=b_qkv, w_out=w_out, w_in=w_in, b_in=b_in, w_fc2=w_fc2, b_out=b_out, cotangent=cotangent)


@jax.custom_vjp
def low(v):
    return lax.optimization_barrier(v.astype(jnp.bfloat16)).astype(jnp.float32)

@jax.custom_vjp
def low_back(v):
    return v

def low_keep(v):
    return (low(v), None)

def low_pass(kept, grad):
    return (grad,)

def back_keep(v):
    return (v, None)

def back_low(kept, grad):
    return (low(grad),)
low.defvjp(low_keep, low_pass)
low_back.defvjp(back_keep, back_low)
epsilon = 1e-05
neg_big = -1e+30
highest = lax.Precision.HIGHEST

def matmul(left, right):
    return jnp.dot(left, right, precision=highest)

def layer_norm(values, gain, shift):
    centre = lax.optimization_barrier(jnp.mean(values, axis=-1, keepdims=True))
    centred = values - centre
    spread = lax.optimization_barrier(jnp.mean(centred * centred, axis=-1, keepdims=True))
    return centred * lax.rsqrt(spread + epsilon) * gain + shift

def exact_gelu(values):
    return jax.nn.gelu(values, approximate=False)

def angles(position, rotary):
    half = rotary // 2
    freq = 10000.0 ** (-2.0 * jnp.arange(half, dtype=jnp.float32) / rotary)
    phase = position.astype(jnp.float32)[:, None] * freq[None, :]
    return (jnp.cos(phase), jnp.sin(phase))

def rotate(heads_in, cosine, sine):
    half = cosine.shape[-1]
    first = heads_in[..., :half]
    second = heads_in[..., half:2 * half]
    cos_b = cosine[:, None, :]
    sin_b = sine[:, None, :]
    return jnp.concatenate([first * cos_b - second * sin_b, second * cos_b + first * sin_b, heads_in[..., 2 * half:]], axis=-1)

def token_meta(lengths, order, rows, block):
    slot_count = order.shape[0]
    owner = rows // block
    picked = lax.optimization_barrier(jnp.sum(jnp.where(owner[:, None] == jnp.arange(slot_count, dtype=jnp.int32)[None, :], order[None, :], 0), axis=1)).astype(jnp.int32)
    packed = picked * block + rows % block
    ends = jnp.cumsum(lengths).astype(jnp.int32)
    document = lax.optimization_barrier(jnp.sum((packed[:, None] >= ends[None, :]).astype(jnp.int32), axis=1)).astype(jnp.int32)
    starts = (ends - lengths).astype(jnp.int32)
    seq_count = lengths.shape[0]
    first = lax.optimization_barrier(jnp.sum(jnp.where(document[:, None] == jnp.arange(seq_count, dtype=jnp.int32)[None, :], starts[None, :], 0), axis=1)).astype(jnp.int32)
    return (document, (packed - first).astype(jnp.int32))

def attend(query, keys, values, document, position):
    rows = query.shape[0]
    qrows = math.gcd(rows, 512)
    blocks = rows // qrows
    scale = HEAD ** (-0.5)

    def block_fn(args):
        query_blk, doc_blk, pos_blk = args
        score = jnp.einsum('qhd,khd->hqk', query_blk, keys, precision=highest) * scale
        score = low_back(score)
        allowed = (doc_blk[:, None] == document[None, :]) & (position[None, :] <= pos_blk[:, None])
        score = jnp.where(allowed[None], score, neg_big)
        row_top = lax.optimization_barrier(jnp.max(score, axis=-1, keepdims=True))
        weight = jnp.exp(score - row_top)
        prob = low(weight / lax.optimization_barrier(jnp.sum(weight, axis=-1, keepdims=True)))
        return jnp.einsum('hqk,khd->qhd', prob, values, precision=highest)
    result = lax.map(jax.checkpoint(block_fn), (query.reshape(blocks, qrows, HEADS, HEAD), document.reshape(blocks, qrows), position.reshape(blocks, qrows)))
    return result.reshape(rows, HEADS, HEAD)

def reference(tokens, seq_lengths, dealing, ln1_gain, ln1_bias, ln2_gain, ln2_bias, w_qkv, b_qkv, w_out, w_in, b_in, w_fc2, b_out, cotangent):
    rows = jnp.arange(GROUP, dtype=jnp.int32)
    document, position = jax.vmap(lambda lengths, order: token_meta(lengths, order, rows, BLK))(seq_lengths, dealing)
    document = document.reshape(TOKENS)
    position = position.reshape(TOKENS)
    cosine, sine = angles(position, ROT)

    def forward(inputs, gain_one, shift_one, gain_two, shift_two, weight_qkv, bias_qkv, weight_out, weight_in, bias_in, weight_fc2, bias_out):
        norm_one = low(layer_norm(inputs, gain_one, shift_one))
        norm_two = low(layer_norm(inputs, gain_two, shift_two))
        joined = low_back(matmul(norm_one, weight_qkv) + bias_qkv)
        query = low(rotate(joined[:, :D].reshape(TOKENS, HEADS, HEAD), cosine, sine))
        keys = low(rotate(joined[:, D:2 * D].reshape(TOKENS, HEADS, HEAD), cosine, sine))
        values = low(joined[:, 2 * D:].reshape(TOKENS, HEADS, HEAD))
        attended = lax.map(lambda group: attend(group[0], group[1], group[2], group[3], group[4]), (query.reshape(N_DP, GROUP, HEADS, HEAD), keys.reshape(N_DP, GROUP, HEADS, HEAD), values.reshape(N_DP, GROUP, HEADS, HEAD), document.reshape(N_DP, GROUP), position.reshape(N_DP, GROUP)))
        attended = low(low_back(attended.reshape(TOKENS, D)))
        up_in = low_back(matmul(norm_two, weight_in) + bias_in)
        hidden = low(exact_gelu(up_in))
        return inputs + matmul(attended, weight_out) + matmul(hidden, weight_fc2) + bias_out
    outputs, back = jax.vjp(forward, tokens.astype(jnp.float32), ln1_gain.astype(jnp.float32), ln1_bias.astype(jnp.float32), ln2_gain.astype(jnp.float32), ln2_bias.astype(jnp.float32), w_qkv.astype(jnp.float32), b_qkv.astype(jnp.float32), w_out.astype(jnp.float32), w_in.astype(jnp.float32), b_in.astype(jnp.float32), w_fc2.astype(jnp.float32), b_out.astype(jnp.float32))
    grads = back(cotangent.astype(jnp.float32))
    return (outputs.astype(jnp.bfloat16), grads[0], grads[1], grads[2], grads[3], grads[4], grads[5], grads[6], grads[7], grads[8], grads[9], grads[10], grads[11])
```

```python
import functools

import jax
import jax.numpy as jnp
from jax import lax
from jax.experimental import pallas as pl
from jax.experimental.pallas import tpu as pltpu
from jax.sharding import Mesh
from jax.sharding import PartitionSpec as P

HEAD = 64
ROT = 16
LONGEST = 2048
GROUP_IN = 4
TILE = 256
EPS = 1e-05
NEG = -1e30
F32 = jnp.float32
BF16 = jnp.bfloat16
G_AXES = ("dp", "out")
ALL_AXES = ("dp", "out", "in")


def dot(a, b):
    return jnp.dot(a, b, preferred_element_type=F32)


def dot_nt(a, b):
    return lax.dot_general(a, b, (((1,), (1,)), ((), ())), preferred_element_type=F32)


def dot_tn(a, b):
    return lax.dot_general(a, b, (((0,), (0,)), ((), ())), preferred_element_type=F32)


def xor_swap(value, axis, size, step):
    return lax.ppermute(value, axis, [(i, i ^ step) for i in range(size)])


def rotary(x, cos, sin_l, sin_r, sign):
    left = pltpu.roll(x, 128 - ROT // 2, 1)
    right = pltpu.roll(x, ROT // 2, 1)
    return x * cos - sign * (left * sin_l) + sign * (right * sin_r)


def prep_kernel(heads, z_ref, n1_ref, dy_ref, w_ref, wo_ref, b_ref, cos_ref, sl_ref, sr_ref, qk_ref, vdo_ref):
    z = z_ref[0]
    joined = dot(n1_ref[...], w_ref[...]) + b_ref[...]
    grad_att = dot_nt(dy_ref[...], wo_ref[...])
    cos, sl, sr = cos_ref[...], sl_ref[...], sr_ref[...]
    base = heads * 128
    for h in range(heads):
        part = joined[:, h * 128 : (h + 1) * 128]
        qk_ref[z ^ h] = rotary(part, cos, sl, sr, 1.0).astype(BF16)
        vdo_ref[z ^ h] = jnp.concatenate(
            [joined[:, base + h * HEAD : base + (h + 1) * HEAD], grad_att[:, h * HEAD : (h + 1) * HEAD]], axis=1
        ).astype(BF16)


def prep(z, n1, dy, w, wo, bias, cos, sl, sr):
    rows, width = n1.shape
    heads = w.shape[1] // (3 * HEAD)
    row = lambda i, z: (i, 0)
    whole = lambda i, z: (0, 0)
    out = jax.ShapeDtypeStruct((heads, rows, 2 * HEAD), BF16)
    out_spec = pl.BlockSpec((heads, TILE, 2 * HEAD), lambda i, z: (0, i, 0))
    return pl.pallas_call(
        functools.partial(prep_kernel, heads),
        grid_spec=pltpu.PrefetchScalarGridSpec(
            num_scalar_prefetch=1,
            grid=(rows // TILE,),
            in_specs=[
                pl.BlockSpec((TILE, width), row),
                pl.BlockSpec((TILE, width), row),
                pl.BlockSpec(w.shape, whole),
                pl.BlockSpec(wo.shape, whole),
                pl.BlockSpec(bias.shape, whole),
                pl.BlockSpec((TILE, 2 * HEAD), row),
                pl.BlockSpec((TILE, 2 * HEAD), row),
                pl.BlockSpec((TILE, 2 * HEAD), row),
            ],
            out_specs=[out_spec, out_spec],
        ),
        out_shape=[out, out],
        compiler_params=pltpu.CompilerParams(vmem_limit_bytes=40 * 2**20),
        cost_estimate=pl.CostEstimate(flops=2 * rows * width * 1024, bytes_accessed=12 * 2**20, transcendentals=0),
    )(z, n1, dy, w, wo, bias, cos, sl, sr)


def post_kernel(heads, z_ref, dqk_ref, dvo_ref, cos_ref, sl_ref, sr_ref, da_ref, o_ref):
    z = z_ref[0]
    cos, sl, sr = cos_ref[...], sl_ref[...], sr_ref[...]
    base = heads * 128
    for h in range(heads):
        part = dqk_ref[z ^ h].astype(F32)
        da_ref[:, h * 128 : (h + 1) * 128] = rotary(part, cos, sl, sr, -1.0).astype(BF16)
    for h in range(0, heads, 2):
        one, two = dvo_ref[z ^ h].astype(F32), dvo_ref[z ^ (h + 1)].astype(F32)
        da_ref[:, base + h * HEAD : base + (h + 2) * HEAD] = jnp.concatenate(
            [one[:, :HEAD], two[:, :HEAD]], axis=1
        ).astype(BF16)
        o_ref[:, h * HEAD : (h + 2) * HEAD] = jnp.concatenate([one[:, HEAD:], two[:, HEAD:]], axis=1).astype(BF16)


def post(z, dqk, dvo, cos, sl, sr):
    heads, rows, _ = dqk.shape
    row = lambda i, z: (i, 0)
    slab = pl.BlockSpec((heads, TILE, 2 * HEAD), lambda i, z: (0, i, 0))
    table = pl.BlockSpec((TILE, 2 * HEAD), row)
    return pl.pallas_call(
        functools.partial(post_kernel, heads),
        grid_spec=pltpu.PrefetchScalarGridSpec(
            num_scalar_prefetch=1,
            grid=(rows // TILE,),
            in_specs=[slab, slab, table, table, table],
            out_specs=[pl.BlockSpec((TILE, heads * 3 * HEAD), row), pl.BlockSpec((TILE, heads * HEAD), row)],
        ),
        out_shape=[
            jax.ShapeDtypeStruct((rows, heads * 3 * HEAD), BF16),
            jax.ShapeDtypeStruct((rows, heads * HEAD), BF16),
        ],
        compiler_params=pltpu.CompilerParams(vmem_limit_bytes=40 * 2**20),
        cost_estimate=pl.CostEstimate(flops=rows * 2048, bytes_accessed=5 * 2**20, transcendentals=0),
    )(z, dqk, dvo, cos, sl, sr)


def doc_start(packed, ends_ref, count):
    start = packed * 0
    for d in range(count):
        start = jnp.where(packed >= ends_ref[d], ends_ref[d], start)
    return start


def doc_end(packed, ends_ref, count):
    end = ends_ref[count - 1]
    for d in range(count - 2, -1, -1):
        end = jnp.where(packed < ends_ref[d], ends_ref[d], end)
    return end


def attend_kernel(
    block, count, source_ref, ends_ref, qk_ref, vdo_ref, dqk_ref, dvo_ref, q_s, k_s, v_s, do_s, qk_t, vdo_t, dq_t, lse_s, delta_s, o_s
):
    rows = qk_ref.shape[0]
    tiles = rows // TILE
    per = TILE // block
    scale = HEAD ** (-0.5)

    def gather(i, carry):
        at = pl.multiple_of(i * TILE, TILE)
        for b in range(per):
            src = pl.multiple_of(source_ref[i * per + b] * block, block)
            dst = pl.multiple_of(at + b * block, block)
            qk = qk_ref[pl.ds(src, block), :].astype(F32)
            vdo = vdo_ref[pl.ds(src, block), :].astype(F32)
            q_s[pl.ds(dst, block), :] = (qk[:, :HEAD] * scale).astype(BF16)
            k_s[pl.ds(dst, block), :] = qk[:, HEAD:].astype(BF16)
            v_s[pl.ds(dst, block), :] = vdo[:, :HEAD].astype(BF16)
            do_s[pl.ds(dst, block), :] = vdo[:, HEAD:].astype(BF16)
        here = pl.ds(at, TILE)
        qk_t[:HEAD, here] = q_s[here, :].astype(F32).T.astype(BF16)
        qk_t[HEAD:, here] = k_s[here, :].astype(F32).T.astype(BF16)
        vdo_t[:HEAD, here] = v_s[here, :].astype(F32).T.astype(BF16)
        vdo_t[HEAD:, here] = do_s[here, :].astype(F32).T.astype(BF16)
        dq_t[:, here] = jnp.zeros((HEAD, TILE), F32)
        return carry

    lax.fori_loop(0, tiles, gather, 0)

    key_at = lax.broadcasted_iota(jnp.int32, (TILE, TILE), 0)
    query_at = lax.broadcasted_iota(jnp.int32, (TILE, TILE), 1)

    def scores(i, j):
        s = dot(k_s[pl.ds(pl.multiple_of(j * TILE, TILE), TILE), :], qk_t[:HEAD, pl.ds(pl.multiple_of(i * TILE, TILE), TILE)])
        query_row = i * TILE + lax.broadcasted_iota(jnp.int32, (1, TILE), 1)
        first = doc_start(query_row, ends_ref, count) - j * TILE
        last = (i - j) * TILE + query_at
        return jnp.where((key_at >= first) & (key_at <= last), s, NEG)

    def forward(i, carry):
        here = pl.ds(pl.multiple_of(i * TILE, TILE), TILE)

        def step(j, state):
            top, total, acc = state
            s = scores(i, j)
            new_top = jnp.maximum(top, jnp.max(s, axis=0, keepdims=True))
            p = jnp.exp(s - new_top)
            fade = jnp.exp(top - new_top)
            total = total * fade + jnp.sum(p, axis=0, keepdims=True)
            acc = acc * fade + dot(vdo_t[:HEAD, pl.ds(pl.multiple_of(j * TILE, TILE), TILE)], p.astype(BF16))
            return new_top, total, acc

        low = doc_start(i * TILE, ends_ref, count) // TILE
        top, total, acc = lax.fori_loop(
            low, i + 1, step, (jnp.full((1, TILE), NEG, F32), jnp.zeros((1, TILE), F32), jnp.zeros((HEAD, TILE), F32))
        )
        out = acc / total
        lse_s[:, here] = top + jnp.log(total)
        delta_s[:, here] = jnp.sum(out * vdo_t[HEAD:, here].astype(F32), axis=0, keepdims=True)
        o_s[here, :] = out.T.astype(BF16)
        return carry

    lax.fori_loop(0, tiles, forward, 0)

    def backward(j, carry):
        keys = pl.ds(pl.multiple_of(j * TILE, TILE), TILE)

        def step(i, state):
            dk, dv = state
            here = pl.ds(pl.multiple_of(i * TILE, TILE), TILE)
            p = jnp.exp(scores(i, j) - lse_s[:, here])
            dp = dot(v_s[keys, :], vdo_t[HEAD:, here])
            ds = (p * (dp - delta_s[:, here])).astype(BF16)
            dv = dv + dot(p.astype(BF16), do_s[here, :])
            dk = dk + dot(ds, q_s[here, :])
            dq_t[:, here] += dot(qk_t[HEAD:, keys], ds)
            return dk, dv

        high = (doc_end(j * TILE + TILE - 1, ends_ref, count) - 1) // TILE
        zero = jnp.zeros((TILE, HEAD), F32)
        dk, dv = lax.fori_loop(j, high + 1, step, (zero, zero))
        k_s[keys, :] = dk.astype(BF16)
        v_s[keys, :] = dv.astype(BF16)
        return carry

    lax.fori_loop(0, tiles, backward, 0)

    def scatter(i, carry):
        at = pl.multiple_of(i * TILE, TILE)
        here = pl.ds(at, TILE)
        dq = (dq_t[:, here] * scale).T
        dqk = jnp.concatenate([dq, k_s[here, :].astype(F32)], axis=1).astype(BF16)
        dvo = jnp.concatenate([v_s[here, :].astype(F32), o_s[here, :].astype(F32)], axis=1).astype(BF16)
        for b in range(per):
            dst = pl.ds(pl.multiple_of(source_ref[i * per + b] * block, block), block)
            dqk_ref[dst, :] = dqk[b * block : (b + 1) * block, :]
            dvo_ref[dst, :] = dvo[b * block : (b + 1) * block, :]
        return carry

    lax.fori_loop(0, tiles, scatter, 0)


def attend(source, ends, qk, vdo, block):
    rows, lanes = qk.shape
    out = jax.ShapeDtypeStruct((rows, lanes), BF16)
    in_vmem = pl.BlockSpec(memory_space=pltpu.VMEM)
    in_smem = pl.BlockSpec(memory_space=pltpu.SMEM)
    half = pltpu.VMEM((rows, HEAD), BF16)
    turned = pltpu.VMEM((lanes, rows), BF16)
    return pl.pallas_call(
        functools.partial(attend_kernel, block, ends.shape[0]),
        in_specs=[in_smem, in_smem, in_vmem, in_vmem],
        out_specs=[in_vmem, in_vmem],
        out_shape=[out, out],
        scratch_shapes=[
            half,
            half,
            half,
            half,
            turned,
            turned,
            pltpu.VMEM((HEAD, rows), F32),
            pltpu.VMEM((1, rows), F32),
            pltpu.VMEM((1, rows), F32),
            half,
        ],
        compiler_params=pltpu.CompilerParams(vmem_limit_bytes=40 * 2**20),
        cost_estimate=pl.CostEstimate(
            flops=rows * rows * HEAD * 8, bytes_accessed=4 * rows * lanes * 2, transcendentals=rows * rows
        ),
    )(source, ends, qk, vdo)


def gather_in(value):
    far = jnp.stack([value, xor_swap(value, "in", GROUP_IN, 2)])
    near = xor_swap(far, "in", GROUP_IN, 1)
    return jnp.stack([far[0], near[0], far[1], near[1]])


def scatter_in(parts):
    near = xor_swap(jnp.stack([parts[1], parts[3]]).astype(BF16), "in", GROUP_IN, 1)
    far = xor_swap((parts[2] + near[1].astype(F32)).astype(BF16), "in", GROUP_IN, 2)
    return parts[0] + near[0].astype(F32) + far.astype(F32)


def exchange_in(parts, t):
    here = [lax.dynamic_index_in_dim(parts, t ^ s, 0, keepdims=False) for s in range(GROUP_IN)]
    there = [here[0]] + [xor_swap(here[s], "in", GROUP_IN, s) for s in range(1, GROUP_IN)]
    stacked = jnp.stack(there)
    return jnp.stack([lax.dynamic_index_in_dim(stacked, t ^ u, 0, keepdims=False) for u in range(GROUP_IN)])


def exchange_out(parts, size):
    return jnp.stack([parts[0]] + [xor_swap(parts[s], "out", size, s) for s in range(1, size)])


def body(
    tokens,
    seq_lengths,
    dealing,
    ln1_gain,
    ln1_bias,
    ln2_gain,
    ln2_bias,
    w_qkv,
    b_qkv,
    w_out,
    w_in,
    b_in,
    w_fc2,
    b_out,
    cotangent,
):
    n_dp, n_out, n_in = lax.axis_size("dp"), lax.axis_size("out"), lax.axis_size("in")
    n_g = n_dp * n_out
    n_all = n_g * n_in
    rows_dev, width = tokens.shape
    ff = w_in.shape[1]
    r_w = w_in.shape[0]
    r_ff = w_fc2.shape[0]
    block = LONGEST // (2 * n_out * n_in)
    slots_dev = rows_dev // block
    heads = width // HEAD
    h_in = heads // n_in
    cols = h_in * HEAD
    rows = rows_dev * n_in
    z, t = lax.axis_index("out"), lax.axis_index("in")
    g = lax.axis_index("dp") * n_out + z
    z_arr = z[None].astype(jnp.int32)
    lengths, order = seq_lengths[0], dealing[0]
    n_seq = lengths.shape[0]
    ends = jnp.cumsum(lengths)

    slots = order.shape[0]
    packed_ids = jnp.arange(slots, dtype=jnp.int32)
    slot_of = jnp.sum(jnp.where(order[None, :] == packed_ids[:, None], packed_ids[None, :], 0), axis=1)
    chunk = slot_of // slots_dev
    source = (((chunk // n_in) ^ z) * n_in + ((chunk % n_in) ^ t)) * slots_dev + slot_of % slots_dev
    source = source.astype(jnp.int32)

    part = jnp.arange(rows, dtype=jnp.int32)
    place_slot = (z * n_in + ((part // rows_dev) ^ t)) * slots_dev + (part % rows_dev) // block
    picked = jnp.sum(jnp.where(place_slot[:, None] == packed_ids[None, :], order[None, :], 0), axis=1)
    packed = picked * block + part % block
    starts = jnp.max(jnp.where(packed[:, None] >= ends[None, :], ends[None, :], 0), axis=1)
    position = (packed - starts).astype(F32)
    lane = jnp.arange(2 * HEAD, dtype=jnp.int32) % HEAD
    half = ROT // 2
    freq = 10000.0 ** (-2.0 * (lane % half).astype(F32) / ROT)
    phase = position[:, None] * freq[None, :]
    cos = jnp.where(lane < ROT, jnp.cos(phase), 1.0)
    sine = jnp.sin(phase)
    sin_l = jnp.where(lane < half, sine, 0.0)
    sin_r = jnp.where((lane >= half) & (lane < ROT), sine, 0.0)

    vectors = [ln1_gain, ln1_bias, ln2_gain, ln2_bias, b_qkv, b_out, b_in]
    sizes = [v.shape[0] for v in vectors]
    n_vec = sum(sizes)
    qkv_cols = w_qkv.reshape(r_w, 3, n_in, h_in, HEAD)
    qk_cols = jnp.transpose(qkv_cols[:, :2], (2, 0, 3, 1, 4)).reshape(n_in, r_w, 2 * cols)
    v_cols = jnp.transpose(qkv_cols[:, 2], (1, 0, 2, 3)).reshape(n_in, r_w, cols)
    in_cols = jnp.transpose(w_in.reshape(r_w, n_g, n_in, r_ff), (2, 0, 1, 3)).reshape(n_in, r_w, ff // n_in)
    joined_cols = exchange_in(jnp.concatenate([qk_cols, v_cols, in_cols], axis=2), t).reshape(n_in * r_w, -1)
    vec_in = exchange_in(jnp.broadcast_to(jnp.concatenate(vectors)[None], (n_in, n_vec)), t).reshape(-1)
    vec_rows = -(-n_in * n_vec // width)
    vec_rows = -(-vec_rows // 16) * 16
    vec_in = jnp.pad(vec_in, (0, vec_rows * width - n_in * n_vec)).reshape(vec_rows, width)
    home = [(d, (d % n_g) * n_in + d // n_g) for d in range(n_all)]
    out_rows = lax.ppermute(w_out, ALL_AXES, home).reshape(n_in * r_w, cols)
    first = jnp.concatenate([jnp.concatenate([joined_cols[:, : 3 * cols], out_rows], axis=1), vec_in], axis=0)
    first = lax.all_gather(first, G_AXES, axis=0, tiled=False)
    second = jnp.concatenate([joined_cols[:, 3 * cols :], w_fc2], axis=1)
    second = lax.all_gather(second, G_AXES, axis=0, tiled=True)
    weight_qkv = first[:, : n_in * r_w, : 3 * cols].reshape(width, 3 * cols)
    weight_out = first[:, : n_in * r_w, 3 * cols :].reshape(cols, width)
    weight_in, weight_fc2 = second[:, : ff // n_in], second[:, ff // n_in :]
    vec_all = first[:, n_in * r_w :].reshape(n_g, -1)[:, : n_in * n_vec].reshape(n_g, n_in, n_vec).astype(F32)
    spans, at = [], 0
    for size in sizes:
        spans.append(vec_all[:, :, at : at + size])
        at += size
    gain_one, shift_one, gain_two, shift_two = [s.reshape(width) for s in spans[:4]]
    bias_out = spans[5].reshape(width)
    bias_in = lax.dynamic_index_in_dim(spans[6], t, 1, keepdims=False).reshape(ff // n_in)
    bias_qkv = lax.dynamic_index_in_dim(spans[4].reshape(3, n_in, h_in, HEAD), t, 1, keepdims=False)
    bias_qkv = jnp.concatenate([jnp.transpose(bias_qkv[:2], (1, 0, 2)).reshape(-1), bias_qkv[2].reshape(-1)])

    both = gather_in(jnp.concatenate([tokens, cotangent], axis=1))
    x_all = both[:, :, :width].reshape(rows, width).astype(F32)
    dy_all = both[:, :, width:].reshape(rows, width)
    centre = jnp.mean(x_all, axis=-1, keepdims=True)
    centred = x_all - centre
    rstd = lax.rsqrt(jnp.mean(centred * centred, axis=-1, keepdims=True) + EPS)
    xhat = centred * rstd
    n1 = (xhat * gain_one + shift_one).astype(BF16)
    n2 = (xhat * gain_two + shift_two).astype(BF16)

    qk, vdo = prep(z_arr, n1, dy_all, weight_qkv, weight_out, bias_qkv[None], cos, sin_l, sin_r)
    qk = exchange_out(qk, n_out).reshape(n_out * rows, 2 * HEAD)
    vdo = exchange_out(vdo, n_out).reshape(n_out * rows, 2 * HEAD)
    dqk, dvo = attend(source, ends, qk, vdo, block)
    dqk = exchange_out(dqk.reshape(n_out, rows, 2 * HEAD), n_out)
    dvo = exchange_out(dvo.reshape(n_out, rows, 2 * HEAD), n_out)
    da, o = post(z_arr, dqk, dvo, cos, sin_l, sin_r)

    up = dot(n2, weight_in) + bias_in
    hidden, back_gelu = jax.vjp(lambda v: jax.nn.gelu(v, approximate=False), up)
    hidden = hidden.astype(BF16)
    grad_up = back_gelu(dot_nt(dy_all, weight_fc2))[0].astype(BF16)
    grad_fc2 = dot_tn(hidden, dy_all)
    grad_in = dot_tn(n2, grad_up)
    grad_b_in = jnp.sum(grad_up.astype(F32), axis=0)
    dn2 = dot_nt(grad_up, weight_in)
    second_grads = jnp.concatenate([grad_in.astype(BF16), grad_fc2.astype(BF16)], axis=1)
    second_grads = lax.psum_scatter(second_grads, G_AXES, scatter_dimension=0, tiled=True)

    y_part = dot(hidden, weight_fc2) + dot(o, weight_out)
    own = tokens.astype(F32)
    mixed = (own + scatter_in(y_part.reshape(n_in, rows_dev, width)) + bias_out).astype(BF16)

    dn1 = dot_nt(da, weight_qkv)
    grad_qkv = dot_tn(n1, da)
    grad_out = dot_tn(o, dy_all)
    grad_b_qkv = jnp.sum(da.astype(F32), axis=0)

    def placed(vector, parts, axis):
        spread = jnp.expand_dims(vector, axis)
        mask = (jnp.arange(parts) == t).reshape([-1 if a == axis else 1 for a in range(spread.ndim)])
        return jnp.where(mask, spread, 0.0)

    qk_grad = jnp.transpose(grad_b_qkv[: 2 * cols].reshape(h_in, 2, HEAD), (1, 0, 2)).reshape(2, cols)
    b_qkv_grad = jnp.concatenate([qk_grad, grad_b_qkv[None, 2 * cols :]], axis=0)
    grad_own = cotangent.astype(F32)
    vec_grads = [
        jnp.sum(dn1 * xhat, axis=0),
        jnp.sum(dn1, axis=0),
        jnp.sum(dn2 * xhat, axis=0),
        jnp.sum(dn2, axis=0),
        placed(b_qkv_grad, n_in, 1).reshape(-1),
        jnp.sum(grad_own, axis=0),
        placed(grad_b_in.reshape(n_g, r_ff), n_in, 1).reshape(-1),
    ]
    vec_grads = jnp.concatenate([v.reshape(n_g, n_in, -1) for v in vec_grads], axis=2).reshape(n_g, -1)
    vec_grads = jnp.pad(vec_grads, ((0, 0), (0, vec_rows * width - n_in * n_vec))).reshape(n_g, vec_rows, width)
    first_grads = jnp.concatenate(
        [
            grad_qkv.astype(BF16).reshape(n_g, n_in * r_w, 3 * cols),
            grad_out.astype(BF16).reshape(n_g, n_in * r_w, cols),
        ],
        axis=2,
    )
    first_grads = jnp.concatenate([first_grads, vec_grads.astype(BF16)], axis=1)
    first_grads = lax.psum_scatter(first_grads, G_AXES, scatter_dimension=0, tiled=False)

    in_part = second_grads[:, : ff // n_in].reshape(n_in, r_w, ff // n_in)
    in_part = exchange_in(in_part, t).reshape(n_in, r_w, n_g, r_ff)
    grad_w_in = jnp.transpose(in_part, (1, 2, 0, 3)).reshape(r_w, ff).astype(F32)
    grad_w_fc2 = second_grads[:, ff // n_in :].astype(F32)
    qkv_part = exchange_in(first_grads[: n_in * r_w, : 3 * cols].reshape(n_in, r_w, 3 * cols), t)
    qk_part = jnp.transpose(qkv_part[:, :, : 2 * cols].reshape(n_in, r_w, h_in, 2, HEAD), (1, 3, 0, 2, 4))
    v_part = jnp.transpose(qkv_part[:, :, 2 * cols :], (1, 0, 2)).reshape(r_w, width)
    grad_w_qkv = jnp.concatenate([qk_part.reshape(r_w, 2 * width), v_part], axis=1).astype(F32)
    back_home = [(b, a) for a, b in home]
    out_part = first_grads[: n_in * r_w, 3 * cols :].reshape(r_w, width)
    grad_w_out = lax.ppermute(out_part, ALL_AXES, back_home).astype(F32)
    vec_part = first_grads[n_in * r_w :].reshape(-1)[: n_in * n_vec].reshape(n_in, n_vec)
    vec_part = jnp.sum(exchange_in(vec_part, t).astype(F32), axis=0)
    vec_out, at = [], 0
    for size in sizes:
        vec_out.append(vec_part[at : at + size])
        at += size

    w_sum = scatter_in((gain_one * dn1 + gain_two * dn2).reshape(n_in, rows_dev, width))
    own_hat, own_rstd = xhat[:rows_dev], rstd[:rows_dev]
    mean_w = jnp.mean(w_sum, axis=-1, keepdims=True)
    mean_wx = jnp.mean(w_sum * own_hat, axis=-1, keepdims=True)
    grad_tokens = grad_own + own_rstd * (w_sum - mean_w - own_hat * mean_wx)
    return (
        mixed,
        grad_tokens,
        vec_out[0],
        vec_out[1],
        vec_out[2],
        vec_out[3],
        grad_w_qkv,
        vec_out[4],
        grad_w_out,
        grad_w_in,
        vec_out[6],
        grad_w_fc2,
        vec_out[5],
    )


def solution(mesh):
    n_dp, n_ctx = mesh.shape["dp"], mesh.shape["ctx"]
    split = Mesh(mesh.devices.reshape(n_dp, n_ctx // GROUP_IN, GROUP_IN), ALL_AXES)
    mat, vec, group = P(ALL_AXES, None), P(ALL_AXES), P("dp", None)
    return jax.shard_map(
        body,
        mesh=split,
        in_specs=(mat, group, group, vec, vec, vec, vec, mat, vec, mat, mat, vec, mat, vec, mat),
        out_specs=(mat, mat, vec, vec, vec, vec, mat, vec, mat, mat, vec, mat, vec),
        check_vma=False,
    )
```

```python
import functools

import jax
import jax.numpy as jnp
from jax import lax
from jax.experimental import pallas as pl
from jax.experimental.pallas import tpu as pltpu
from jax.sharding import Mesh
from jax.sharding import PartitionSpec as P

HEAD = 64
ROT = 16
LONGEST = 2048
GROUP_IN = 4
TILE = 256
EPS = 1e-05
NEG = -1e30
F32 = jnp.float32
BF16 = jnp.bfloat16
G_AXES = ("dp", "out")
ALL_AXES = ("dp", "in", "out")


def dot(a, b):
    return jnp.dot(a, b, preferred_element_type=F32)


def dot_nt(a, b):
    return lax.dot_general(a, b, (((1,), (1,)), ((), ())), preferred_element_type=F32)


def dot_tn(a, b):
    return lax.dot_general(a, b, (((0,), (0,)), ((), ())), preferred_element_type=F32)


def xor_swap(value, axis, size, step):
    return lax.ppermute(value, axis, [(i, i ^ step) for i in range(size)])


def rotary(x, cos, sin_l, sin_r, sign):
    left = pltpu.roll(x, 128 - ROT // 2, 1)
    right = pltpu.roll(x, ROT // 2, 1)
    return x * cos - sign * (left * sin_l) + sign * (right * sin_r)


def pair_up(x, block):
    blocks = [x[i : i + block] for i in range(0, x.shape[0], block)]
    return jnp.concatenate([jnp.concatenate(blocks[i : i + 2], axis=1) for i in range(0, len(blocks), 2)], axis=0)


def unpair(x, block):
    parts = []
    for i in range(0, x.shape[0], block):
        parts += [x[i : i + block, :HEAD], x[i : i + block, HEAD:]]
    return jnp.concatenate(parts, axis=0)


def params(flops, size, exps=0):
    return dict(
        compiler_params=pltpu.CompilerParams(vmem_limit_bytes=40 * 2**20),
        cost_estimate=pl.CostEstimate(flops=flops, bytes_accessed=size, transcendentals=exps),
    )


def row_at(i, z):
    return (i, 0)


def whole_at(i, z):
    return (0, 0)


def slab_at(i, z):
    return (0, i, 0)


def prep_kernel(heads, block, z_ref, n1_ref, w_ref, b_ref, cos_ref, sl_ref, sr_ref, qk_ref, v_ref):
    z = z_ref[0]
    joined = dot(n1_ref[...], w_ref[...]) + b_ref[...]
    cos, sl, sr = cos_ref[...], sl_ref[...], sr_ref[...]
    base = heads * 128
    for h in range(heads):
        part = joined[:, h * 128 : (h + 1) * 128]
        qk_ref[z ^ h] = rotary(part, cos, sl, sr, 1.0).astype(BF16)
        v_ref[z ^ h] = pair_up(joined[:, base + h * HEAD : base + (h + 1) * HEAD], block).astype(BF16)


def prep(z, n1, w, bias, cos, sl, sr, block):
    rows, width = n1.shape
    heads = w.shape[1] // (3 * HEAD)
    table = pl.BlockSpec((TILE, 2 * HEAD), row_at)
    return pl.pallas_call(
        functools.partial(prep_kernel, heads, block),
        grid_spec=pltpu.PrefetchScalarGridSpec(
            num_scalar_prefetch=1,
            grid=(rows // TILE,),
            in_specs=[
                pl.BlockSpec((TILE, width), row_at),
                pl.BlockSpec(w.shape, whole_at),
                pl.BlockSpec(bias.shape, whole_at),
                table,
                table,
                table,
            ],
            out_specs=[
                pl.BlockSpec((heads, TILE, 2 * HEAD), slab_at),
                pl.BlockSpec((heads, TILE // 2, 2 * HEAD), slab_at),
            ],
        ),
        out_shape=[
            jax.ShapeDtypeStruct((heads, rows, 2 * HEAD), BF16),
            jax.ShapeDtypeStruct((heads, rows // 2, 2 * HEAD), BF16),
        ],
        **params(2 * rows * width * w.shape[1], 8 * 2**20),
    )(z, n1, w, bias, cos, sl, sr)


def grad_att_kernel(heads, block, z_ref, dy_ref, wo_ref, do_ref):
    z = z_ref[0]
    grad = dot_nt(dy_ref[...], wo_ref[...])
    for h in range(heads):
        do_ref[z ^ h] = pair_up(grad[:, h * HEAD : (h + 1) * HEAD], block).astype(BF16)


def grad_att(z, dy, wo, block):
    rows, width = dy.shape
    heads = wo.shape[0] // HEAD
    return pl.pallas_call(
        functools.partial(grad_att_kernel, heads, block),
        grid_spec=pltpu.PrefetchScalarGridSpec(
            num_scalar_prefetch=1,
            grid=(rows // TILE,),
            in_specs=[pl.BlockSpec((TILE, width), row_at), pl.BlockSpec(wo.shape, whole_at)],
            out_specs=pl.BlockSpec((heads, TILE // 2, 2 * HEAD), slab_at),
        ),
        out_shape=jax.ShapeDtypeStruct((heads, rows // 2, 2 * HEAD), BF16),
        **params(2 * rows * width * wo.shape[0], 4 * 2**20),
    )(z, dy, wo)


def merge_heads_kernel(heads, block, z_ref, part_ref, o_ref):
    z = z_ref[0]
    for h in range(0, heads, 2):
        one, two = unpair(part_ref[z ^ h].astype(F32), block), unpair(part_ref[z ^ (h + 1)].astype(F32), block)
        o_ref[:, h * HEAD : (h + 2) * HEAD] = jnp.concatenate([one, two], axis=1).astype(BF16)


def merge_heads(z, parts, block):
    heads, half_rows, _ = parts.shape
    return pl.pallas_call(
        functools.partial(merge_heads_kernel, heads, block),
        grid_spec=pltpu.PrefetchScalarGridSpec(
            num_scalar_prefetch=1,
            grid=(2 * half_rows // TILE,),
            in_specs=[pl.BlockSpec((heads, TILE // 2, 2 * HEAD), slab_at)],
            out_specs=pl.BlockSpec((TILE, heads * HEAD), row_at),
        ),
        out_shape=jax.ShapeDtypeStruct((2 * half_rows, heads * HEAD), BF16),
        **params(half_rows * 1024, 2**20),
    )(z, parts)


def post_kernel(heads, block, z_ref, dqk_ref, dv_ref, cos_ref, sl_ref, sr_ref, da_ref):
    z = z_ref[0]
    cos, sl, sr = cos_ref[...], sl_ref[...], sr_ref[...]
    base = heads * 128
    for h in range(heads):
        part = dqk_ref[z ^ h].astype(F32)
        da_ref[:, h * 128 : (h + 1) * 128] = rotary(part, cos, sl, sr, -1.0).astype(BF16)
    for h in range(0, heads, 2):
        one, two = unpair(dv_ref[z ^ h].astype(F32), block), unpair(dv_ref[z ^ (h + 1)].astype(F32), block)
        da_ref[:, base + h * HEAD : base + (h + 2) * HEAD] = jnp.concatenate([one, two], axis=1).astype(BF16)


def post(z, dqk, dv, cos, sl, sr, block):
    heads, rows, _ = dqk.shape
    table = pl.BlockSpec((TILE, 2 * HEAD), row_at)
    return pl.pallas_call(
        functools.partial(post_kernel, heads, block),
        grid_spec=pltpu.PrefetchScalarGridSpec(
            num_scalar_prefetch=1,
            grid=(rows // TILE,),
            in_specs=[
                pl.BlockSpec((heads, TILE, 2 * HEAD), slab_at),
                pl.BlockSpec((heads, TILE // 2, 2 * HEAD), slab_at),
                table,
                table,
                table,
            ],
            out_specs=pl.BlockSpec((TILE, heads * 3 * HEAD), row_at),
        ),
        out_shape=jax.ShapeDtypeStruct((rows, heads * 3 * HEAD), BF16),
        **params(rows * 4096, 5 * 2**20),
    )(z, dqk, dv, cos, sl, sr)


def doc_start(packed, ends_ref, count):
    start = packed * 0
    for d in range(count):
        start = jnp.where(packed >= ends_ref[d], ends_ref[d], start)
    return start


def doc_end(packed, ends_ref, count):
    end = ends_ref[count - 1]
    for d in range(count - 2, -1, -1):
        end = jnp.where(packed < ends_ref[d], ends_ref[d], end)
    return end


def tile_at(i):
    return pl.ds(pl.multiple_of(i * TILE, TILE), TILE)


def load_half(ref, source, block):
    both = ref[pl.ds(pl.multiple_of((source // 2) * block, block), block), :].astype(F32)
    return jnp.where(source % 2 == 0, both[:, :HEAD], both[:, HEAD:])


def masked_scores(k_s, q_t, ends_ref, count, i, j):
    s = dot(k_s[tile_at(j), :], q_t[:HEAD, tile_at(i)])
    key_at = lax.broadcasted_iota(jnp.int32, (TILE, TILE), 0)
    query_at = lax.broadcasted_iota(jnp.int32, (TILE, TILE), 1)
    query_row = i * TILE + lax.broadcasted_iota(jnp.int32, (1, TILE), 1)
    first = doc_start(query_row, ends_ref, count) - j * TILE
    last = (i - j) * TILE + query_at
    return jnp.where((key_at >= first) & (key_at <= last), s, NEG)


def forward_kernel(block, count, source_ref, packed_ref, ends_ref, qk_ref, v_ref, o_ref, o_t, lse_ref, k_s, q_t, v_t, o_s):
    rows = qk_ref.shape[0]
    tiles = rows // TILE
    per = TILE // block
    scale = HEAD ** (-0.5)

    def gather(i, carry):
        qk, v = [], []
        for b in range(per):
            src = source_ref[i * per + b]
            qk.append(qk_ref[pl.ds(pl.multiple_of(src * block, block), block), :].astype(F32))
            v.append(load_half(v_ref, src, block))
        qk, v = jnp.concatenate(qk, axis=0), jnp.concatenate(v, axis=0)
        k_s[tile_at(i), :] = qk[:, HEAD:].astype(BF16)
        q_t[:, tile_at(i)] = (qk.T[:HEAD] * scale).astype(BF16)
        v_t[:, tile_at(i)] = v.T.astype(BF16)
        return carry

    lax.fori_loop(0, tiles, gather, 0)

    def forward(i, carry):
        def step(j, state):
            top, total, acc = state
            s = masked_scores(k_s, q_t, ends_ref, count, i, j)
            new_top = jnp.maximum(top, jnp.max(s, axis=0, keepdims=True))
            p = jnp.exp(s - new_top)
            fade = jnp.exp(top - new_top)
            total = total * fade + jnp.sum(p, axis=0, keepdims=True)
            acc = acc * fade + dot(v_t[:, tile_at(j)], p.astype(BF16))
            return new_top, total, acc

        low = doc_start(i * TILE, ends_ref, count) // TILE
        top, total, acc = lax.fori_loop(
            low, i + 1, step, (jnp.full((1, TILE), NEG, F32), jnp.zeros((1, TILE), F32), jnp.zeros((HEAD, TILE), F32))
        )
        out = acc / total
        lse_ref[:, tile_at(i)] = top + jnp.log(total)
        o_t[:, tile_at(i)] = out
        o_s[tile_at(i), :] = out.T
        return carry

    lax.fori_loop(0, tiles, forward, 0)

    def scatter(i, carry):
        both = [o_s[pl.ds(pl.multiple_of(packed_ref[2 * i + b] * block, block), block), :] for b in range(2)]
        o_ref[pl.ds(pl.multiple_of(i * block, block), block), :] = jnp.concatenate(both, axis=1).astype(BF16)
        return carry

    lax.fori_loop(0, rows // (2 * block), scatter, 0)


def backward_kernel(
    block, count, source_ref, packed_ref, ends_ref, qk_ref, v_ref, do_ref, o_t, lse_ref, dqk_ref, dv_ref, q_s, k_s, v_s, do_s, qk_t, do_t, dq_t, delta_s, dk_s, dv_s
):
    rows = qk_ref.shape[0]
    tiles = rows // TILE
    per = TILE // block
    scale = HEAD ** (-0.5)

    def gather(i, carry):
        qk, v, do = [], [], []
        for b in range(per):
            src = source_ref[i * per + b]
            qk.append(qk_ref[pl.ds(pl.multiple_of(src * block, block), block), :].astype(F32))
            v.append(load_half(v_ref, src, block))
            do.append(load_half(do_ref, src, block))
        qk, v, do = jnp.concatenate(qk, axis=0), jnp.concatenate(v, axis=0), jnp.concatenate(do, axis=0)
        here = tile_at(i)
        q_s[here, :] = (qk[:, :HEAD] * scale).astype(BF16)
        k_s[here, :] = qk[:, HEAD:].astype(BF16)
        turned = qk.T
        qk_t[:HEAD, here] = (turned[:HEAD] * scale).astype(BF16)
        qk_t[HEAD:, here] = turned[HEAD:].astype(BF16)
        v_s[here, :] = v.astype(BF16)
        do_s[here, :] = do.astype(BF16)
        do_turned = do.T
        do_t[:, here] = do_turned.astype(BF16)
        dq_t[:, here] = jnp.zeros((HEAD, TILE), F32)
        delta_s[:, here] = jnp.sum(o_t[:, here] * do_turned, axis=0, keepdims=True)
        return carry

    lax.fori_loop(0, tiles, gather, 0)

    def backward(j, carry):
        keys = tile_at(j)

        def step(i, state):
            dk, dv = state
            here = tile_at(i)
            p = jnp.exp(masked_scores(k_s, qk_t, ends_ref, count, i, j) - lse_ref[:, here])
            dp = dot(v_s[keys, :], do_t[:, here])
            ds = (p * (dp - delta_s[:, here])).astype(BF16)
            dv = dv + dot(p.astype(BF16), do_s[here, :])
            dk = dk + dot(ds, q_s[here, :])
            dq_t[:, here] += dot(qk_t[HEAD:, keys], ds)
            return dk, dv

        high = (doc_end(j * TILE + TILE - 1, ends_ref, count) - 1) // TILE
        zero = jnp.zeros((TILE, HEAD), F32)
        dk, dv = lax.fori_loop(j, high + 1, step, (zero, zero))
        dk_s[keys, :] = dk
        dv_s[keys, :] = dv
        return carry

    lax.fori_loop(0, tiles, backward, 0)

    def scatter(i, carry):
        here = tile_at(i)
        dq = (dq_t[:, here] * scale).T
        dqk = jnp.concatenate([dq, dk_s[here, :]], axis=1).astype(BF16)
        for b in range(per):
            dst = pl.ds(pl.multiple_of(source_ref[i * per + b] * block, block), block)
            dqk_ref[dst, :] = dqk[b * block : (b + 1) * block, :]
        return carry

    lax.fori_loop(0, tiles, scatter, 0)

    def scatter_v(i, carry):
        both = [dv_s[pl.ds(pl.multiple_of(packed_ref[2 * i + b] * block, block), block), :] for b in range(2)]
        dv_ref[pl.ds(pl.multiple_of(i * block, block), block), :] = jnp.concatenate(both, axis=1).astype(BF16)
        return carry

    lax.fori_loop(0, rows // (2 * block), scatter_v, 0)


IN_VMEM = pl.BlockSpec(memory_space=pltpu.VMEM)
IN_SMEM = pl.BlockSpec(memory_space=pltpu.SMEM)


def attend_forward(source, packed, ends, qk, v, block):
    rows = qk.shape[0]
    turned = pltpu.VMEM((HEAD, rows), BF16)
    return pl.pallas_call(
        functools.partial(forward_kernel, block, ends.shape[0]),
        in_specs=[IN_SMEM] * 3 + [IN_VMEM] * 2,
        out_specs=[IN_VMEM] * 3,
        out_shape=[
            jax.ShapeDtypeStruct((rows // 2, 2 * HEAD), BF16),
            jax.ShapeDtypeStruct((HEAD, rows), F32),
            jax.ShapeDtypeStruct((1, rows), F32),
        ],
        scratch_shapes=[pltpu.VMEM((rows, HEAD), BF16), turned, turned, pltpu.VMEM((rows, HEAD), F32)],
        **params(rows * rows * HEAD * 4, 6 * rows * HEAD * 2, rows * rows),
    )(source, packed, ends, qk, v)


def attend_backward(source, packed, ends, qk, v, do, o_t, lse, block):
    rows = qk.shape[0]
    half = pltpu.VMEM((rows, HEAD), BF16)
    wide = pltpu.VMEM((rows, HEAD), F32)
    return pl.pallas_call(
        functools.partial(backward_kernel, block, ends.shape[0]),
        in_specs=[IN_SMEM] * 3 + [IN_VMEM] * 5,
        out_specs=[IN_VMEM] * 2,
        out_shape=[
            jax.ShapeDtypeStruct((rows, 2 * HEAD), BF16),
            jax.ShapeDtypeStruct((rows // 2, 2 * HEAD), BF16),
        ],
        scratch_shapes=[
            half,
            half,
            half,
            half,
            pltpu.VMEM((2 * HEAD, rows), BF16),
            pltpu.VMEM((HEAD, rows), BF16),
            pltpu.VMEM((HEAD, rows), F32),
            pltpu.VMEM((1, rows), F32),
            wide,
            wide,
        ],
        **params(rows * rows * HEAD * 10, 12 * rows * HEAD * 2, rows * rows),
    )(source, packed, ends, qk, v, do, o_t, lse)


def gather_in(value):
    far = jnp.stack([value, xor_swap(value, "in", GROUP_IN, 2)])
    near = xor_swap(far, "in", GROUP_IN, 1)
    return jnp.stack([far[0], near[0], far[1], near[1]])


def scatter_in(parts):
    half = parts.shape[-1] // 2
    low = parts.astype(BF16)
    sums = []
    for at in (0, half):
        cut = slice(at, at + half)
        near = xor_swap(jnp.stack([low[1, :, cut], low[3, :, cut]]), "in", GROUP_IN, 1)
        far = xor_swap((parts[2, :, cut] + near[1].astype(F32)).astype(BF16), "in", GROUP_IN, 2)
        sums.append(parts[0, :, cut] + near[0].astype(F32) + far.astype(F32))
    return jnp.concatenate(sums, axis=1)


def exchange_in(parts, t):
    here = [lax.dynamic_index_in_dim(parts, t ^ s, 0, keepdims=False) for s in range(GROUP_IN)]
    there = [here[0]] + [xor_swap(here[s], "in", GROUP_IN, s) for s in range(1, GROUP_IN)]
    stacked = jnp.stack(there)
    return jnp.stack([lax.dynamic_index_in_dim(stacked, t ^ u, 0, keepdims=False) for u in range(GROUP_IN)])


def exchange_out(parts, size):
    return jnp.stack([parts[0]] + [xor_swap(parts[s], "out", size, s) for s in range(1, size)])


def body(
    tokens,
    seq_lengths,
    dealing,
    ln1_gain,
    ln1_bias,
    ln2_gain,
    ln2_bias,
    w_qkv,
    b_qkv,
    w_out,
    w_in,
    b_in,
    w_fc2,
    b_out,
    cotangent,
):
    n_dp, n_out, n_in = lax.axis_size("dp"), lax.axis_size("out"), lax.axis_size("in")
    n_g = n_dp * n_out
    n_all = n_g * n_in
    rows_dev, width = tokens.shape
    ff = w_in.shape[1]
    ff_in = ff // n_in
    r_w = w_in.shape[0]
    r_ff = w_fc2.shape[0]
    block = LONGEST // (2 * n_out * n_in)
    slots_dev = rows_dev // block
    heads = width // HEAD
    h_in = heads // n_in
    cols = h_in * HEAD
    rows = rows_dev * n_in
    z, t = lax.axis_index("out"), lax.axis_index("in")
    z_arr = z[None].astype(jnp.int32)
    lengths, order = seq_lengths[0], dealing[0]
    ends = jnp.cumsum(lengths)

    slots = order.shape[0]
    ids = jnp.arange(slots, dtype=jnp.int32)
    slot_of = jnp.sum(jnp.where(order[None, :] == ids[:, None], ids[None, :], 0), axis=1)
    chunk = slot_of // slots_dev
    source = (((chunk % n_out) ^ z) * n_in + ((chunk // n_out) ^ t)) * slots_dev + slot_of % slots_dev
    source = source.astype(jnp.int32)
    lies = ids // slots_dev
    slot_here = (((lies % n_in) ^ t) * n_out + ((lies // n_in) ^ z)) * slots_dev + ids % slots_dev
    packed_of = jnp.sum(jnp.where(slot_here[:, None] == ids[None, :], order[None, :], 0), axis=1).astype(jnp.int32)

    part = jnp.arange(rows, dtype=jnp.int32)
    packed = packed_of[: rows // block].reshape(-1, 1) * block + jnp.arange(block, dtype=jnp.int32)[None, :]
    packed = packed.reshape(rows)
    starts = jnp.max(jnp.where(packed[:, None] >= ends[None, :], ends[None, :], 0), axis=1)
    position = (packed - starts).astype(F32)
    lane = jnp.arange(2 * HEAD, dtype=jnp.int32) % HEAD
    half = ROT // 2
    freq = 10000.0 ** (-2.0 * (lane % half).astype(F32) / ROT)
    phase = position[:, None] * freq[None, :]
    cos = jnp.where(lane < ROT, jnp.cos(phase), 1.0)
    sine = jnp.sin(phase)
    sin_l = jnp.where(lane < half, sine, 0.0)
    sin_r = jnp.where((lane >= half) & (lane < ROT), sine, 0.0)

    vectors = [ln1_gain, ln1_bias, ln2_gain, ln2_bias, b_qkv, b_out, b_in]
    sizes = [v.shape[0] for v in vectors]
    n_vec = sum(sizes)
    vec_cols = n_vec // r_w
    qkv_cols = w_qkv.reshape(r_w, 3, n_in, h_in, HEAD)
    qk_cols = jnp.transpose(qkv_cols[:, :2], (2, 0, 3, 1, 4)).reshape(n_in, r_w, 2 * cols)
    v_cols = jnp.transpose(qkv_cols[:, 2], (1, 0, 2, 3)).reshape(n_in, r_w, cols)
    in_cols = jnp.transpose(w_in.reshape(r_w, n_dp, n_in, n_out, r_ff), (2, 0, 1, 3, 4)).reshape(n_in, r_w, ff_in)
    vec = jnp.pad(jnp.concatenate(vectors).reshape(r_w, vec_cols), ((0, 0), (0, 128 - vec_cols)))
    vec = jnp.broadcast_to(vec[None], (n_in, r_w, 128))
    joined_cols = exchange_in(jnp.concatenate([qk_cols, v_cols, vec, in_cols], axis=2), t).reshape(n_in * r_w, -1)
    home = []
    for b in range(n_all):
        t_to, g_to = b // n_g, b % n_g
        home.append((b, ((g_to // n_out) * n_in + t_to) * n_out + g_to % n_out))
    out_rows = lax.ppermute(w_out, ALL_AXES, home).reshape(n_in * r_w, cols)
    first = jnp.concatenate([joined_cols[:, : 3 * cols + 128], out_rows], axis=1)
    first = lax.all_gather(first, G_AXES, axis=0, tiled=False)
    second = jnp.concatenate([joined_cols[:, 3 * cols + 128 :], w_fc2], axis=1)
    second = lax.all_gather(second, G_AXES, axis=0, tiled=False)

    def natural(value):
        value = value.reshape(n_dp, n_out, n_in, r_w, -1)
        return jnp.transpose(value, (0, 2, 1, 3, 4)).reshape(n_all * r_w, -1)

    def by_owner(value):
        value = value.reshape(n_dp, n_in, n_out, r_w, -1)
        return jnp.transpose(value, (0, 2, 1, 3, 4)).reshape(n_g, n_in * r_w, -1)

    weight_qkv = natural(first[:, :, : 3 * cols])
    weight_out = first[:, :, 3 * cols + 128 :].reshape(cols, width)
    weight_in = natural(second[:, :, :ff_in])
    weight_fc2 = second[:, :, ff_in:].reshape(ff_in, width)
    vec_all = first[:, :, 3 * cols : 3 * cols + vec_cols].reshape(n_dp, n_out, n_in, n_vec).astype(F32)
    vec_all = jnp.transpose(vec_all, (0, 2, 1, 3))
    spans, at = [], 0
    for size in sizes:
        spans.append(vec_all[..., at : at + size])
        at += size
    gain_one, shift_one, gain_two, shift_two = [s.reshape(width) for s in spans[:4]]
    bias_out = spans[5].reshape(width)
    bias_in = lax.dynamic_index_in_dim(spans[6], t, 1, keepdims=False).reshape(ff_in)
    bias_qkv = lax.dynamic_index_in_dim(spans[4].reshape(3, n_in, h_in, HEAD), t, 1, keepdims=False)
    bias_qkv = jnp.concatenate([jnp.transpose(bias_qkv[:2], (1, 0, 2)).reshape(-1), bias_qkv[2].reshape(-1)])

    x_all = gather_in(tokens).reshape(rows, width).astype(F32)
    dy_all = gather_in(cotangent).reshape(rows, width)
    centre = jnp.mean(x_all, axis=-1, keepdims=True)
    centred = x_all - centre
    rstd = lax.rsqrt(jnp.mean(centred * centred, axis=-1, keepdims=True) + EPS)
    xhat = centred * rstd
    n1 = (xhat * gain_one + shift_one).astype(BF16)
    n2 = (xhat * gain_two + shift_two).astype(BF16)

    qk, v = prep(z_arr, n1, weight_qkv, bias_qkv[None], cos, sin_l, sin_r, block)
    qk = exchange_out(qk, n_out).reshape(n_out * rows, 2 * HEAD)
    v = exchange_out(v, n_out).reshape(n_out * rows // 2, 2 * HEAD)
    do = grad_att(z_arr, dy_all, weight_out, block)
    do = exchange_out(do, n_out).reshape(n_out * rows // 2, 2 * HEAD)
    o, o_t, lse = attend_forward(source, packed_of, ends, qk, v, block)
    o = exchange_out(o.reshape(n_out, rows // 2, 2 * HEAD), n_out)

    up = dot(n2, weight_in) + bias_in
    hidden, back_gelu = jax.vjp(lambda v: jax.nn.gelu(v, approximate=False), up)
    hidden = hidden.astype(BF16)
    grad_up = back_gelu(dot_nt(dy_all, weight_fc2))[0].astype(BF16)
    grad_fc2 = dot_tn(hidden, dy_all)
    grad_in = dot_tn(n2, grad_up)
    grad_b_in = jnp.sum(grad_up.astype(F32), axis=0)
    dn2 = dot_nt(grad_up, weight_in)
    second_grads = jnp.concatenate(
        [by_owner(grad_in.astype(BF16)), grad_fc2.astype(BF16).reshape(n_g, r_ff, width)], axis=2
    )

    o = merge_heads(z_arr, o, block)
    y_part = dot(hidden, weight_fc2) + dot(o, weight_out)

    do, second_grads, y_part = lax.optimization_barrier((do, second_grads, y_part))
    second_grads = lax.psum_scatter(second_grads, G_AXES, scatter_dimension=0, tiled=False)
    own = tokens.astype(F32)
    mixed = (own + scatter_in(y_part.reshape(n_in, rows_dev, width)) + bias_out).astype(BF16)
    dqk, dv = attend_backward(source, packed_of, ends, qk, v, do, o_t, lse, block)
    dqk = exchange_out(dqk.reshape(n_out, rows, 2 * HEAD), n_out)
    dv = exchange_out(dv.reshape(n_out, rows // 2, 2 * HEAD), n_out)
    da = post(z_arr, dqk, dv, cos, sin_l, sin_r, block)

    dn1 = dot_nt(da, weight_qkv)
    grad_qkv = dot_tn(n1, da)
    grad_out = dot_tn(o, dy_all)
    grad_b_qkv = jnp.sum(da.astype(F32), axis=0)

    def placed(vector, axis):
        spread = jnp.expand_dims(vector, axis)
        mask = (jnp.arange(n_in) == t).reshape([-1 if a == axis else 1 for a in range(spread.ndim)])
        return jnp.where(mask, spread, 0.0).reshape(-1)

    qk_grad = jnp.transpose(grad_b_qkv[: 2 * cols].reshape(h_in, 2, HEAD), (1, 0, 2)).reshape(2, cols)
    b_qkv_grad = jnp.concatenate([qk_grad, grad_b_qkv[None, 2 * cols :]], axis=0)
    grad_own = cotangent.astype(F32)
    vec_grads = [
        jnp.sum(dn1 * xhat, axis=0),
        jnp.sum(dn1, axis=0),
        jnp.sum(dn2 * xhat, axis=0),
        jnp.sum(dn2, axis=0),
        placed(b_qkv_grad, 1),
        jnp.sum(grad_own, axis=0),
        placed(grad_b_in.reshape(n_dp, n_out, r_ff), 1),
    ]
    vec_grads = jnp.concatenate([v.reshape(n_dp, n_in, n_out, -1) for v in vec_grads], axis=3)
    vec_grads = jnp.transpose(vec_grads, (0, 2, 1, 3)).reshape(n_g, n_in * r_w, vec_cols)
    vec_grads = jnp.pad(vec_grads, ((0, 0), (0, 0), (0, 128 - vec_cols)))
    first_grads = jnp.concatenate(
        [
            by_owner(grad_qkv.astype(BF16)),
            vec_grads.astype(BF16),
            grad_out.astype(BF16).reshape(n_g, n_in * r_w, cols),
        ],
        axis=2,
    )
    first_grads = lax.psum_scatter(first_grads, G_AXES, scatter_dimension=0, tiled=False)

    in_part = exchange_in(second_grads[:, :ff_in].reshape(n_in, r_w, ff_in), t)
    in_part = in_part.reshape(n_in, r_w, n_dp, n_out, r_ff)
    grad_w_in = jnp.transpose(in_part, (1, 2, 0, 3, 4)).reshape(r_w, ff).astype(F32)
    grad_w_fc2 = second_grads[:, ff_in:].astype(F32)
    back_home = [(b, a) for a, b in home]
    out_part = first_grads[:, 3 * cols + 128 :].reshape(r_w, width)
    grad_w_out = lax.ppermute(out_part, ALL_AXES, back_home).astype(F32)
    qkv_part = exchange_in(first_grads[:, : 3 * cols + 128].reshape(n_in, r_w, 3 * cols + 128), t)
    qk_part = jnp.transpose(qkv_part[:, :, : 2 * cols].reshape(n_in, r_w, h_in, 2, HEAD), (1, 3, 0, 2, 4))
    v_part = jnp.transpose(qkv_part[:, :, 2 * cols : 3 * cols], (1, 0, 2)).reshape(r_w, width)
    grad_w_qkv = jnp.concatenate([qk_part.reshape(r_w, 2 * width), v_part], axis=1).astype(F32)
    vec_part = qkv_part[:, :, 3 * cols : 3 * cols + vec_cols].reshape(n_in, n_vec).astype(F32)
    vec_part = jnp.sum(vec_part, axis=0)
    vec_out, at = [], 0
    for size in sizes:
        vec_out.append(vec_part[at : at + size])
        at += size

    w_sum = scatter_in((gain_one * dn1 + gain_two * dn2).reshape(n_in, rows_dev, width))
    own_hat, own_rstd = xhat[:rows_dev], rstd[:rows_dev]
    mean_w = jnp.mean(w_sum, axis=-1, keepdims=True)
    mean_wx = jnp.mean(w_sum * own_hat, axis=-1, keepdims=True)
    grad_tokens = grad_own + own_rstd * (w_sum - mean_w - own_hat * mean_wx)
    return (
        mixed,
        grad_tokens,
        vec_out[0],
        vec_out[1],
        vec_out[2],
        vec_out[3],
        grad_w_qkv,
        vec_out[4],
        grad_w_out,
        grad_w_in,
        vec_out[6],
        grad_w_fc2,
        vec_out[5],
    )


def solution(mesh):
    n_dp, n_ctx = mesh.shape["dp"], mesh.shape["ctx"]
    split = Mesh(mesh.devices.reshape(n_dp, GROUP_IN, n_ctx // GROUP_IN), ALL_AXES)
    mat, vec, group = P(ALL_AXES, None), P(ALL_AXES), P("dp", None)
    return jax.shard_map(
        body,
        mesh=split,
        in_specs=(mat, group, group, vec, vec, vec, vec, mat, vec, mat, mat, vec, mat, vec, mat),
        out_specs=(mat, mat, vec, vec, vec, vec, mat, vec, mat, mat, vec, mat, vec),
        check_vma=False,
    )
```

```python
import functools

import jax
import jax.numpy as jnp
from jax import lax
from jax.experimental import pallas as pl
from jax.experimental.pallas import tpu as pltpu
from jax.sharding import Mesh
from jax.sharding import PartitionSpec as P

HEAD = 64
ROT = 16
LONGEST = 2048
GROUP_IN = 4
TILE = 256
EPS = 1e-05
NEG = -1e30
F32 = jnp.float32
BF16 = jnp.bfloat16
G_AXES = ("dp", "out")
ALL_AXES = ("dp", "in", "out")


def dot(a, b):
    return jnp.dot(a, b, preferred_element_type=F32)


def dot_nt(a, b):
    return lax.dot_general(a, b, (((1,), (1,)), ((), ())), preferred_element_type=F32)


def dot_tn(a, b):
    return lax.dot_general(a, b, (((0,), (0,)), ((), ())), preferred_element_type=F32)


def xor_swap(value, axis, size, step):
    return lax.ppermute(value, axis, [(i, i ^ step) for i in range(size)])


def rotary(x, cos, sin_l, sin_r, sign):
    left = pltpu.roll(x, 128 - ROT // 2, 1)
    right = pltpu.roll(x, ROT // 2, 1)
    return x * cos - sign * (left * sin_l) + sign * (right * sin_r)


def pair_up(x, block):
    blocks = [x[i : i + block] for i in range(0, x.shape[0], block)]
    return jnp.concatenate([jnp.concatenate(blocks[i : i + 2], axis=1) for i in range(0, len(blocks), 2)], axis=0)


def unpair(x, block):
    parts = []
    for i in range(0, x.shape[0], block):
        parts += [x[i : i + block, :HEAD], x[i : i + block, HEAD:]]
    return jnp.concatenate(parts, axis=0)


def params(flops, size, exps=0):
    return dict(
        compiler_params=pltpu.CompilerParams(vmem_limit_bytes=40 * 2**20),
        cost_estimate=pl.CostEstimate(flops=flops, bytes_accessed=size, transcendentals=exps),
    )


def row_at(i, z):
    return (i, 0)


def whole_at(i, z):
    return (0, 0)


def slab_at(i, z):
    return (0, i, 0)


def normalized(x_ref):
    x = x_ref[...].astype(F32)
    centred = x - jnp.mean(x, axis=-1, keepdims=True)
    return centred * lax.rsqrt(jnp.mean(centred * centred, axis=-1, keepdims=True) + EPS)


def prep_kernel(heads, block, z_ref, x_ref, norm_ref, w_ref, b_ref, cos_ref, sl_ref, sr_ref, qk_ref, v_ref, n1_ref, n2_ref):
    z = z_ref[0]
    xhat = normalized(x_ref)
    n1 = (xhat * norm_ref[0:1] + norm_ref[1:2]).astype(BF16)
    n1_ref[...] = n1
    n2_ref[...] = (xhat * norm_ref[2:3] + norm_ref[3:4]).astype(BF16)
    joined = dot(n1, w_ref[...]) + b_ref[...]
    cos, sl, sr = cos_ref[...], sl_ref[...], sr_ref[...]
    cols = heads * HEAD
    for h in range(heads):
        at = h * HEAD
        part = jnp.concatenate([joined[:, at : at + HEAD], joined[:, cols + at : cols + at + HEAD]], axis=1)
        qk_ref[z ^ h] = rotary(part, cos, sl, sr, 1.0).astype(BF16)
        v_ref[z ^ h] = pair_up(joined[:, 2 * cols + at : 2 * cols + at + HEAD], block).astype(BF16)


def prep(z, x, norms, w, bias, cos, sl, sr, block):
    rows, width = x.shape
    heads = w.shape[1] // (3 * HEAD)
    table = pl.BlockSpec((TILE, 2 * HEAD), row_at)
    tile = pl.BlockSpec((TILE, width), row_at)
    norm = jax.ShapeDtypeStruct((rows, width), BF16)
    return pl.pallas_call(
        functools.partial(prep_kernel, heads, block),
        grid_spec=pltpu.PrefetchScalarGridSpec(
            num_scalar_prefetch=1,
            grid=(rows // TILE,),
            in_specs=[
                tile,
                pl.BlockSpec(norms.shape, whole_at),
                pl.BlockSpec(w.shape, whole_at),
                pl.BlockSpec(bias.shape, whole_at),
                table,
                table,
                table,
            ],
            out_specs=[
                pl.BlockSpec((heads, TILE, 2 * HEAD), slab_at),
                pl.BlockSpec((heads, TILE // 2, 2 * HEAD), slab_at),
                tile,
                tile,
            ],
        ),
        out_shape=[
            jax.ShapeDtypeStruct((heads, rows, 2 * HEAD), BF16),
            jax.ShapeDtypeStruct((heads, rows // 2, 2 * HEAD), BF16),
            norm,
            norm,
        ],
        **params(2 * rows * width * w.shape[1], 12 * 2**20),
    )(z, x, norms, w, bias, cos, sl, sr)


def feed_kernel(x_ref, n2_ref, dy_ref, norm_ref, w_in_ref, w_fc2_ref, b_ref, h_ref, du_ref, y_ref, dx_ref, sums_ref, db_ref):
    up = dot(n2_ref[...], w_in_ref[...]) + b_ref[...]
    cdf = 0.5 + 0.5 * lax.erf(up * (0.5**0.5))
    hidden = (up * cdf).astype(BF16)
    slope = cdf + up * (jnp.exp(-0.5 * up * up) * 0.3989422804014327)
    grad_up = (dot_nt(dy_ref[...], w_fc2_ref[...]) * slope).astype(BF16)
    h_ref[...] = hidden
    du_ref[...] = grad_up
    y_ref[...] = dot(hidden, w_fc2_ref[...])
    grad_norm = dot_nt(grad_up, w_in_ref[...])
    dx_ref[...] = grad_norm * norm_ref[2:3]
    gain = jnp.sum(grad_norm * normalized(x_ref), axis=0, keepdims=True)
    shift = jnp.sum(grad_norm, axis=0, keepdims=True)
    bias = jnp.sum(grad_up.astype(F32), axis=0, keepdims=True)

    @pl.when(pl.program_id(0) == 0)
    def _():
        sums_ref[...] = jnp.zeros_like(sums_ref)
        db_ref[...] = jnp.zeros_like(db_ref)

    sums_ref[0:1] += gain
    sums_ref[1:2] += shift
    db_ref[0:1] += bias


def feed(x, n2, dy, norms, w_in, w_fc2, bias):
    rows, width = x.shape
    units = w_in.shape[1]
    row, whole = lambda i: (i, 0), lambda i: (0, 0)
    tile, tile_ff = pl.BlockSpec((TILE, width), row), pl.BlockSpec((TILE, units), row)
    return pl.pallas_call(
        feed_kernel,
        grid=(rows // TILE,),
        in_specs=[
            tile,
            tile,
            tile,
            pl.BlockSpec(norms.shape, whole),
            pl.BlockSpec(w_in.shape, whole),
            pl.BlockSpec(w_fc2.shape, whole),
            pl.BlockSpec(bias.shape, whole),
        ],
        out_specs=[
            tile_ff,
            tile_ff,
            tile,
            tile,
            pl.BlockSpec((8, width), whole),
            pl.BlockSpec((8, units), whole),
        ],
        out_shape=[
            jax.ShapeDtypeStruct((rows, units), BF16),
            jax.ShapeDtypeStruct((rows, units), BF16),
            jax.ShapeDtypeStruct((rows, width), F32),
            jax.ShapeDtypeStruct((rows, width), F32),
            jax.ShapeDtypeStruct((8, width), F32),
            jax.ShapeDtypeStruct((8, units), F32),
        ],
        **params(8 * rows * width * units, 24 * 2**20, 2 * rows * units),
    )(x, n2, dy, norms, w_in, w_fc2, bias)


def grad_att_kernel(heads, block, z_ref, dy_ref, wo_ref, do_ref):
    z = z_ref[0]
    grad = dot_nt(dy_ref[...], wo_ref[...])
    for h in range(heads):
        do_ref[z ^ h] = pair_up(grad[:, h * HEAD : (h + 1) * HEAD], block).astype(BF16)


def grad_att(z, dy, wo, block):
    rows, width = dy.shape
    heads = wo.shape[0] // HEAD
    return pl.pallas_call(
        functools.partial(grad_att_kernel, heads, block),
        grid_spec=pltpu.PrefetchScalarGridSpec(
            num_scalar_prefetch=1,
            grid=(rows // TILE,),
            in_specs=[pl.BlockSpec((TILE, width), row_at), pl.BlockSpec(wo.shape, whole_at)],
            out_specs=pl.BlockSpec((heads, TILE // 2, 2 * HEAD), slab_at),
        ),
        out_shape=jax.ShapeDtypeStruct((heads, rows // 2, 2 * HEAD), BF16),
        **params(2 * rows * width * wo.shape[0], 4 * 2**20),
    )(z, dy, wo)


def merge_heads_kernel(heads, block, z_ref, part_ref, o_ref):
    z = z_ref[0]
    for h in range(0, heads, 2):
        one, two = unpair(part_ref[z ^ h].astype(F32), block), unpair(part_ref[z ^ (h + 1)].astype(F32), block)
        o_ref[:, h * HEAD : (h + 2) * HEAD] = jnp.concatenate([one, two], axis=1).astype(BF16)


def merge_heads(z, parts, block):
    heads, half_rows, _ = parts.shape
    return pl.pallas_call(
        functools.partial(merge_heads_kernel, heads, block),
        grid_spec=pltpu.PrefetchScalarGridSpec(
            num_scalar_prefetch=1,
            grid=(2 * half_rows // TILE,),
            in_specs=[pl.BlockSpec((heads, TILE // 2, 2 * HEAD), slab_at)],
            out_specs=pl.BlockSpec((TILE, heads * HEAD), row_at),
        ),
        out_shape=jax.ShapeDtypeStruct((2 * half_rows, heads * HEAD), BF16),
        **params(half_rows * 1024, 2**20),
    )(z, parts)


def post_kernel(
    heads, block, z_ref, dqk_ref, dv_ref, x_ref, dx_ref, norm_ref, w_ref, cos_ref, sl_ref, sr_ref, da_ref, sum_ref, sums_ref, db_ref
):
    z = z_ref[0]
    cos, sl, sr = cos_ref[...], sl_ref[...], sr_ref[...]
    cols = heads * HEAD
    for h in range(0, heads, 2):
        at = h * HEAD
        one = rotary(dqk_ref[z ^ h].astype(F32), cos, sl, sr, -1.0)
        two = rotary(dqk_ref[z ^ (h + 1)].astype(F32), cos, sl, sr, -1.0)
        da_ref[:, at : at + 2 * HEAD] = jnp.concatenate([one[:, :HEAD], two[:, :HEAD]], axis=1).astype(BF16)
        da_ref[:, cols + at : cols + at + 2 * HEAD] = jnp.concatenate([one[:, HEAD:], two[:, HEAD:]], axis=1).astype(BF16)
        one, two = unpair(dv_ref[z ^ h].astype(F32), block), unpair(dv_ref[z ^ (h + 1)].astype(F32), block)
        da_ref[:, 2 * cols + at : 2 * cols + at + 2 * HEAD] = jnp.concatenate([one, two], axis=1).astype(BF16)
    grad = da_ref[...]
    grad_norm = dot_nt(grad, w_ref[...])
    sum_ref[...] = (dx_ref[...] + grad_norm * norm_ref[0:1]).astype(BF16)
    gain = jnp.sum(grad_norm * normalized(x_ref), axis=0, keepdims=True)
    shift = jnp.sum(grad_norm, axis=0, keepdims=True)
    bias = jnp.sum(grad.astype(F32), axis=0, keepdims=True)

    @pl.when(pl.program_id(0) == 0)
    def _():
        sums_ref[...] = jnp.zeros_like(sums_ref)
        db_ref[...] = jnp.zeros_like(db_ref)

    sums_ref[0:1] += gain
    sums_ref[1:2] += shift
    db_ref[0:1] += bias


def post(z, dqk, dv, x, dx, norms, w, cos, sl, sr, block):
    heads, rows, _ = dqk.shape
    width = x.shape[1]
    three = heads * 3 * HEAD
    table = pl.BlockSpec((TILE, 2 * HEAD), row_at)
    tile = pl.BlockSpec((TILE, width), row_at)
    return pl.pallas_call(
        functools.partial(post_kernel, heads, block),
        grid_spec=pltpu.PrefetchScalarGridSpec(
            num_scalar_prefetch=1,
            grid=(rows // TILE,),
            in_specs=[
                pl.BlockSpec((heads, TILE, 2 * HEAD), slab_at),
                pl.BlockSpec((heads, TILE // 2, 2 * HEAD), slab_at),
                tile,
                tile,
                pl.BlockSpec(norms.shape, whole_at),
                pl.BlockSpec(w.shape, whole_at),
                table,
                table,
                table,
            ],
            out_specs=[
                pl.BlockSpec((TILE, three), row_at),
                tile,
                pl.BlockSpec((8, width), whole_at),
                pl.BlockSpec((8, three), whole_at),
            ],
        ),
        out_shape=[
            jax.ShapeDtypeStruct((rows, three), BF16),
            jax.ShapeDtypeStruct((rows, width), BF16),
            jax.ShapeDtypeStruct((8, width), F32),
            jax.ShapeDtypeStruct((8, three), F32),
        ],
        **params(2 * rows * width * three, 14 * 2**20),
    )(z, dqk, dv, x, dx, norms, w, cos, sl, sr)


def doc_start(packed, ends_ref, count):
    start = packed * 0
    for d in range(count):
        start = jnp.where(packed >= ends_ref[d], ends_ref[d], start)
    return start


def doc_end(packed, ends_ref, count):
    end = ends_ref[count - 1]
    for d in range(count - 2, -1, -1):
        end = jnp.where(packed < ends_ref[d], ends_ref[d], end)
    return end


def tile_at(i):
    return pl.ds(pl.multiple_of(i * TILE, TILE), TILE)


def load_half(ref, source, block):
    both = ref[pl.ds(pl.multiple_of((source // 2) * block, block), block), :].astype(F32)
    return jnp.where(source % 2 == 0, both[:, :HEAD], both[:, HEAD:])


def masked_scores(k_s, q_t, ends_ref, count, i, j):
    s = dot(k_s[tile_at(j), :], q_t[:HEAD, tile_at(i)])
    key_at = lax.broadcasted_iota(jnp.int32, (TILE, TILE), 0)
    query_at = lax.broadcasted_iota(jnp.int32, (TILE, TILE), 1)
    query_row = i * TILE + lax.broadcasted_iota(jnp.int32, (1, TILE), 1)
    first = doc_start(query_row, ends_ref, count) - j * TILE
    last = (i - j) * TILE + query_at
    return jnp.where((key_at >= first) & (key_at <= last), s, NEG)


def forward_kernel(block, count, source_ref, packed_ref, ends_ref, qk_ref, v_ref, o_ref, o_t, lse_ref, k_s, q_t, v_t, o_s):
    rows = qk_ref.shape[0]
    tiles = rows // TILE
    per = TILE // block
    scale = HEAD ** (-0.5)

    def gather(i, carry):
        qk, v = [], []
        for b in range(per):
            src = source_ref[i * per + b]
            qk.append(qk_ref[pl.ds(pl.multiple_of(src * block, block), block), :].astype(F32))
            v.append(load_half(v_ref, src, block))
        qk, v = jnp.concatenate(qk, axis=0), jnp.concatenate(v, axis=0)
        k_s[tile_at(i), :] = qk[:, HEAD:].astype(BF16)
        q_t[:, tile_at(i)] = (qk.T[:HEAD] * scale).astype(BF16)
        v_t[:, tile_at(i)] = v.T.astype(BF16)
        return carry

    lax.fori_loop(0, tiles, gather, 0)

    def forward(i, carry):
        def step(j, state):
            top, total, acc = state
            s = masked_scores(k_s, q_t, ends_ref, count, i, j)
            new_top = jnp.maximum(top, jnp.max(s, axis=0, keepdims=True))
            p = jnp.exp(s - new_top)
            fade = jnp.exp(top - new_top)
            total = total * fade + jnp.sum(p, axis=0, keepdims=True)
            acc = acc * fade + dot(v_t[:, tile_at(j)], p.astype(BF16))
            return new_top, total, acc

        low = doc_start(i * TILE, ends_ref, count) // TILE
        top, total, acc = lax.fori_loop(
            low, i + 1, step, (jnp.full((1, TILE), NEG, F32), jnp.zeros((1, TILE), F32), jnp.zeros((HEAD, TILE), F32))
        )
        out = acc / total
        lse_ref[:, tile_at(i)] = top + jnp.log(total)
        o_t[:, tile_at(i)] = out
        o_s[tile_at(i), :] = out.T
        return carry

    lax.fori_loop(0, tiles, forward, 0)

    def scatter(i, carry):
        both = [o_s[pl.ds(pl.multiple_of(packed_ref[2 * i + b] * block, block), block), :] for b in range(2)]
        o_ref[pl.ds(pl.multiple_of(i * block, block), block), :] = jnp.concatenate(both, axis=1).astype(BF16)
        return carry

    lax.fori_loop(0, rows // (2 * block), scatter, 0)


def backward_kernel(
    block, count, source_ref, packed_ref, ends_ref, qk_ref, v_ref, do_ref, o_t, lse_ref, dqk_ref, dv_ref, q_s, k_s, v_s, do_s, qk_t, do_t, dq_t, delta_s, dk_s, dv_s
):
    rows = qk_ref.shape[0]
    tiles = rows // TILE
    per = TILE // block
    scale = HEAD ** (-0.5)

    def gather(i, carry):
        qk, v, do = [], [], []
        for b in range(per):
            src = source_ref[i * per + b]
            qk.append(qk_ref[pl.ds(pl.multiple_of(src * block, block), block), :].astype(F32))
            v.append(load_half(v_ref, src, block))
            do.append(load_half(do_ref, src, block))
        qk, v, do = jnp.concatenate(qk, axis=0), jnp.concatenate(v, axis=0), jnp.concatenate(do, axis=0)
        here = tile_at(i)
        q_s[here, :] = (qk[:, :HEAD] * scale).astype(BF16)
        k_s[here, :] = qk[:, HEAD:].astype(BF16)
        turned = qk.T
        qk_t[:HEAD, here] = (turned[:HEAD] * scale).astype(BF16)
        qk_t[HEAD:, here] = turned[HEAD:].astype(BF16)
        v_s[here, :] = v.astype(BF16)
        do_s[here, :] = do.astype(BF16)
        do_turned = do.T
        do_t[:, here] = do_turned.astype(BF16)
        dq_t[:, here] = jnp.zeros((HEAD, TILE), F32)
        delta_s[:, here] = jnp.sum(o_t[:, here] * do_turned, axis=0, keepdims=True)
        return carry

    lax.fori_loop(0, tiles, gather, 0)

    def backward(j, carry):
        keys = tile_at(j)

        def step(i, state):
            dk, dv = state
            here = tile_at(i)
            p = jnp.exp(masked_scores(k_s, qk_t, ends_ref, count, i, j) - lse_ref[:, here])
            dp = dot(v_s[keys, :], do_t[:, here])
            ds = (p * (dp - delta_s[:, here])).astype(BF16)
            dv = dv + dot(p.astype(BF16), do_s[here, :])
            dk = dk + dot(ds, q_s[here, :])
            dq_t[:, here] += dot(qk_t[HEAD:, keys], ds)
            return dk, dv

        high = (doc_end(j * TILE + TILE - 1, ends_ref, count) - 1) // TILE
        zero = jnp.zeros((TILE, HEAD), F32)
        dk, dv = lax.fori_loop(j, high + 1, step, (zero, zero))
        dk_s[keys, :] = dk
        dv_s[keys, :] = dv
        return carry

    lax.fori_loop(0, tiles, backward, 0)

    def scatter(i, carry):
        here = tile_at(i)
        dq = (dq_t[:, here] * scale).T
        dqk = jnp.concatenate([dq, dk_s[here, :]], axis=1).astype(BF16)
        for b in range(per):
            dst = pl.ds(pl.multiple_of(source_ref[i * per + b] * block, block), block)
            dqk_ref[dst, :] = dqk[b * block : (b + 1) * block, :]
        return carry

    lax.fori_loop(0, tiles, scatter, 0)

    def scatter_v(i, carry):
        both = [dv_s[pl.ds(pl.multiple_of(packed_ref[2 * i + b] * block, block), block), :] for b in range(2)]
        dv_ref[pl.ds(pl.multiple_of(i * block, block), block), :] = jnp.concatenate(both, axis=1).astype(BF16)
        return carry

    lax.fori_loop(0, rows // (2 * block), scatter_v, 0)


IN_VMEM = pl.BlockSpec(memory_space=pltpu.VMEM)
IN_SMEM = pl.BlockSpec(memory_space=pltpu.SMEM)


def attend_forward(source, packed, ends, qk, v, block):
    rows = qk.shape[0]
    turned = pltpu.VMEM((HEAD, rows), BF16)
    return pl.pallas_call(
        functools.partial(forward_kernel, block, ends.shape[0]),
        in_specs=[IN_SMEM] * 3 + [IN_VMEM] * 2,
        out_specs=[IN_VMEM] * 3,
        out_shape=[
            jax.ShapeDtypeStruct((rows // 2, 2 * HEAD), BF16),
            jax.ShapeDtypeStruct((HEAD, rows), F32),
            jax.ShapeDtypeStruct((1, rows), F32),
        ],
        scratch_shapes=[pltpu.VMEM((rows, HEAD), BF16), turned, turned, pltpu.VMEM((rows, HEAD), F32)],
        **params(rows * rows * HEAD * 4, 6 * rows * HEAD * 2, rows * rows),
    )(source, packed, ends, qk, v)


def attend_backward(source, packed, ends, qk, v, do, o_t, lse, block):
    rows = qk.shape[0]
    half = pltpu.VMEM((rows, HEAD), BF16)
    wide = pltpu.VMEM((rows, HEAD), F32)
    return pl.pallas_call(
        functools.partial(backward_kernel, block, ends.shape[0]),
        in_specs=[IN_SMEM] * 3 + [IN_VMEM] * 5,
        out_specs=[IN_VMEM] * 2,
        out_shape=[
            jax.ShapeDtypeStruct((rows, 2 * HEAD), BF16),
            jax.ShapeDtypeStruct((rows // 2, 2 * HEAD), BF16),
        ],
        scratch_shapes=[
            half,
            half,
            half,
            half,
            pltpu.VMEM((2 * HEAD, rows), BF16),
            pltpu.VMEM((HEAD, rows), BF16),
            pltpu.VMEM((HEAD, rows), F32),
            pltpu.VMEM((1, rows), F32),
            wide,
            wide,
        ],
        **params(rows * rows * HEAD * 10, 12 * rows * HEAD * 2, rows * rows),
    )(source, packed, ends, qk, v, do, o_t, lse)


def join_in(value, far):
    far = jnp.stack([value, far])
    near = xor_swap(far, "in", GROUP_IN, 1)
    return jnp.stack([far[0], near[0], far[1], near[1]])


def scatter_in(parts):
    half = parts.shape[-1] // 2
    sums = []
    for at in (0, half):
        cut = slice(at, at + half)
        near = xor_swap(jnp.stack([parts[1, :, cut], parts[3, :, cut]]), "in", GROUP_IN, 1)
        far = (parts[2, :, cut].astype(F32) + near[1].astype(F32)).astype(BF16)
        far = xor_swap(far, "in", GROUP_IN, 2)
        sums.append(parts[0, :, cut].astype(F32) + near[0].astype(F32) + far.astype(F32))
    return jnp.concatenate(sums, axis=1)


def exchange_in(parts, t):
    here = [lax.dynamic_index_in_dim(parts, t ^ s, 0, keepdims=False) for s in range(GROUP_IN)]
    there = [here[0]] + [xor_swap(here[s], "in", GROUP_IN, s) for s in range(1, GROUP_IN)]
    stacked = jnp.stack(there)
    return jnp.stack([lax.dynamic_index_in_dim(stacked, t ^ u, 0, keepdims=False) for u in range(GROUP_IN)])


def exchange_out(parts, size):
    return jnp.stack([parts[0]] + [xor_swap(parts[s], "out", size, s) for s in range(1, size)])


def body(
    tokens,
    seq_lengths,
    dealing,
    ln1_gain,
    ln1_bias,
    ln2_gain,
    ln2_bias,
    w_qkv,
    b_qkv,
    w_out,
    w_in,
    b_in,
    w_fc2,
    b_out,
    cotangent,
):
    n_dp, n_out, n_in = lax.axis_size("dp"), lax.axis_size("out"), lax.axis_size("in")
    n_g = n_dp * n_out
    n_all = n_g * n_in
    rows_dev, width = tokens.shape
    ff = w_in.shape[1]
    ff_in = ff // n_in
    r_w = w_in.shape[0]
    r_ff = w_fc2.shape[0]
    block = LONGEST // (2 * n_out * n_in)
    slots_dev = rows_dev // block
    heads = width // HEAD
    h_in = heads // n_in
    cols = h_in * HEAD
    rows = rows_dev * n_in
    z, t = lax.axis_index("out"), lax.axis_index("in")
    z_arr = z[None].astype(jnp.int32)
    lengths, order = seq_lengths[0], dealing[0]
    ends = jnp.cumsum(lengths)

    slots = order.shape[0]
    ids = jnp.arange(slots, dtype=jnp.int32)
    slot_of = jnp.sum(jnp.where(order[None, :] == ids[:, None], ids[None, :], 0), axis=1)
    chunk = slot_of // slots_dev
    source = (((chunk % n_out) ^ z) * n_in + ((chunk // n_out) ^ t)) * slots_dev + slot_of % slots_dev
    source = source.astype(jnp.int32)
    lies = ids // slots_dev
    slot_here = (((lies % n_in) ^ t) * n_out + ((lies // n_in) ^ z)) * slots_dev + ids % slots_dev
    packed_of = jnp.sum(jnp.where(slot_here[:, None] == ids[None, :], order[None, :], 0), axis=1).astype(jnp.int32)

    part = jnp.arange(rows, dtype=jnp.int32)
    packed = packed_of[: rows // block].reshape(-1, 1) * block + jnp.arange(block, dtype=jnp.int32)[None, :]
    packed = packed.reshape(rows)
    starts = jnp.max(jnp.where(packed[:, None] >= ends[None, :], ends[None, :], 0), axis=1)
    position = (packed - starts).astype(F32)
    lane = jnp.arange(2 * HEAD, dtype=jnp.int32) % HEAD
    half = ROT // 2
    freq = 10000.0 ** (-2.0 * (lane % half).astype(F32) / ROT)
    phase = position[:, None] * freq[None, :]
    cos = jnp.where(lane < ROT, jnp.cos(phase), 1.0)
    sine = jnp.sin(phase)
    sin_l = jnp.where(lane < half, sine, 0.0)
    sin_r = jnp.where((lane >= half) & (lane < ROT), sine, 0.0)

    vectors = [ln1_gain, ln1_bias, ln2_gain, ln2_bias, b_qkv, b_out, b_in]
    sizes = [v.shape[0] for v in vectors]
    n_vec = sum(sizes)
    vec_cols = n_vec // r_w
    x_far = xor_swap(tokens, "in", n_in, 2)
    qkv_cols = jnp.transpose(w_qkv.reshape(r_w, 3, n_in, cols), (2, 0, 1, 3)).reshape(n_in, r_w, 3 * cols)
    in_cols = jnp.transpose(w_in.reshape(r_w, n_dp, n_in, n_out, r_ff), (2, 0, 1, 3, 4)).reshape(n_in, r_w, ff_in)
    vec = jnp.pad(jnp.concatenate(vectors).reshape(r_w, vec_cols), ((0, 0), (0, 128 - vec_cols)))
    vec = jnp.broadcast_to(vec[None], (n_in, r_w, 128))
    joined_cols = exchange_in(jnp.concatenate([qkv_cols, vec, in_cols], axis=2), t).reshape(n_in * r_w, -1)
    home = []
    for b in range(n_all):
        t_to, g_to = b // n_g, b % n_g
        home.append((b, ((g_to // n_out) * n_in + t_to) * n_out + g_to % n_out))
    out_rows = lax.ppermute(w_out, ALL_AXES, home).reshape(n_in * r_w, cols)
    first = jnp.concatenate([joined_cols[:, : 3 * cols + 128], out_rows], axis=1)
    first, x_far, cotangent = lax.optimization_barrier((first, x_far, cotangent))
    dy_far = xor_swap(cotangent, "in", n_in, 2)
    first = lax.all_gather(first, G_AXES, axis=0, tiled=False)
    second = jnp.concatenate([joined_cols[:, 3 * cols + 128 :], w_fc2], axis=1)
    second = lax.all_gather(second, G_AXES, axis=0, tiled=False)

    def natural(value):
        value = value.reshape(n_dp, n_out, n_in, r_w, -1)
        return jnp.transpose(value, (0, 2, 1, 3, 4)).reshape(n_all * r_w, -1)

    def by_owner(value):
        value = value.reshape(n_dp, n_in, n_out, r_w, -1)
        return jnp.transpose(value, (0, 2, 1, 3, 4)).reshape(n_g, n_in * r_w, -1)

    weight_qkv = natural(first[:, :, : 3 * cols])
    weight_out = first[:, :, 3 * cols + 128 :].reshape(cols, width)
    weight_in = natural(second[:, :, :ff_in])
    weight_fc2 = second[:, :, ff_in:].reshape(ff_in, width)
    vec_all = first[:, :, 3 * cols : 3 * cols + vec_cols].reshape(n_dp, n_out, n_in, n_vec).astype(F32)
    vec_all = jnp.transpose(vec_all, (0, 2, 1, 3))
    spans, at = [], 0
    for size in sizes:
        spans.append(vec_all[..., at : at + size])
        at += size
    gain_one, shift_one, gain_two, shift_two = [s.reshape(width) for s in spans[:4]]
    bias_out = spans[5].reshape(width)
    bias_in = lax.dynamic_index_in_dim(spans[6], t, 1, keepdims=False).reshape(ff_in)
    bias_qkv = lax.dynamic_index_in_dim(spans[4].reshape(3, n_in, cols), t, 1, keepdims=False).reshape(-1)
    norms = jnp.concatenate([jnp.stack([gain_one, shift_one, gain_two, shift_two]), jnp.zeros((4, width), F32)])

    x_all = join_in(tokens, x_far).reshape(rows, width)
    dy_all = join_in(cotangent, dy_far).reshape(rows, width)

    qk, v, n1, n2 = prep(z_arr, x_all, norms, weight_qkv, bias_qkv[None], cos, sin_l, sin_r, block)
    qk = exchange_out(qk, n_out).reshape(n_out * rows, 2 * HEAD)
    v = exchange_out(v, n_out).reshape(n_out * rows // 2, 2 * HEAD)
    do = grad_att(z_arr, dy_all, weight_out, block)
    do = exchange_out(do, n_out).reshape(n_out * rows // 2, 2 * HEAD)
    o, o_t, lse = attend_forward(source, packed_of, ends, qk, v, block)
    o = exchange_out(o.reshape(n_out, rows // 2, 2 * HEAD), n_out)

    hidden, grad_up, y_ff, dx_ff, sums_two, grad_b_in = feed(x_all, n2, dy_all, norms, weight_in, weight_fc2, bias_in[None])
    grad_fc2 = dot_tn(hidden, dy_all)
    grad_in = dot_tn(n2, grad_up)
    second_grads = jnp.concatenate(
        [by_owner(grad_in.astype(BF16)), grad_fc2.astype(BF16).reshape(n_g, r_ff, width)], axis=2
    )

    o = merge_heads(z_arr, o, block)
    y_part = (y_ff + dot(o, weight_out)).astype(BF16)

    do, second_grads, y_part = lax.optimization_barrier((do, second_grads, y_part))
    second_grads = lax.psum_scatter(second_grads, G_AXES, scatter_dimension=0, tiled=False)
    own = tokens.astype(F32)
    mixed = (own + scatter_in(y_part.reshape(n_in, rows_dev, width)) + bias_out).astype(BF16)
    dqk, dv = attend_backward(source, packed_of, ends, qk, v, do, o_t, lse, block)
    dqk = exchange_out(dqk.reshape(n_out, rows, 2 * HEAD), n_out)
    dv = exchange_out(dv.reshape(n_out, rows // 2, 2 * HEAD), n_out)
    dqk, dv, mixed, second_grads = lax.optimization_barrier((dqk, dv, mixed, second_grads))
    da, w_parts, sums_one, grad_b_qkv = post(
        z_arr, dqk, dv, x_all, dx_ff, norms, weight_qkv, cos, sin_l, sin_r, block
    )

    grad_qkv = dot_tn(n1, da)
    grad_out = dot_tn(o, dy_all)

    def placed(vector, axis):
        spread = jnp.expand_dims(vector, axis)
        mask = (jnp.arange(n_in) == t).reshape([-1 if a == axis else 1 for a in range(spread.ndim)])
        return jnp.where(mask, spread, 0.0).reshape(-1)

    grad_own = cotangent.astype(F32)
    vec_grads = [
        sums_one[0],
        sums_one[1],
        sums_two[0],
        sums_two[1],
        placed(grad_b_qkv[0].reshape(3, cols), 1),
        jnp.sum(grad_own, axis=0),
        placed(grad_b_in[0].reshape(n_dp, n_out, r_ff), 1),
    ]
    vec_grads = jnp.concatenate([v.reshape(n_dp, n_in, n_out, -1) for v in vec_grads], axis=3)
    vec_grads = jnp.transpose(vec_grads, (0, 2, 1, 3)).reshape(n_g, n_in * r_w, vec_cols)
    vec_grads = jnp.pad(vec_grads, ((0, 0), (0, 0), (0, 128 - vec_cols)))
    first_grads = jnp.concatenate(
        [
            by_owner(grad_qkv.astype(BF16)),
            vec_grads.astype(BF16),
            grad_out.astype(BF16).reshape(n_g, n_in * r_w, cols),
        ],
        axis=2,
    )
    first_grads = lax.psum_scatter(first_grads, G_AXES, scatter_dimension=0, tiled=False)

    in_part = exchange_in(second_grads[:, :ff_in].reshape(n_in, r_w, ff_in), t)
    in_part = in_part.reshape(n_in, r_w, n_dp, n_out, r_ff)
    grad_w_in = jnp.transpose(in_part, (1, 2, 0, 3, 4)).reshape(r_w, ff).astype(F32)
    grad_w_fc2 = second_grads[:, ff_in:].astype(F32)
    back_home = [(b, a) for a, b in home]
    out_part = first_grads[:, 3 * cols + 128 :].reshape(r_w, width)
    grad_w_out = lax.ppermute(out_part, ALL_AXES, back_home).astype(F32)
    qkv_part = exchange_in(first_grads[:, : 3 * cols + 128].reshape(n_in, r_w, 3 * cols + 128), t)
    qkv_grad = jnp.transpose(qkv_part[:, :, : 3 * cols].reshape(n_in, r_w, 3, cols), (1, 2, 0, 3))
    grad_w_qkv = qkv_grad.reshape(r_w, 3 * width).astype(F32)
    vec_part = qkv_part[:, :, 3 * cols : 3 * cols + vec_cols].reshape(n_in, n_vec).astype(F32)
    vec_part = jnp.sum(vec_part, axis=0)
    vec_out, at = [], 0
    for size in sizes:
        vec_out.append(vec_part[at : at + size])
        at += size

    w_sum = scatter_in(w_parts.reshape(n_in, rows_dev, width))
    centred = own - jnp.mean(own, axis=-1, keepdims=True)
    own_rstd = lax.rsqrt(jnp.mean(centred * centred, axis=-1, keepdims=True) + EPS)
    own_hat = centred * own_rstd
    mean_w = jnp.mean(w_sum, axis=-1, keepdims=True)
    mean_wx = jnp.mean(w_sum * own_hat, axis=-1, keepdims=True)
    grad_tokens = grad_own + own_rstd * (w_sum - mean_w - own_hat * mean_wx)
    return (
        mixed,
        grad_tokens,
        vec_out[0],
        vec_out[1],
        vec_out[2],
        vec_out[3],
        grad_w_qkv,
        vec_out[4],
        grad_w_out,
        grad_w_in,
        vec_out[6],
        grad_w_fc2,
        vec_out[5],
    )


def solution(mesh):
    n_dp, n_ctx = mesh.shape["dp"], mesh.shape["ctx"]
    split = Mesh(mesh.devices.reshape(n_dp, GROUP_IN, n_ctx // GROUP_IN), ALL_AXES)
    mat, vec, group = P(ALL_AXES, None), P(ALL_AXES), P("dp", None)
    return jax.shard_map(
        body,
        mesh=split,
        in_specs=(mat, group, group, vec, vec, vec, vec, mat, vec, mat, mat, vec, mat, vec, mat),
        out_specs=(mat, mat, vec, vec, vec, vec, mat, vec, mat, mat, vec, mat, vec),
        check_vma=False,
    )
```

```python
import functools

import jax
import jax.numpy as jnp
from jax import lax
from jax.experimental import pallas as pl
from jax.experimental.pallas import tpu as pltpu
from jax.sharding import Mesh
from jax.sharding import PartitionSpec as P

HEAD = 64
ROT = 16
LONGEST = 2048
GROUP_IN = 4
TILE = 256
EPS = 1e-05
NEG = -1e30
F32 = jnp.float32
BF16 = jnp.bfloat16
G_AXES = ("dp", "out")
ALL_AXES = ("dp", "in", "out")


def dot(a, b):
    return jnp.dot(a, b, preferred_element_type=F32)


def dot_nt(a, b):
    return lax.dot_general(a, b, (((1,), (1,)), ((), ())), preferred_element_type=F32)


def dot_tn(a, b):
    return lax.dot_general(a, b, (((0,), (0,)), ((), ())), preferred_element_type=F32)


def xor_swap(value, axis, size, step):
    return lax.ppermute(value, axis, [(i, i ^ step) for i in range(size)])


def rotary(x, cos, sin_l, sin_r, sign):
    left = pltpu.roll(x, 128 - ROT // 2, 1)
    right = pltpu.roll(x, ROT // 2, 1)
    return x * cos - sign * (left * sin_l) + sign * (right * sin_r)


def pair_up(x, block):
    blocks = [x[i : i + block] for i in range(0, x.shape[0], block)]
    return jnp.concatenate([jnp.concatenate(blocks[i : i + 2], axis=1) for i in range(0, len(blocks), 2)], axis=0)


def unpair(x, block):
    parts = []
    for i in range(0, x.shape[0], block):
        parts += [x[i : i + block, :HEAD], x[i : i + block, HEAD:]]
    return jnp.concatenate(parts, axis=0)


def params(flops, size, exps=0):
    return dict(
        compiler_params=pltpu.CompilerParams(vmem_limit_bytes=60 * 2**20),
        cost_estimate=pl.CostEstimate(flops=flops, bytes_accessed=size, transcendentals=exps),
    )


def row_at(i, z):
    return (i, 0)


def whole_at(i, z):
    return (0, 0)


def slab_at(i, z):
    return (0, i, 0)


def normalized(x_ref):
    x = x_ref[...].astype(F32)
    centred = x - jnp.mean(x, axis=-1, keepdims=True)
    return centred * lax.rsqrt(jnp.mean(centred * centred, axis=-1, keepdims=True) + EPS)


def prep_kernel(heads, block, z_ref, x_ref, norm_ref, w_ref, b_ref, cos_ref, sl_ref, sr_ref, qk_ref, v_ref, n1_ref, n2_ref):
    z = z_ref[0]
    xhat = normalized(x_ref)
    n1 = (xhat * norm_ref[0:1] + norm_ref[1:2]).astype(BF16)
    n1_ref[...] = n1
    n2_ref[...] = (xhat * norm_ref[2:3] + norm_ref[3:4]).astype(BF16)
    joined = dot(n1, w_ref[...]) + b_ref[...]
    cos, sl, sr = cos_ref[...], sl_ref[...], sr_ref[...]
    cols = heads * HEAD
    for h in range(heads):
        at = h * HEAD
        part = jnp.concatenate([joined[:, at : at + HEAD], joined[:, cols + at : cols + at + HEAD]], axis=1)
        qk_ref[z ^ h] = rotary(part, cos, sl, sr, 1.0).astype(BF16)
        v_ref[z ^ h] = pair_up(joined[:, 2 * cols + at : 2 * cols + at + HEAD], block).astype(BF16)


def prep(z, x, norms, w, bias, cos, sl, sr, block):
    rows, width = x.shape
    heads = w.shape[1] // (3 * HEAD)
    table = pl.BlockSpec((TILE, 2 * HEAD), row_at)
    tile = pl.BlockSpec((TILE, width), row_at)
    norm = jax.ShapeDtypeStruct((rows, width), BF16)
    return pl.pallas_call(
        functools.partial(prep_kernel, heads, block),
        grid_spec=pltpu.PrefetchScalarGridSpec(
            num_scalar_prefetch=1,
            grid=(rows // TILE,),
            in_specs=[
                tile,
                pl.BlockSpec(norms.shape, whole_at),
                pl.BlockSpec(w.shape, whole_at),
                pl.BlockSpec(bias.shape, whole_at),
                table,
                table,
                table,
            ],
            out_specs=[
                pl.BlockSpec((heads, TILE, 2 * HEAD), slab_at),
                pl.BlockSpec((heads, TILE // 2, 2 * HEAD), slab_at),
                tile,
                tile,
            ],
        ),
        out_shape=[
            jax.ShapeDtypeStruct((heads, rows, 2 * HEAD), BF16),
            jax.ShapeDtypeStruct((heads, rows // 2, 2 * HEAD), BF16),
            norm,
            norm,
        ],
        **params(2 * rows * width * w.shape[1], 12 * 2**20),
    )(z, x, norms, w, bias, cos, sl, sr)


def feed_kernel(x_ref, n2_ref, dy_ref, norm_ref, w_in_ref, w_fc2_ref, b_ref, h_ref, du_ref, y_ref, dx_ref, sums_ref, db_ref):
    up = dot(n2_ref[...], w_in_ref[...]) + b_ref[...]
    cdf = 0.5 + 0.5 * lax.erf(up * (0.5**0.5))
    hidden = (up * cdf).astype(BF16)
    slope = cdf + up * (jnp.exp(-0.5 * up * up) * 0.3989422804014327)
    grad_up = (dot_nt(dy_ref[...], w_fc2_ref[...]) * slope).astype(BF16)
    h_ref[...] = hidden
    du_ref[...] = grad_up
    y_ref[...] = dot(hidden, w_fc2_ref[...])
    grad_norm = dot_nt(grad_up, w_in_ref[...])
    dx_ref[...] = grad_norm * norm_ref[2:3]
    gain = jnp.sum(grad_norm * normalized(x_ref), axis=0, keepdims=True)
    shift = jnp.sum(grad_norm, axis=0, keepdims=True)
    bias = jnp.sum(grad_up.astype(F32), axis=0, keepdims=True)

    @pl.when(pl.program_id(0) == 0)
    def _():
        sums_ref[...] = jnp.zeros_like(sums_ref)
        db_ref[...] = jnp.zeros_like(db_ref)

    sums_ref[0:1] += gain
    sums_ref[1:2] += shift
    db_ref[0:1] += bias


def feed(x, n2, dy, norms, w_in, w_fc2, bias):
    rows, width = x.shape
    units = w_in.shape[1]
    row, whole = lambda i: (i, 0), lambda i: (0, 0)
    tile, tile_ff = pl.BlockSpec((TILE, width), row), pl.BlockSpec((TILE, units), row)
    return pl.pallas_call(
        feed_kernel,
        grid=(rows // TILE,),
        in_specs=[
            tile,
            tile,
            tile,
            pl.BlockSpec(norms.shape, whole),
            pl.BlockSpec(w_in.shape, whole),
            pl.BlockSpec(w_fc2.shape, whole),
            pl.BlockSpec(bias.shape, whole),
        ],
        out_specs=[
            tile_ff,
            tile_ff,
            tile,
            tile,
            pl.BlockSpec((8, width), whole),
            pl.BlockSpec((8, units), whole),
        ],
        out_shape=[
            jax.ShapeDtypeStruct((rows, units), BF16),
            jax.ShapeDtypeStruct((rows, units), BF16),
            jax.ShapeDtypeStruct((rows, width), F32),
            jax.ShapeDtypeStruct((rows, width), F32),
            jax.ShapeDtypeStruct((8, width), F32),
            jax.ShapeDtypeStruct((8, units), F32),
        ],
        **params(8 * rows * width * units, 24 * 2**20, 2 * rows * units),
    )(x, n2, dy, norms, w_in, w_fc2, bias)


def grad_att_kernel(heads, block, z_ref, dy_ref, wo_ref, do_ref):
    z = z_ref[0]
    grad = dot_nt(dy_ref[...], wo_ref[...])
    for h in range(heads):
        do_ref[z ^ h] = pair_up(grad[:, h * HEAD : (h + 1) * HEAD], block).astype(BF16)


def grad_att(z, dy, wo, block):
    rows, width = dy.shape
    heads = wo.shape[0] // HEAD
    return pl.pallas_call(
        functools.partial(grad_att_kernel, heads, block),
        grid_spec=pltpu.PrefetchScalarGridSpec(
            num_scalar_prefetch=1,
            grid=(rows // TILE,),
            in_specs=[pl.BlockSpec((TILE, width), row_at), pl.BlockSpec(wo.shape, whole_at)],
            out_specs=pl.BlockSpec((heads, TILE // 2, 2 * HEAD), slab_at),
        ),
        out_shape=jax.ShapeDtypeStruct((heads, rows // 2, 2 * HEAD), BF16),
        **params(2 * rows * width * wo.shape[0], 4 * 2**20),
    )(z, dy, wo)


def merge_heads_kernel(heads, block, z_ref, part_ref, o_ref):
    z = z_ref[0]
    for h in range(0, heads, 2):
        one, two = unpair(part_ref[z ^ h].astype(F32), block), unpair(part_ref[z ^ (h + 1)].astype(F32), block)
        o_ref[:, h * HEAD : (h + 2) * HEAD] = jnp.concatenate([one, two], axis=1).astype(BF16)


def merge_heads(z, parts, block):
    heads, half_rows, _ = parts.shape
    return pl.pallas_call(
        functools.partial(merge_heads_kernel, heads, block),
        grid_spec=pltpu.PrefetchScalarGridSpec(
            num_scalar_prefetch=1,
            grid=(2 * half_rows // TILE,),
            in_specs=[pl.BlockSpec((heads, TILE // 2, 2 * HEAD), slab_at)],
            out_specs=pl.BlockSpec((TILE, heads * HEAD), row_at),
        ),
        out_shape=jax.ShapeDtypeStruct((2 * half_rows, heads * HEAD), BF16),
        **params(half_rows * 1024, 2**20),
    )(z, parts)


def post_kernel(
    heads, block, z_ref, dqk_ref, dv_ref, x_ref, dx_ref, norm_ref, w_ref, cos_ref, sl_ref, sr_ref, da_ref, sum_ref, sums_ref, db_ref
):
    z = z_ref[0]
    cos, sl, sr = cos_ref[...], sl_ref[...], sr_ref[...]
    cols = heads * HEAD
    for h in range(0, heads, 2):
        at = h * HEAD
        one = rotary(dqk_ref[z ^ h].astype(F32), cos, sl, sr, -1.0)
        two = rotary(dqk_ref[z ^ (h + 1)].astype(F32), cos, sl, sr, -1.0)
        da_ref[:, at : at + 2 * HEAD] = jnp.concatenate([one[:, :HEAD], two[:, :HEAD]], axis=1).astype(BF16)
        da_ref[:, cols + at : cols + at + 2 * HEAD] = jnp.concatenate([one[:, HEAD:], two[:, HEAD:]], axis=1).astype(BF16)
        one, two = unpair(dv_ref[z ^ h].astype(F32), block), unpair(dv_ref[z ^ (h + 1)].astype(F32), block)
        da_ref[:, 2 * cols + at : 2 * cols + at + 2 * HEAD] = jnp.concatenate([one, two], axis=1).astype(BF16)
    grad = da_ref[...]
    grad_norm = dot_nt(grad, w_ref[...])
    sum_ref[...] = (dx_ref[...] + grad_norm * norm_ref[0:1]).astype(BF16)
    gain = jnp.sum(grad_norm * normalized(x_ref), axis=0, keepdims=True)
    shift = jnp.sum(grad_norm, axis=0, keepdims=True)
    bias = jnp.sum(grad.astype(F32), axis=0, keepdims=True)

    @pl.when(pl.program_id(0) == 0)
    def _():
        sums_ref[...] = jnp.zeros_like(sums_ref)
        db_ref[...] = jnp.zeros_like(db_ref)

    sums_ref[0:1] += gain
    sums_ref[1:2] += shift
    db_ref[0:1] += bias


def post(z, dqk, dv, x, dx, norms, w, cos, sl, sr, block):
    heads, rows, _ = dqk.shape
    width = x.shape[1]
    three = heads * 3 * HEAD
    table = pl.BlockSpec((TILE, 2 * HEAD), row_at)
    tile = pl.BlockSpec((TILE, width), row_at)
    return pl.pallas_call(
        functools.partial(post_kernel, heads, block),
        grid_spec=pltpu.PrefetchScalarGridSpec(
            num_scalar_prefetch=1,
            grid=(rows // TILE,),
            in_specs=[
                pl.BlockSpec((heads, TILE, 2 * HEAD), slab_at),
                pl.BlockSpec((heads, TILE // 2, 2 * HEAD), slab_at),
                tile,
                tile,
                pl.BlockSpec(norms.shape, whole_at),
                pl.BlockSpec(w.shape, whole_at),
                table,
                table,
                table,
            ],
            out_specs=[
                pl.BlockSpec((TILE, three), row_at),
                tile,
                pl.BlockSpec((8, width), whole_at),
                pl.BlockSpec((8, three), whole_at),
            ],
        ),
        out_shape=[
            jax.ShapeDtypeStruct((rows, three), BF16),
            jax.ShapeDtypeStruct((rows, width), BF16),
            jax.ShapeDtypeStruct((8, width), F32),
            jax.ShapeDtypeStruct((8, three), F32),
        ],
        **params(2 * rows * width * three, 14 * 2**20),
    )(z, dqk, dv, x, dx, norms, w, cos, sl, sr)


def doc_start(packed, ends_ref, count):
    start = packed * 0
    for d in range(count):
        start = jnp.where(packed >= ends_ref[d], ends_ref[d], start)
    return start


def doc_end(packed, ends_ref, count):
    end = ends_ref[count - 1]
    for d in range(count - 2, -1, -1):
        end = jnp.where(packed < ends_ref[d], ends_ref[d], end)
    return end


def tile_at(i):
    return pl.ds(pl.multiple_of(i * TILE, TILE), TILE)


def load_half(ref, source, block):
    both = ref[pl.ds(pl.multiple_of((source // 2) * block, block), block), :].astype(F32)
    return jnp.where(source % 2 == 0, both[:, :HEAD], both[:, HEAD:])


def masked_scores(k_s, q_t, ends_ref, count, i, j):
    s = dot(k_s[tile_at(j), :], q_t[:HEAD, tile_at(i)])
    key_at = lax.broadcasted_iota(jnp.int32, (TILE, TILE), 0)
    query_at = lax.broadcasted_iota(jnp.int32, (TILE, TILE), 1)
    query_row = i * TILE + lax.broadcasted_iota(jnp.int32, (1, TILE), 1)
    first = doc_start(query_row, ends_ref, count) - j * TILE
    last = (i - j) * TILE + query_at
    return jnp.where((key_at >= first) & (key_at <= last), s, NEG)


def forward_kernel(block, count, source_ref, packed_ref, ends_ref, qk_ref, v_ref, o_ref, o_t, lse_ref, k_s, q_t, v_t, o_s):
    rows = qk_ref.shape[0]
    tiles = rows // TILE
    per = TILE // block
    scale = HEAD ** (-0.5)

    def gather(i, carry):
        qk, v = [], []
        for b in range(per):
            src = source_ref[i * per + b]
            qk.append(qk_ref[pl.ds(pl.multiple_of(src * block, block), block), :].astype(F32))
            v.append(load_half(v_ref, src, block))
        qk, v = jnp.concatenate(qk, axis=0), jnp.concatenate(v, axis=0)
        k_s[tile_at(i), :] = qk[:, HEAD:].astype(BF16)
        q_t[:, tile_at(i)] = (qk.T[:HEAD] * scale).astype(BF16)
        v_t[:, tile_at(i)] = v.T.astype(BF16)
        return carry

    lax.fori_loop(0, tiles, gather, 0)

    def forward(i, carry):
        def step(j, state):
            top, total, acc = state
            s = masked_scores(k_s, q_t, ends_ref, count, i, j)
            new_top = jnp.maximum(top, jnp.max(s, axis=0, keepdims=True))
            p = jnp.exp(s - new_top)
            fade = jnp.exp(top - new_top)
            total = total * fade + jnp.sum(p, axis=0, keepdims=True)
            acc = acc * fade + dot(v_t[:, tile_at(j)], p.astype(BF16))
            return new_top, total, acc

        low = doc_start(i * TILE, ends_ref, count) // TILE
        top, total, acc = lax.fori_loop(
            low, i + 1, step, (jnp.full((1, TILE), NEG, F32), jnp.zeros((1, TILE), F32), jnp.zeros((HEAD, TILE), F32))
        )
        out = acc / total
        lse_ref[:, tile_at(i)] = top + jnp.log(total)
        o_t[:, tile_at(i)] = out
        o_s[tile_at(i), :] = out.T
        return carry

    lax.fori_loop(0, tiles, forward, 0)

    def scatter(i, carry):
        both = [o_s[pl.ds(pl.multiple_of(packed_ref[2 * i + b] * block, block), block), :] for b in range(2)]
        o_ref[pl.ds(pl.multiple_of(i * block, block), block), :] = jnp.concatenate(both, axis=1).astype(BF16)
        return carry

    lax.fori_loop(0, rows // (2 * block), scatter, 0)


def backward_kernel(
    block, count, source_ref, packed_ref, ends_ref, qk_ref, v_ref, do_ref, o_t, lse_ref, dqk_ref, dv_ref, q_s, k_s, v_s, do_s, qk_t, do_t, dq_t, delta_s, dk_s, dv_s
):
    rows = qk_ref.shape[0]
    tiles = rows // TILE
    per = TILE // block
    scale = HEAD ** (-0.5)

    def gather(i, carry):
        qk, v, do = [], [], []
        for b in range(per):
            src = source_ref[i * per + b]
            qk.append(qk_ref[pl.ds(pl.multiple_of(src * block, block), block), :].astype(F32))
            v.append(load_half(v_ref, src, block))
            do.append(load_half(do_ref, src, block))
        qk, v, do = jnp.concatenate(qk, axis=0), jnp.concatenate(v, axis=0), jnp.concatenate(do, axis=0)
        here = tile_at(i)
        q_s[here, :] = (qk[:, :HEAD] * scale).astype(BF16)
        k_s[here, :] = qk[:, HEAD:].astype(BF16)
        turned = qk.T
        qk_t[:HEAD, here] = (turned[:HEAD] * scale).astype(BF16)
        qk_t[HEAD:, here] = turned[HEAD:].astype(BF16)
        v_s[here, :] = v.astype(BF16)
        do_s[here, :] = do.astype(BF16)
        do_turned = do.T
        do_t[:, here] = do_turned.astype(BF16)
        dq_t[:, here] = jnp.zeros((HEAD, TILE), F32)
        delta_s[:, here] = jnp.sum(o_t[:, here] * do_turned, axis=0, keepdims=True)
        return carry

    lax.fori_loop(0, tiles, gather, 0)

    def backward(j, carry):
        keys = tile_at(j)

        def step(i, state):
            dk, dv = state
            here = tile_at(i)
            p = jnp.exp(masked_scores(k_s, qk_t, ends_ref, count, i, j) - lse_ref[:, here])
            dp = dot(v_s[keys, :], do_t[:, here])
            ds = (p * (dp - delta_s[:, here])).astype(BF16)
            dv = dv + dot(p.astype(BF16), do_s[here, :])
            dk = dk + dot(ds, q_s[here, :])
            dq_t[:, here] += dot(qk_t[HEAD:, keys], ds)
            return dk, dv

        high = (doc_end(j * TILE + TILE - 1, ends_ref, count) - 1) // TILE
        zero = jnp.zeros((TILE, HEAD), F32)
        dk, dv = lax.fori_loop(j, high + 1, step, (zero, zero))
        dk_s[keys, :] = dk
        dv_s[keys, :] = dv
        return carry

    lax.fori_loop(0, tiles, backward, 0)

    def scatter(i, carry):
        here = tile_at(i)
        dq = (dq_t[:, here] * scale).T
        dqk = jnp.concatenate([dq, dk_s[here, :]], axis=1).astype(BF16)
        for b in range(per):
            dst = pl.ds(pl.multiple_of(source_ref[i * per + b] * block, block), block)
            dqk_ref[dst, :] = dqk[b * block : (b + 1) * block, :]
        return carry

    lax.fori_loop(0, tiles, scatter, 0)

    def scatter_v(i, carry):
        both = [dv_s[pl.ds(pl.multiple_of(packed_ref[2 * i + b] * block, block), block), :] for b in range(2)]
        dv_ref[pl.ds(pl.multiple_of(i * block, block), block), :] = jnp.concatenate(both, axis=1).astype(BF16)
        return carry

    lax.fori_loop(0, rows // (2 * block), scatter_v, 0)


IN_VMEM = pl.BlockSpec(memory_space=pltpu.VMEM)
IN_SMEM = pl.BlockSpec(memory_space=pltpu.SMEM)


def attend_forward(source, packed, ends, qk, v, block):
    rows = qk.shape[0]
    turned = pltpu.VMEM((HEAD, rows), BF16)
    return pl.pallas_call(
        functools.partial(forward_kernel, block, ends.shape[0]),
        in_specs=[IN_SMEM] * 3 + [IN_VMEM] * 2,
        out_specs=[IN_VMEM] * 3,
        out_shape=[
            jax.ShapeDtypeStruct((rows // 2, 2 * HEAD), BF16),
            jax.ShapeDtypeStruct((HEAD, rows), F32),
            jax.ShapeDtypeStruct((1, rows), F32),
        ],
        scratch_shapes=[pltpu.VMEM((rows, HEAD), BF16), turned, turned, pltpu.VMEM((rows, HEAD), F32)],
        **params(rows * rows * HEAD * 40, 6 * rows * HEAD * 2, rows * rows),
    )(source, packed, ends, qk, v)


def attend_backward(source, packed, ends, qk, v, do, o_t, lse, block):
    rows = qk.shape[0]
    half = pltpu.VMEM((rows, HEAD), BF16)
    wide = pltpu.VMEM((rows, HEAD), F32)
    return pl.pallas_call(
        functools.partial(backward_kernel, block, ends.shape[0]),
        in_specs=[IN_SMEM] * 3 + [IN_VMEM] * 5,
        out_specs=[IN_VMEM] * 2,
        out_shape=[
            jax.ShapeDtypeStruct((rows, 2 * HEAD), BF16),
            jax.ShapeDtypeStruct((rows // 2, 2 * HEAD), BF16),
        ],
        scratch_shapes=[
            half,
            half,
            half,
            half,
            pltpu.VMEM((2 * HEAD, rows), BF16),
            pltpu.VMEM((HEAD, rows), BF16),
            pltpu.VMEM((HEAD, rows), F32),
            pltpu.VMEM((1, rows), F32),
            wide,
            wide,
        ],
        **params(rows * rows * HEAD * 40, 12 * rows * HEAD * 2, rows * rows),
    )(source, packed, ends, qk, v, do, o_t, lse)


def join_in(value, far):
    far = jnp.stack([value, far])
    near = xor_swap(far, "in", GROUP_IN, 1)
    return jnp.stack([far[0], near[0], far[1], near[1]])


def halves(parts):
    cut = parts.shape[-1] // 2
    return [parts[..., :cut], parts[..., cut:]]


def near_in(parts):
    return xor_swap(jnp.stack([parts[1], parts[3]]), "in", GROUP_IN, 1)


def far_in(parts, near):
    far = xor_swap((parts[2].astype(F32) + near[1].astype(F32)).astype(BF16), "in", GROUP_IN, 2)
    return parts[0].astype(F32) + near[0].astype(F32) + far.astype(F32)


def exchange_in(parts, t):
    here = [lax.dynamic_index_in_dim(parts, t ^ s, 0, keepdims=False) for s in range(GROUP_IN)]
    there = [here[0]] + [xor_swap(here[s], "in", GROUP_IN, s) for s in range(1, GROUP_IN)]
    stacked = jnp.stack(there)
    return jnp.stack([lax.dynamic_index_in_dim(stacked, t ^ u, 0, keepdims=False) for u in range(GROUP_IN)])


def exchange_out(parts, size):
    return jnp.stack([parts[0]] + [xor_swap(parts[s], "out", size, s) for s in range(1, size)])


def body(
    tokens,
    seq_lengths,
    dealing,
    ln1_gain,
    ln1_bias,
    ln2_gain,
    ln2_bias,
    w_qkv,
    b_qkv,
    w_out,
    w_in,
    b_in,
    w_fc2,
    b_out,
    cotangent,
):
    n_dp, n_out, n_in = lax.axis_size("dp"), lax.axis_size("out"), lax.axis_size("in")
    n_g = n_dp * n_out
    n_all = n_g * n_in
    rows_dev, width = tokens.shape
    ff = w_in.shape[1]
    ff_in = ff // n_in
    r_w = w_in.shape[0]
    r_ff = w_fc2.shape[0]
    block = LONGEST // (2 * n_out * n_in)
    slots_dev = rows_dev // block
    heads = width // HEAD
    h_in = heads // n_in
    cols = h_in * HEAD
    rows = rows_dev * n_in
    z, t = lax.axis_index("out"), lax.axis_index("in")
    z_arr = z[None].astype(jnp.int32)
    lengths, order = seq_lengths[0], dealing[0]
    ends = jnp.cumsum(lengths)

    slots = order.shape[0]
    ids = jnp.arange(slots, dtype=jnp.int32)
    slot_of = jnp.sum(jnp.where(order[None, :] == ids[:, None], ids[None, :], 0), axis=1)
    chunk = slot_of // slots_dev
    source = (((chunk % n_out) ^ z) * n_in + ((chunk // n_out) ^ t)) * slots_dev + slot_of % slots_dev
    source = source.astype(jnp.int32)
    lies = ids // slots_dev
    slot_here = (((lies % n_in) ^ t) * n_out + ((lies // n_in) ^ z)) * slots_dev + ids % slots_dev
    packed_of = jnp.sum(jnp.where(slot_here[:, None] == ids[None, :], order[None, :], 0), axis=1).astype(jnp.int32)

    part = jnp.arange(rows, dtype=jnp.int32)
    packed = packed_of[: rows // block].reshape(-1, 1) * block + jnp.arange(block, dtype=jnp.int32)[None, :]
    packed = packed.reshape(rows)
    starts = jnp.max(jnp.where(packed[:, None] >= ends[None, :], ends[None, :], 0), axis=1)
    position = (packed - starts).astype(F32)
    lane = jnp.arange(2 * HEAD, dtype=jnp.int32) % HEAD
    half = ROT // 2
    freq = 10000.0 ** (-2.0 * (lane % half).astype(F32) / ROT)
    phase = position[:, None] * freq[None, :]
    cos = jnp.where(lane < ROT, jnp.cos(phase), 1.0)
    sine = jnp.sin(phase)
    sin_l = jnp.where(lane < half, sine, 0.0)
    sin_r = jnp.where((lane >= half) & (lane < ROT), sine, 0.0)

    vectors = [ln1_gain, ln1_bias, ln2_gain, ln2_bias, b_qkv, b_out, b_in]
    sizes = [v.shape[0] for v in vectors]
    per_row = -(-len(vectors) // r_w)
    lanes = 128 // per_row
    qkv_cols = jnp.transpose(w_qkv.reshape(r_w, 3, n_in, cols), (2, 0, 1, 3)).reshape(n_in, r_w, 3 * cols)
    in_cols = jnp.transpose(w_in.reshape(r_w, n_dp, n_in, n_out, r_ff), (2, 0, 1, 3, 4)).reshape(n_in, r_w, ff_in)
    vec = jnp.stack([jnp.pad(v, (0, lanes - v.shape[0])) for v in vectors])
    vec = jnp.pad(vec, ((0, r_w * per_row - len(vectors)), (0, 0))).reshape(r_w, 128)
    vec = jnp.broadcast_to(vec[None], (n_in, r_w, 128))
    all_cols = jnp.concatenate([qkv_cols, vec, in_cols], axis=2)
    joined_cols = exchange_in(all_cols, t).reshape(n_in * r_w, -1)
    home = []
    for b in range(n_all):
        t_to, g_to = b // n_g, b % n_g
        home.append((b, ((g_to // n_out) * n_in + t_to) * n_out + g_to % n_out))
    out_rows = lax.ppermute(w_out, ALL_AXES, home).reshape(n_in * r_w, cols)
    first = jnp.concatenate([joined_cols[:, : 3 * cols + 128], out_rows], axis=1)
    first, to_send = lax.optimization_barrier((first, tokens))
    x_far = xor_swap(to_send, "in", n_in, 2)
    first = lax.all_gather(first, G_AXES, axis=0, tiled=False)
    second = jnp.concatenate([joined_cols[:, 3 * cols + 128 :], w_fc2], axis=1)
    second = lax.all_gather(second, G_AXES, axis=0, tiled=False)

    def natural(value):
        value = value.reshape(n_dp, n_out, n_in, r_w, -1)
        return jnp.transpose(value, (0, 2, 1, 3, 4)).reshape(n_all * r_w, -1)

    def by_owner(value):
        value = value.reshape(n_dp, n_in, n_out, r_w, -1)
        return jnp.transpose(value, (0, 2, 1, 3, 4)).reshape(n_g, n_in * r_w, -1)

    weight_qkv = natural(first[:, :, : 3 * cols])
    weight_out = first[:, :, 3 * cols + 128 :].reshape(cols, width)
    weight_in = natural(second[:, :, :ff_in])
    weight_fc2 = second[:, :, ff_in:].reshape(ff_in, width)
    vec_all = first[:, :, 3 * cols : 3 * cols + 128].reshape(n_dp, n_out, n_in, r_w * per_row, lanes)
    vec_all = jnp.transpose(vec_all[:, :, :, : len(vectors)], (3, 0, 2, 1, 4)).astype(F32)
    spans = [vec_all[i, ..., :size] for i, size in enumerate(sizes)]
    gain_one, shift_one, gain_two, shift_two = [s.reshape(width) for s in spans[:4]]
    bias_out = spans[5].reshape(width)
    bias_in = lax.dynamic_index_in_dim(spans[6], t, 1, keepdims=False).reshape(ff_in)
    bias_qkv = lax.dynamic_index_in_dim(spans[4].reshape(3, n_in, cols), t, 1, keepdims=False).reshape(-1)
    norms = jnp.concatenate([jnp.stack([gain_one, shift_one, gain_two, shift_two]), jnp.zeros((4, width), F32)])

    x_all = join_in(tokens, x_far).reshape(rows, width)
    x_all, to_send = lax.optimization_barrier((x_all, cotangent))
    dy_far = xor_swap(to_send, "in", n_in, 2)

    qk, v, n1, n2 = prep(z_arr, x_all, norms, weight_qkv, bias_qkv[None], cos, sin_l, sin_r, block)
    qk = exchange_out(qk, n_out).reshape(n_out * rows, 2 * HEAD)
    v = exchange_out(v, n_out).reshape(n_out * rows // 2, 2 * HEAD)
    qk, v, dy_far = lax.optimization_barrier((qk, v, dy_far))
    dy_all = join_in(cotangent, dy_far).reshape(rows, width)
    o, o_t, lse = attend_forward(source, packed_of, ends, qk, v, block)
    o, dy_all = lax.optimization_barrier((o, dy_all))
    o = exchange_out(o.reshape(n_out, rows // 2, 2 * HEAD), n_out)
    do = grad_att(z_arr, dy_all, weight_out, block)
    do = exchange_out(do, n_out).reshape(n_out * rows // 2, 2 * HEAD)

    hidden, grad_up, y_ff, dx_ff, sums_two, grad_b_in = feed(x_all, n2, dy_all, norms, weight_in, weight_fc2, bias_in[None])
    o, y_ff = lax.optimization_barrier((o, y_ff))
    o = merge_heads(z_arr, o, block)
    y_part = (y_ff + dot(o, weight_out)).astype(BF16).reshape(n_in, rows_dev, width)
    grad_fc2 = dot_tn(hidden, dy_all)
    grad_in = dot_tn(n2, grad_up)
    grad_out = dot_tn(o, dy_all)
    second_grads = jnp.concatenate(
        [
            by_owner(grad_in.astype(BF16)),
            grad_fc2.astype(BF16).reshape(n_g, r_ff, width),
            grad_out.astype(BF16).reshape(n_g, n_in * r_w, cols),
        ],
        axis=2,
    )

    do, second_grads, y_part = lax.optimization_barrier((do, second_grads, y_part))
    second_grads = lax.psum_scatter(second_grads, G_AXES, scatter_dimension=0, tiled=False)
    y_near = near_in(y_part)
    own = tokens.astype(F32)
    dqk, dv = attend_backward(source, packed_of, ends, qk, v, do, o_t, lse, block)
    dqk, dv, y_near = lax.optimization_barrier((dqk, dv, y_near))
    dqk = exchange_out(dqk.reshape(n_out, rows, 2 * HEAD), n_out)
    dv = exchange_out(dv.reshape(n_out, rows // 2, 2 * HEAD), n_out)
    mixed = (own + far_in(y_part, y_near) + bias_out).astype(BF16)
    da, w_parts, sums_one, grad_b_qkv = post(
        z_arr, dqk, dv, x_all, dx_ff, norms, weight_qkv, cos, sin_l, sin_r, block
    )
    in_part = exchange_in(second_grads[:, :ff_in].reshape(n_in, r_w, ff_in), t)
    w_parts, da, mixed, in_part = lax.optimization_barrier((w_parts, da, mixed, in_part))
    w_parts = halves(w_parts.reshape(n_in, rows_dev, width))
    near = near_in(w_parts[0])
    near, w_next = lax.optimization_barrier((near, w_parts[1]))
    w_sum = jnp.concatenate([far_in(w_parts[0], near), far_in(w_next, near_in(w_next))], axis=1)

    grad_qkv = dot_tn(n1, da)

    def placed(vector, axis):
        spread = jnp.expand_dims(vector, axis)
        mask = (jnp.arange(n_in) == t).reshape([-1 if a == axis else 1 for a in range(spread.ndim)])
        return jnp.where(mask, spread, 0.0).reshape(-1)

    grad_own = cotangent.astype(F32)
    vec_grads = [
        sums_one[0],
        sums_one[1],
        sums_two[0],
        sums_two[1],
        placed(grad_b_qkv[0].reshape(3, cols), 1),
        jnp.sum(grad_own, axis=0),
        placed(grad_b_in[0].reshape(n_dp, n_out, r_ff), 1),
    ]
    vec_grads = [v.astype(BF16).reshape(n_dp, n_in, n_out, -1) for v in vec_grads]
    vec_grads = jnp.stack([jnp.pad(v, ((0, 0), (0, 0), (0, 0), (0, lanes - v.shape[-1]))) for v in vec_grads], axis=3)
    spare = r_w * per_row - len(vectors)
    vec_grads = jnp.pad(vec_grads, ((0, 0), (0, 0), (0, 0), (0, spare), (0, 0)))
    vec_grads = jnp.transpose(vec_grads, (0, 2, 1, 3, 4)).reshape(n_g, n_in * r_w, 128)
    first_grads = jnp.concatenate(
        [
            by_owner(grad_qkv.astype(BF16)),
            vec_grads,
        ],
        axis=2,
    )
    first_grads = lax.psum_scatter(first_grads, G_AXES, scatter_dimension=0, tiled=False)

    in_part = in_part.reshape(n_in, r_w, n_dp, n_out, r_ff)
    grad_w_in = jnp.transpose(in_part, (1, 2, 0, 3, 4)).reshape(r_w, ff).astype(F32)
    grad_w_fc2 = second_grads[:, ff_in : ff_in + width].astype(F32)
    back_home = [(b, a) for a, b in home]
    out_part = second_grads[:, ff_in + width :].reshape(r_w, width)
    grad_w_out = lax.ppermute(out_part, ALL_AXES, back_home).astype(F32)
    qkv_part = exchange_in(first_grads.reshape(n_in, r_w, 3 * cols + 128), t)
    qkv_grad = jnp.transpose(qkv_part[:, :, : 3 * cols].reshape(n_in, r_w, 3, cols), (1, 2, 0, 3))
    grad_w_qkv = qkv_grad.reshape(r_w, 3 * width).astype(F32)
    vec_part = jnp.sum(qkv_part[:, :, 3 * cols :].astype(F32), axis=0).reshape(r_w * per_row, lanes)
    vec_out = [vec_part[i, :size] for i, size in enumerate(sizes)]

    centred = own - jnp.mean(own, axis=-1, keepdims=True)
    own_rstd = lax.rsqrt(jnp.mean(centred * centred, axis=-1, keepdims=True) + EPS)
    own_hat = centred * own_rstd
    mean_w = jnp.mean(w_sum, axis=-1, keepdims=True)
    mean_wx = jnp.mean(w_sum * own_hat, axis=-1, keepdims=True)
    grad_tokens = grad_own + own_rstd * (w_sum - mean_w - own_hat * mean_wx)
    return (
        mixed,
        grad_tokens,
        vec_out[0],
        vec_out[1],
        vec_out[2],
        vec_out[3],
        grad_w_qkv,
        vec_out[4],
        grad_w_out,
        grad_w_in,
        vec_out[6],
        grad_w_fc2,
        vec_out[5],
    )


def solution(mesh):
    n_dp, n_ctx = mesh.shape["dp"], mesh.shape["ctx"]
    split = Mesh(mesh.devices.reshape(n_dp, GROUP_IN, n_ctx // GROUP_IN), ALL_AXES)
    mat, vec, group = P(ALL_AXES, None), P(ALL_AXES), P("dp", None)
    return jax.shard_map(
        body,
        mesh=split,
        in_specs=(mat, group, group, vec, vec, vec, vec, mat, vec, mat, mat, vec, mat, vec, mat),
        out_specs=(mat, mat, vec, vec, vec, vec, mat, vec, mat, mat, vec, mat, vec),
        check_vma=False,
    )
```

```python
import functools

import jax
import jax.numpy as jnp
from jax import lax
from jax.experimental import pallas as pl
from jax.experimental.pallas import tpu as pltpu
from jax.sharding import Mesh
from jax.sharding import PartitionSpec as P

HEAD = 64
ROT = 16
LONGEST = 2048
GROUP_IN = 4
TILE = 256
FQ, FK = 512, 512
BQ, BK = 512, 256
EPS = 1e-05
NEG = -1e30
F32 = jnp.float32
BF16 = jnp.bfloat16
G_AXES = ("dp", "out")
ALL_AXES = ("dp", "in", "out")


def dot(a, b):
    return jnp.dot(a, b, preferred_element_type=F32)


def dot_nt(a, b):
    return lax.dot_general(a, b, (((1,), (1,)), ((), ())), preferred_element_type=F32)


def dot_tn(a, b):
    return lax.dot_general(a, b, (((0,), (0,)), ((), ())), preferred_element_type=F32)


def xor_swap(value, axis, size, step):
    return lax.ppermute(value, axis, [(i, i ^ step) for i in range(size)])


def rotary(x, cos, sin_l, sin_r, sign):
    left = pltpu.roll(x, 128 - ROT // 2, 1)
    right = pltpu.roll(x, ROT // 2, 1)
    return x * cos - sign * (left * sin_l) + sign * (right * sin_r)


def pair_up(x, block):
    blocks = [x[i : i + block] for i in range(0, x.shape[0], block)]
    return jnp.concatenate([jnp.concatenate(blocks[i : i + 2], axis=1) for i in range(0, len(blocks), 2)], axis=0)


def unpair(x, block):
    parts = []
    for i in range(0, x.shape[0], block):
        parts += [x[i : i + block, :HEAD], x[i : i + block, HEAD:]]
    return jnp.concatenate(parts, axis=0)


def params(flops, size, exps=0):
    return dict(
        compiler_params=pltpu.CompilerParams(vmem_limit_bytes=60 * 2**20),
        cost_estimate=pl.CostEstimate(flops=flops, bytes_accessed=size, transcendentals=exps),
    )


def row_at(i, z):
    return (i, 0)


def whole_at(i, z):
    return (0, 0)


def piece(size):
    return pl.BlockSpec((size, 2 * HEAD), row_at)


def bf16_rows(rows):
    return jax.ShapeDtypeStruct((rows, 2 * HEAD), BF16)


def normalized(x_ref):
    x = x_ref[...].astype(F32)
    centred = x - jnp.mean(x, axis=-1, keepdims=True)
    return centred * lax.rsqrt(jnp.mean(centred * centred, axis=-1, keepdims=True) + EPS)


def turn(z, parts):
    out = []
    for step in range(len(parts)):
        pick = parts[step]
        for at in range(1, len(parts)):
            pick = jnp.where(z == at, parts[at ^ step], pick)
        out.append(pick)
    return out


def prep_kernel(heads, block, z_ref, x_ref, norm_ref, w_ref, b_ref, cos_ref, sl_ref, sr_ref, n1_ref, n2_ref, *out_refs):
    z = z_ref[0]
    xhat = normalized(x_ref)
    n1 = (xhat * norm_ref[0:1] + norm_ref[1:2]).astype(BF16)
    n1_ref[...] = n1
    n2_ref[...] = (xhat * norm_ref[2:3] + norm_ref[3:4]).astype(BF16)
    joined = dot(n1, w_ref[...]) + b_ref[...]
    cos, sl, sr = cos_ref[...], sl_ref[...], sr_ref[...]
    cols = heads * HEAD
    qk, v = [], []
    for h in range(heads):
        at = h * HEAD
        part = jnp.concatenate([joined[:, at : at + HEAD], joined[:, cols + at : cols + at + HEAD]], axis=1)
        qk.append(rotary(part, cos, sl, sr, 1.0))
        v.append(pair_up(joined[:, 2 * cols + at : 2 * cols + at + HEAD], block))
    for ref, part in zip(out_refs, turn(z, qk) + turn(z, v)):
        ref[...] = part.astype(BF16)


def prep(z, x, norms, w, bias, cos, sl, sr, block):
    rows, width = x.shape
    heads = w.shape[1] // (3 * HEAD)
    table = pl.BlockSpec((TILE, 2 * HEAD), row_at)
    tile = pl.BlockSpec((TILE, width), row_at)
    norm = jax.ShapeDtypeStruct((rows, width), BF16)
    return pl.pallas_call(
        functools.partial(prep_kernel, heads, block),
        grid_spec=pltpu.PrefetchScalarGridSpec(
            num_scalar_prefetch=1,
            grid=(rows // TILE,),
            in_specs=[
                tile,
                pl.BlockSpec(norms.shape, whole_at),
                pl.BlockSpec(w.shape, whole_at),
                pl.BlockSpec(bias.shape, whole_at),
                table,
                table,
                table,
            ],
            out_specs=[tile, tile] + [piece(TILE)] * heads + [piece(TILE // 2)] * heads,
        ),
        out_shape=[norm, norm] + [bf16_rows(rows)] * heads + [bf16_rows(rows // 2)] * heads,
        **params(2 * rows * width * w.shape[1], 12 * 2**20),
    )(z, x, norms, w, bias, cos, sl, sr)


def feed_kernel(x_ref, n2_ref, dy_ref, norm_ref, w_in_ref, w_fc2_ref, b_ref, h_ref, du_ref, y_ref, dx_ref, sums_ref, db_ref):
    up = dot(n2_ref[...], w_in_ref[...]) + b_ref[...]
    cdf = 0.5 + 0.5 * lax.erf(up * (0.5**0.5))
    hidden = (up * cdf).astype(BF16)
    slope = cdf + up * (jnp.exp(-0.5 * up * up) * 0.3989422804014327)
    grad_up = (dot_nt(dy_ref[...], w_fc2_ref[...]) * slope).astype(BF16)
    h_ref[...] = hidden
    du_ref[...] = grad_up
    y_ref[...] = dot(hidden, w_fc2_ref[...])
    grad_norm = dot_nt(grad_up, w_in_ref[...])
    dx_ref[...] = grad_norm * norm_ref[2:3]
    gain = jnp.sum(grad_norm * normalized(x_ref), axis=0, keepdims=True)
    shift = jnp.sum(grad_norm, axis=0, keepdims=True)
    bias = jnp.sum(grad_up.astype(F32), axis=0, keepdims=True)

    @pl.when(pl.program_id(0) == 0)
    def _():
        sums_ref[...] = jnp.zeros_like(sums_ref)
        db_ref[...] = jnp.zeros_like(db_ref)

    sums_ref[0:1] += gain
    sums_ref[1:2] += shift
    db_ref[0:1] += bias


def feed(x, n2, dy, norms, w_in, w_fc2, bias):
    rows, width = x.shape
    units = w_in.shape[1]
    row, whole = lambda i: (i, 0), lambda i: (0, 0)
    tile, tile_ff = pl.BlockSpec((TILE, width), row), pl.BlockSpec((TILE, units), row)
    return pl.pallas_call(
        feed_kernel,
        grid=(rows // TILE,),
        in_specs=[
            tile,
            tile,
            tile,
            pl.BlockSpec(norms.shape, whole),
            pl.BlockSpec(w_in.shape, whole),
            pl.BlockSpec(w_fc2.shape, whole),
            pl.BlockSpec(bias.shape, whole),
        ],
        out_specs=[
            tile_ff,
            tile_ff,
            tile,
            tile,
            pl.BlockSpec((8, width), whole),
            pl.BlockSpec((8, units), whole),
        ],
        out_shape=[
            jax.ShapeDtypeStruct((rows, units), BF16),
            jax.ShapeDtypeStruct((rows, units), BF16),
            jax.ShapeDtypeStruct((rows, width), F32),
            jax.ShapeDtypeStruct((rows, width), F32),
            jax.ShapeDtypeStruct((8, width), F32),
            jax.ShapeDtypeStruct((8, units), F32),
        ],
        **params(8 * rows * width * units, 24 * 2**20, 2 * rows * units),
    )(x, n2, dy, norms, w_in, w_fc2, bias)


def grad_att_kernel(heads, block, z_ref, dy_ref, wo_ref, *out_refs):
    grad = dot_nt(dy_ref[...], wo_ref[...])
    parts = [pair_up(grad[:, h * HEAD : (h + 1) * HEAD], block) for h in range(heads)]
    for ref, part in zip(out_refs, turn(z_ref[0], parts)):
        ref[...] = part.astype(BF16)


def grad_att(z, dy, wo, block):
    rows, width = dy.shape
    heads = wo.shape[0] // HEAD
    return pl.pallas_call(
        functools.partial(grad_att_kernel, heads, block),
        grid_spec=pltpu.PrefetchScalarGridSpec(
            num_scalar_prefetch=1,
            grid=(rows // TILE,),
            in_specs=[pl.BlockSpec((TILE, width), row_at), pl.BlockSpec(wo.shape, whole_at)],
            out_specs=[piece(TILE // 2)] * heads,
        ),
        out_shape=[bf16_rows(rows // 2)] * heads,
        **params(2 * rows * width * wo.shape[0], 4 * 2**20),
    )(z, dy, wo)


def project_kernel(heads, block, z_ref, y_ref, wo_ref, *refs):
    parts = turn(z_ref[0], [unpair(ref[...].astype(F32), block) for ref in refs[:heads]])
    o_ref, out_ref = refs[heads:]
    for h in range(0, heads, 2):
        o_ref[:, h * HEAD : (h + 2) * HEAD] = jnp.concatenate(parts[h : h + 2], axis=1).astype(BF16)
    out_ref[...] = (y_ref[...] + dot(o_ref[...], wo_ref[...])).astype(BF16)


def project(z, parts, y, wo, block):
    heads = len(parts)
    rows, width = y.shape
    tile = pl.BlockSpec((TILE, width), row_at)
    return pl.pallas_call(
        functools.partial(project_kernel, heads, block),
        grid_spec=pltpu.PrefetchScalarGridSpec(
            num_scalar_prefetch=1,
            grid=(rows // TILE,),
            in_specs=[tile, pl.BlockSpec(wo.shape, whole_at)] + [piece(TILE // 2)] * heads,
            out_specs=[pl.BlockSpec((TILE, heads * HEAD), row_at), tile],
        ),
        out_shape=[
            jax.ShapeDtypeStruct((rows, heads * HEAD), BF16),
            jax.ShapeDtypeStruct((rows, width), BF16),
        ],
        **params(2 * rows * width * wo.shape[0], 8 * 2**20),
    )(z, y, wo, *parts)


def post_kernel(
    heads, block, z_ref, x_ref, dx_ref, norm_ref, w_ref, cos_ref, sl_ref, sr_ref, *refs
):
    z = z_ref[0]
    dqk = turn(z, [ref[...].astype(F32) for ref in refs[:heads]])
    dv = turn(z, [unpair(ref[...].astype(F32), block) for ref in refs[heads : 2 * heads]])
    da_ref, sum_ref, sums_ref, db_ref = refs[2 * heads :]
    cos, sl, sr = cos_ref[...], sl_ref[...], sr_ref[...]
    cols = heads * HEAD
    for h in range(0, heads, 2):
        at = h * HEAD
        one = rotary(dqk[h], cos, sl, sr, -1.0)
        two = rotary(dqk[h + 1], cos, sl, sr, -1.0)
        da_ref[:, at : at + 2 * HEAD] = jnp.concatenate([one[:, :HEAD], two[:, :HEAD]], axis=1).astype(BF16)
        da_ref[:, cols + at : cols + at + 2 * HEAD] = jnp.concatenate([one[:, HEAD:], two[:, HEAD:]], axis=1).astype(BF16)
        da_ref[:, 2 * cols + at : 2 * cols + at + 2 * HEAD] = jnp.concatenate(dv[h : h + 2], axis=1).astype(BF16)
    grad = da_ref[...]
    grad_norm = dot_nt(grad, w_ref[...])
    sum_ref[...] = (dx_ref[...] + grad_norm * norm_ref[0:1]).astype(BF16)
    gain = jnp.sum(grad_norm * normalized(x_ref), axis=0, keepdims=True)
    shift = jnp.sum(grad_norm, axis=0, keepdims=True)
    bias = jnp.sum(grad.astype(F32), axis=0, keepdims=True)

    @pl.when(pl.program_id(0) == 0)
    def _():
        sums_ref[...] = jnp.zeros_like(sums_ref)
        db_ref[...] = jnp.zeros_like(db_ref)

    sums_ref[0:1] += gain
    sums_ref[1:2] += shift
    db_ref[0:1] += bias


def post(z, dqk, dv, x, dx, norms, w, cos, sl, sr, block):
    heads = len(dqk)
    rows, width = x.shape
    three = heads * 3 * HEAD
    table = pl.BlockSpec((TILE, 2 * HEAD), row_at)
    tile = pl.BlockSpec((TILE, width), row_at)
    return pl.pallas_call(
        functools.partial(post_kernel, heads, block),
        grid_spec=pltpu.PrefetchScalarGridSpec(
            num_scalar_prefetch=1,
            grid=(rows // TILE,),
            in_specs=[
                tile,
                tile,
                pl.BlockSpec(norms.shape, whole_at),
                pl.BlockSpec(w.shape, whole_at),
                table,
                table,
                table,
            ]
            + [piece(TILE)] * heads
            + [piece(TILE // 2)] * heads,
            out_specs=[
                pl.BlockSpec((TILE, three), row_at),
                tile,
                pl.BlockSpec((8, width), whole_at),
                pl.BlockSpec((8, three), whole_at),
            ],
        ),
        out_shape=[
            jax.ShapeDtypeStruct((rows, three), BF16),
            jax.ShapeDtypeStruct((rows, width), BF16),
            jax.ShapeDtypeStruct((8, width), F32),
            jax.ShapeDtypeStruct((8, three), F32),
        ],
        **params(2 * rows * width * three, 14 * 2**20),
    )(z, x, dx, norms, w, cos, sl, sr, *dqk, *dv)


def doc_start(packed, ends_ref, count):
    start = packed * 0
    for d in range(count):
        start = jnp.where(packed >= ends_ref[d], ends_ref[d], start)
    return start


def doc_end(packed, ends_ref, count):
    end = ends_ref[count - 1]
    for d in range(count - 2, -1, -1):
        end = jnp.where(packed < ends_ref[d], ends_ref[d], end)
    return end


def tile_at(i, size=TILE):
    return pl.ds(pl.multiple_of(i * size, size), size)


def load_half(ref, source, block):
    both = ref[pl.ds(pl.multiple_of((source // 2) * block, block), block), :].astype(F32)
    return jnp.where(source % 2 == 0, both[:, :HEAD], both[:, HEAD:])


def masked_scores(k_s, q_t, ends_ref, count, i, j, q_size, k_size):
    s = dot(k_s[tile_at(j, k_size), :], q_t[:HEAD, tile_at(i, q_size)])
    key_at = lax.broadcasted_iota(jnp.int32, (k_size, q_size), 0)
    query_at = lax.broadcasted_iota(jnp.int32, (k_size, q_size), 1)
    query_row = i * q_size + lax.broadcasted_iota(jnp.int32, (1, q_size), 1)
    first = doc_start(query_row, ends_ref, count) - j * k_size
    last = i * q_size - j * k_size + query_at
    return jnp.where((key_at >= first) & (key_at <= last), s, NEG)


def lay_out(pieces, whole):
    size = pieces[0].shape[0]
    for i, ref in enumerate(pieces):
        whole[i * size : (i + 1) * size, :] = ref[...]


def forward_kernel(block, count, source_ref, packed_ref, ends_ref, *refs):
    pieces = (len(refs) - 8) // 3
    qk_in, v_in, o_out = refs[:pieces], refs[pieces : 2 * pieces], refs[2 * pieces : 3 * pieces]
    o_t, lse_ref, k_s, q_t, v_t, o_s, qk_ref, v_ref = refs[3 * pieces :]
    rows = qk_ref.shape[0]
    lay_out(qk_in, qk_ref)
    lay_out(v_in, v_ref)
    tiles = rows // TILE
    per = TILE // block
    scale = HEAD ** (-0.5)

    def gather(i, carry):
        qk, v = [], []
        for b in range(per):
            src = source_ref[i * per + b]
            qk.append(qk_ref[pl.ds(pl.multiple_of(src * block, block), block), :].astype(F32))
            v.append(load_half(v_ref, src, block))
        qk, v = jnp.concatenate(qk, axis=0), jnp.concatenate(v, axis=0)
        k_s[tile_at(i), :] = qk[:, HEAD:].astype(BF16)
        q_t[:, tile_at(i)] = (qk.T[:HEAD] * scale).astype(BF16)
        v_t[:, tile_at(i)] = v.T.astype(BF16)
        return carry

    lax.fori_loop(0, tiles, gather, 0)

    def forward(i, carry):
        here = tile_at(i, FQ)

        def step(j, state):
            top, total, acc = state
            s = masked_scores(k_s, q_t, ends_ref, count, i, j, FQ, FK)
            new_top = jnp.maximum(top, jnp.max(s, axis=0, keepdims=True))
            p = jnp.exp(s - new_top)
            fade = jnp.exp(top - new_top)
            total = total * fade + jnp.sum(p, axis=0, keepdims=True)
            acc = acc * fade + dot(v_t[:, tile_at(j, FK)], p.astype(BF16))
            return new_top, total, acc

        low = doc_start(i * FQ, ends_ref, count) // FK
        high = (i * FQ + FQ - 1) // FK
        top, total, acc = lax.fori_loop(
            low, high + 1, step, (jnp.full((1, FQ), NEG, F32), jnp.zeros((1, FQ), F32), jnp.zeros((HEAD, FQ), F32))
        )
        out = acc / total
        lse_ref[:, here] = top + jnp.log(total)
        o_t[:, here] = out
        o_s[here, :] = out.T
        return carry

    lax.fori_loop(0, rows // FQ, forward, 0)

    send_pairs(o_s, o_out, packed_ref, block)


def send_pairs(whole, out_refs, packed_ref, block):
    per = out_refs[0].shape[0] // block
    for at, ref in enumerate(out_refs):

        def one(i, carry):
            row = 2 * (at * per + i)
            both = [whole[pl.ds(pl.multiple_of(packed_ref[row + b] * block, block), block), :] for b in range(2)]
            ref[pl.ds(pl.multiple_of(i * block, block), block), :] = jnp.concatenate(both, axis=1).astype(BF16)
            return carry

        lax.fori_loop(0, per, one, 0)


def backward_kernel(block, count, source_ref, packed_ref, ends_ref, *refs):
    pieces = (len(refs) - 16) // 5
    qk_in, v_in, do_in = [refs[i * pieces : (i + 1) * pieces] for i in range(3)]
    o_t, lse_ref = refs[3 * pieces : 3 * pieces + 2]
    dqk_out, dv_out = [refs[i * pieces + 2 : (i + 1) * pieces + 2] for i in (3, 4)]
    q_s, k_s, v_s, do_s, qk_t, do_t, dq_t, delta_s, dk_s, dv_s, qk_ref, v_ref, do_ref, dqk_ref = refs[5 * pieces + 2 :]
    rows = qk_ref.shape[0]
    lay_out(qk_in, qk_ref)
    lay_out(v_in, v_ref)
    lay_out(do_in, do_ref)
    tiles = rows // TILE
    per = TILE // block
    scale = HEAD ** (-0.5)

    def gather(i, carry):
        qk, v, do = [], [], []
        for b in range(per):
            src = source_ref[i * per + b]
            qk.append(qk_ref[pl.ds(pl.multiple_of(src * block, block), block), :].astype(F32))
            v.append(load_half(v_ref, src, block))
            do.append(load_half(do_ref, src, block))
        qk, v, do = jnp.concatenate(qk, axis=0), jnp.concatenate(v, axis=0), jnp.concatenate(do, axis=0)
        here = tile_at(i)
        q_s[here, :] = (qk[:, :HEAD] * scale).astype(BF16)
        k_s[here, :] = qk[:, HEAD:].astype(BF16)
        turned = qk.T
        qk_t[:HEAD, here] = (turned[:HEAD] * scale).astype(BF16)
        qk_t[HEAD:, here] = turned[HEAD:].astype(BF16)
        v_s[here, :] = v.astype(BF16)
        do_s[here, :] = do.astype(BF16)
        do_turned = do.T
        do_t[:, here] = do_turned.astype(BF16)
        dq_t[:, here] = jnp.zeros((HEAD, TILE), F32)
        delta_s[:, here] = jnp.sum(o_t[:, here] * do_turned, axis=0, keepdims=True)
        return carry

    lax.fori_loop(0, tiles, gather, 0)

    def backward(j, carry):
        keys = tile_at(j, BK)

        def step(i, state):
            dk, dv = state
            here = tile_at(i, BQ)
            p = jnp.exp(masked_scores(k_s, qk_t, ends_ref, count, i, j, BQ, BK) - lse_ref[:, here])
            dp = dot(v_s[keys, :], do_t[:, here])
            ds = (p * (dp - delta_s[:, here])).astype(BF16)
            dv = dv + dot(p.astype(BF16), do_s[here, :])
            dk = dk + dot(ds, q_s[here, :])
            dq_t[:, here] += dot(qk_t[HEAD:, keys], ds)
            return dk, dv

        high = (doc_end(j * BK + BK - 1, ends_ref, count) - 1) // BQ
        zero = jnp.zeros((BK, HEAD), F32)
        dk, dv = lax.fori_loop(j * BK // BQ, high + 1, step, (zero, zero))
        dk_s[keys, :] = dk
        dv_s[keys, :] = dv
        return carry

    lax.fori_loop(0, rows // BK, backward, 0)

    def scatter(i, carry):
        here = tile_at(i)
        dq = (dq_t[:, here] * scale).T
        dqk = jnp.concatenate([dq, dk_s[here, :]], axis=1).astype(BF16)
        for b in range(per):
            dst = pl.ds(pl.multiple_of(source_ref[i * per + b] * block, block), block)
            dqk_ref[dst, :] = dqk[b * block : (b + 1) * block, :]
        return carry

    lax.fori_loop(0, tiles, scatter, 0)

    size = rows // pieces
    for i, ref in enumerate(dqk_out):
        ref[...] = dqk_ref[i * size : (i + 1) * size, :]
    send_pairs(dv_s, dv_out, packed_ref, block)


IN_VMEM = pl.BlockSpec(memory_space=pltpu.VMEM)
IN_SMEM = pl.BlockSpec(memory_space=pltpu.SMEM)


def attend_forward(source, packed, ends, qk, v, block):
    pieces = len(qk)
    rows = pieces * qk[0].shape[0]
    turned = pltpu.VMEM((HEAD, rows), BF16)
    return pl.pallas_call(
        functools.partial(forward_kernel, block, ends.shape[0]),
        in_specs=[IN_SMEM] * 3 + [IN_VMEM] * (2 * pieces),
        out_specs=[IN_VMEM] * (pieces + 2),
        out_shape=[bf16_rows(rows // (2 * pieces))] * pieces
        + [
            jax.ShapeDtypeStruct((HEAD, rows), F32),
            jax.ShapeDtypeStruct((1, rows), F32),
        ],
        scratch_shapes=[
            pltpu.VMEM((rows, HEAD), BF16),
            turned,
            turned,
            pltpu.VMEM((rows, HEAD), F32),
            pltpu.VMEM((rows, 2 * HEAD), BF16),
            pltpu.VMEM((rows // 2, 2 * HEAD), BF16),
        ],
        **params(rows * rows * HEAD * 40, 6 * rows * HEAD * 2, rows * rows),
    )(source, packed, ends, *qk, *v)


def attend_backward(source, packed, ends, qk, v, do, o_t, lse, block):
    pieces = len(qk)
    rows = pieces * qk[0].shape[0]
    half = pltpu.VMEM((rows, HEAD), BF16)
    wide = pltpu.VMEM((rows, HEAD), F32)
    pairs = pltpu.VMEM((rows // 2, 2 * HEAD), BF16)
    whole = pltpu.VMEM((rows, 2 * HEAD), BF16)
    return pl.pallas_call(
        functools.partial(backward_kernel, block, ends.shape[0]),
        in_specs=[IN_SMEM] * 3 + [IN_VMEM] * (3 * pieces + 2),
        out_specs=[IN_VMEM] * (2 * pieces),
        out_shape=[bf16_rows(rows // pieces)] * pieces + [bf16_rows(rows // (2 * pieces))] * pieces,
        scratch_shapes=[
            half,
            half,
            half,
            half,
            pltpu.VMEM((2 * HEAD, rows), BF16),
            pltpu.VMEM((HEAD, rows), BF16),
            pltpu.VMEM((HEAD, rows), F32),
            pltpu.VMEM((1, rows), F32),
            wide,
            wide,
            whole,
            pairs,
            pairs,
            whole,
        ],
        **params(rows * rows * HEAD * 40, 12 * rows * HEAD * 2, rows * rows),
    )(source, packed, ends, *qk, *v, *do, o_t, lse)


def join_in(value, far, near):
    return jnp.concatenate([value, near[0], far, near[1]])


def halves(parts):
    cut = parts.shape[-1] // 2
    return [parts[..., :cut], parts[..., cut:]]


def near_in(parts):
    return xor_swap(jnp.stack([parts[1], parts[3]]), "in", GROUP_IN, 1)


def far_in(parts, near):
    far = xor_swap((parts[2].astype(F32) + near[1].astype(F32)).astype(BF16), "in", GROUP_IN, 2)
    return parts[0].astype(F32) + near[0].astype(F32) + far.astype(F32)


def exchange_in(parts, t):
    here = [lax.dynamic_index_in_dim(parts, t ^ s, 0, keepdims=False) for s in range(GROUP_IN)]
    there = [here[0]] + [xor_swap(here[s], "in", GROUP_IN, s) for s in range(1, GROUP_IN)]
    stacked = jnp.stack(there)
    return jnp.stack([lax.dynamic_index_in_dim(stacked, t ^ u, 0, keepdims=False) for u in range(GROUP_IN)])


def exchange_out(parts):
    size = len(parts)
    return [parts[0]] + [xor_swap(parts[s], "out", size, s) for s in range(1, size)]


def body(
    tokens,
    seq_lengths,
    dealing,
    ln1_gain,
    ln1_bias,
    ln2_gain,
    ln2_bias,
    w_qkv,
    b_qkv,
    w_out,
    w_in,
    b_in,
    w_fc2,
    b_out,
    cotangent,
):
    n_dp, n_out, n_in = lax.axis_size("dp"), lax.axis_size("out"), lax.axis_size("in")
    n_g = n_dp * n_out
    n_all = n_g * n_in
    rows_dev, width = tokens.shape
    ff = w_in.shape[1]
    ff_in = ff // n_in
    r_w = w_in.shape[0]
    r_ff = w_fc2.shape[0]
    block = LONGEST // (2 * n_out * n_in)
    slots_dev = rows_dev // block
    heads = width // HEAD
    h_in = heads // n_in
    cols = h_in * HEAD
    rows = rows_dev * n_in
    z, t = lax.axis_index("out"), lax.axis_index("in")
    z_arr = z[None].astype(jnp.int32)
    lengths, order = seq_lengths[0], dealing[0]
    ends = jnp.cumsum(lengths)

    slots = order.shape[0]
    ids = jnp.arange(slots, dtype=jnp.int32)
    slot_of = jnp.sum(jnp.where(order[None, :] == ids[:, None], ids[None, :], 0), axis=1)
    chunk = slot_of // slots_dev
    source = (((chunk % n_out) ^ z) * n_in + ((chunk // n_out) ^ t)) * slots_dev + slot_of % slots_dev
    source = source.astype(jnp.int32)
    lies = ids // slots_dev
    slot_here = (((lies % n_in) ^ t) * n_out + ((lies // n_in) ^ z)) * slots_dev + ids % slots_dev
    packed_of = jnp.sum(jnp.where(slot_here[:, None] == ids[None, :], order[None, :], 0), axis=1).astype(jnp.int32)

    part = jnp.arange(rows, dtype=jnp.int32)
    packed = packed_of[: rows // block].reshape(-1, 1) * block + jnp.arange(block, dtype=jnp.int32)[None, :]
    packed = packed.reshape(rows)
    starts = jnp.max(jnp.where(packed[:, None] >= ends[None, :], ends[None, :], 0), axis=1)
    position = (packed - starts).astype(F32)
    lane = jnp.arange(2 * HEAD, dtype=jnp.int32) % HEAD
    half = ROT // 2
    freq = 10000.0 ** (-2.0 * (lane % half).astype(F32) / ROT)
    phase = position[:, None] * freq[None, :]
    cos = jnp.where(lane < ROT, jnp.cos(phase), 1.0)
    sine = jnp.sin(phase)
    sin_l = jnp.where(lane < half, sine, 0.0)
    sin_r = jnp.where((lane >= half) & (lane < ROT), sine, 0.0)

    vectors = [ln1_gain, ln1_bias, ln2_gain, ln2_bias, b_qkv, b_out, b_in]
    sizes = [v.shape[0] for v in vectors]
    per_row = -(-len(vectors) // r_w)
    lanes = 128 // per_row
    qkv_cols = jnp.transpose(w_qkv.reshape(r_w, 3, n_in, cols), (2, 0, 1, 3)).reshape(n_in, r_w, 3 * cols)
    in_cols = jnp.transpose(w_in.reshape(r_w, n_dp, n_in, n_out, r_ff), (2, 0, 1, 3, 4)).reshape(n_in, r_w, ff_in)
    vec = jnp.stack([jnp.pad(v, (0, lanes - v.shape[0])) for v in vectors])
    vec = jnp.pad(vec, ((0, r_w * per_row - len(vectors)), (0, 0))).reshape(r_w, 128)
    vec = jnp.broadcast_to(vec[None], (n_in, r_w, 128))
    joined_cols = exchange_in(jnp.concatenate([qkv_cols, vec, in_cols], axis=2), t).reshape(n_in * r_w, -1)
    home = []
    for b in range(n_all):
        t_to, g_to = b // n_g, b % n_g
        home.append((b, ((g_to // n_out) * n_in + t_to) * n_out + g_to % n_out))
    out_rows = lax.ppermute(w_out, ALL_AXES, home).reshape(n_in * r_w, cols)
    first = jnp.concatenate([joined_cols[:, : 3 * cols + 128], out_rows], axis=1)
    first, to_send = lax.optimization_barrier((first, tokens))
    x_far = xor_swap(to_send, "in", n_in, 2)
    first = lax.all_gather(first, G_AXES, axis=0, tiled=False)
    second = jnp.concatenate([joined_cols[:, 3 * cols + 128 :], w_fc2], axis=1)
    second = lax.all_gather(second, G_AXES, axis=0, tiled=False)

    def natural(value):
        value = value.reshape(n_dp, n_out, n_in, r_w, -1)
        return jnp.transpose(value, (0, 2, 1, 3, 4)).reshape(n_all * r_w, -1)

    def by_owner(value):
        value = value.reshape(n_dp, n_in, n_out, r_w, -1)
        return jnp.transpose(value, (0, 2, 1, 3, 4)).reshape(n_g, n_in * r_w, -1)

    weight_qkv = natural(first[:, :, : 3 * cols])
    weight_out = first[:, :, 3 * cols + 128 :].reshape(cols, width)
    weight_in = natural(second[:, :, :ff_in])
    weight_fc2 = second[:, :, ff_in:].reshape(ff_in, width)
    vec_all = first[:, :, 3 * cols : 3 * cols + 128].reshape(n_dp, n_out, n_in, r_w * per_row, lanes)
    vec_all = jnp.transpose(vec_all[:, :, :, : len(vectors)], (3, 0, 2, 1, 4)).astype(F32)
    spans = [vec_all[i, ..., :size] for i, size in enumerate(sizes)]
    gain_one, shift_one, gain_two, shift_two = [s.reshape(width) for s in spans[:4]]
    bias_out = spans[5].reshape(width)
    bias_in = lax.dynamic_index_in_dim(spans[6], t, 1, keepdims=False).reshape(ff_in)
    bias_qkv = lax.dynamic_index_in_dim(spans[4].reshape(3, n_in, cols), t, 1, keepdims=False).reshape(-1)
    norms = jnp.concatenate([jnp.stack([gain_one, shift_one, gain_two, shift_two]), jnp.zeros((4, width), F32)])

    x_near = xor_swap(jnp.stack([tokens, x_far]), "in", n_in, 1)
    x_near, weight_qkv, norms, bias_qkv = lax.optimization_barrier((x_near, weight_qkv, norms, bias_qkv))
    x_all = join_in(tokens, x_far, x_near)
    x_all, to_send = lax.optimization_barrier((x_all, cotangent))
    dy_far = xor_swap(to_send, "in", n_in, 2)

    n1, n2, *parts = prep(z_arr, x_all, norms, weight_qkv, bias_qkv[None], cos, sin_l, sin_r, block)
    qk = exchange_out(parts[:h_in])
    v = exchange_out(parts[h_in:])
    qk, v, dy_far = lax.optimization_barrier((qk, v, dy_far))
    dy_near = xor_swap(jnp.stack([cotangent, dy_far]), "in", n_in, 1)
    *o, o_t, lse = attend_forward(source, packed_of, ends, qk, v, block)
    o, dy_near = lax.optimization_barrier((o, dy_near))
    dy_all = join_in(cotangent, dy_far, dy_near)
    o = exchange_out(o)
    do = exchange_out(grad_att(z_arr, dy_all, weight_out, block))

    hidden, grad_up, y_ff, dx_ff, sums_two, grad_b_in = feed(x_all, n2, dy_all, norms, weight_in, weight_fc2, bias_in[None])
    o, y_ff = lax.optimization_barrier((o, y_ff))
    o, y_part = project(z_arr, o, y_ff, weight_out, block)
    y_part = y_part.reshape(n_in, rows_dev, width)
    grad_fc2 = dot_tn(hidden, dy_all)
    grad_in = dot_tn(n2, grad_up)
    grad_out = dot_tn(o, dy_all)
    second_grads = jnp.concatenate(
        [
            by_owner(grad_in.astype(BF16)),
            grad_fc2.astype(BF16).reshape(n_g, r_ff, width),
            grad_out.astype(BF16).reshape(n_g, n_in * r_w, cols),
        ],
        axis=2,
    )

    do, second_grads, y_part = lax.optimization_barrier((do, second_grads, y_part))
    second_grads = lax.psum_scatter(second_grads, G_AXES, scatter_dimension=0, tiled=False)
    y_near = near_in(y_part)
    own = tokens.astype(F32)
    parts = attend_backward(source, packed_of, ends, qk, v, do, o_t, lse, block)
    parts, y_near = lax.optimization_barrier((parts, y_near))
    dqk = exchange_out(parts[:h_in])
    dv = exchange_out(parts[h_in:])
    y_far = xor_swap((y_part[2].astype(F32) + y_near[1].astype(F32)).astype(BF16), "in", n_in, 2)
    dqk, dv, y_far = lax.optimization_barrier((dqk, dv, y_far))
    y_sum = y_part[0].astype(F32) + y_near[0].astype(F32) + y_far.astype(F32)
    mixed = (own + y_sum + bias_out).astype(BF16)
    da, w_parts, sums_one, grad_b_qkv = post(
        z_arr, dqk, dv, x_all, dx_ff, norms, weight_qkv, cos, sin_l, sin_r, block
    )
    w_parts, da, mixed, second_grads = lax.optimization_barrier((w_parts, da, mixed, second_grads))
    in_part = exchange_in(second_grads[:, :ff_in].reshape(n_in, r_w, ff_in), t)
    w_parts = halves(w_parts.reshape(n_in, rows_dev, width))
    near = near_in(w_parts[0])
    near, w_next = lax.optimization_barrier((near, w_parts[1]))
    w_sum = jnp.concatenate([far_in(w_parts[0], near), far_in(w_next, near_in(w_next))], axis=1)

    grad_qkv = dot_tn(n1, da)

    def placed(vector, axis):
        spread = jnp.expand_dims(vector, axis)
        mask = (jnp.arange(n_in) == t).reshape([-1 if a == axis else 1 for a in range(spread.ndim)])
        return jnp.where(mask, spread, 0.0).reshape(-1)

    grad_own = cotangent.astype(F32)
    vec_grads = [
        sums_one[0],
        sums_one[1],
        sums_two[0],
        sums_two[1],
        placed(grad_b_qkv[0].reshape(3, cols), 1),
        jnp.sum(grad_own, axis=0),
        placed(grad_b_in[0].reshape(n_dp, n_out, r_ff), 1),
    ]
    vec_grads = [v.astype(BF16).reshape(n_dp, n_in, n_out, -1) for v in vec_grads]
    vec_grads = jnp.stack([jnp.pad(v, ((0, 0), (0, 0), (0, 0), (0, lanes - v.shape[-1]))) for v in vec_grads], axis=3)
    spare = r_w * per_row - len(vectors)
    vec_grads = jnp.pad(vec_grads, ((0, 0), (0, 0), (0, 0), (0, spare), (0, 0)))
    vec_grads = jnp.transpose(vec_grads, (0, 2, 1, 3, 4)).reshape(n_g, n_in * r_w, 128)
    first_grads = jnp.concatenate(
        [
            by_owner(grad_qkv.astype(BF16)),
            vec_grads,
        ],
        axis=2,
    )
    first_grads = lax.psum_scatter(first_grads, G_AXES, scatter_dimension=0, tiled=False)

    in_part = in_part.reshape(n_in, r_w, n_dp, n_out, r_ff)
    grad_w_in = jnp.transpose(in_part, (1, 2, 0, 3, 4)).reshape(r_w, ff).astype(F32)
    grad_w_fc2 = second_grads[:, ff_in : ff_in + width].astype(F32)
    back_home = [(b, a) for a, b in home]
    out_part = second_grads[:, ff_in + width :].reshape(r_w, width)
    grad_w_out = lax.ppermute(out_part, ALL_AXES, back_home).astype(F32)
    qkv_part = exchange_in(first_grads.reshape(n_in, r_w, 3 * cols + 128), t)
    qkv_grad = jnp.transpose(qkv_part[:, :, : 3 * cols].reshape(n_in, r_w, 3, cols), (1, 2, 0, 3))
    grad_w_qkv = qkv_grad.reshape(r_w, 3 * width).astype(F32)
    vec_part = jnp.sum(qkv_part[:, :, 3 * cols :].astype(F32), axis=0).reshape(r_w * per_row, lanes)
    vec_out = [vec_part[i, :size] for i, size in enumerate(sizes)]

    centred = own - jnp.mean(own, axis=-1, keepdims=True)
    own_rstd = lax.rsqrt(jnp.mean(centred * centred, axis=-1, keepdims=True) + EPS)
    own_hat = centred * own_rstd
    mean_w = jnp.mean(w_sum, axis=-1, keepdims=True)
    mean_wx = jnp.mean(w_sum * own_hat, axis=-1, keepdims=True)
    grad_tokens = grad_own + own_rstd * (w_sum - mean_w - own_hat * mean_wx)
    return (
        mixed,
        grad_tokens,
        vec_out[0],
        vec_out[1],
        vec_out[2],
        vec_out[3],
        grad_w_qkv,
        vec_out[4],
        grad_w_out,
        grad_w_in,
        vec_out[6],
        grad_w_fc2,
        vec_out[5],
    )


def solution(mesh):
    n_dp, n_ctx = mesh.shape["dp"], mesh.shape["ctx"]
    split = Mesh(mesh.devices.reshape(n_dp, GROUP_IN, n_ctx // GROUP_IN), ALL_AXES)
    mat, vec, group = P(ALL_AXES, None), P(ALL_AXES), P("dp", None)
    return jax.shard_map(
        body,
        mesh=split,
        in_specs=(mat, group, group, vec, vec, vec, vec, mat, vec, mat, mat, vec, mat, vec, mat),
        out_specs=(mat, mat, vec, vec, vec, vec, mat, vec, mat, mat, vec, mat, vec),
        check_vma=False,
    )
```

```python
import functools

import jax
import jax.numpy as jnp
from jax import lax
from jax.experimental import pallas as pl
from jax.experimental.pallas import tpu as pltpu
from jax.sharding import Mesh
from jax.sharding import PartitionSpec as P

HEAD = 64
ROT = 16
LONGEST = 2048
GROUP_IN = 4
TILE = 256
JOINT = TILE + TILE // 2
FQ, FK = 512, 512
BQ, BK = 512, 256
EPS = 1e-05
NEG = -1e30
F32 = jnp.float32
BF16 = jnp.bfloat16
G_AXES = ("dp", "out")
ALL_AXES = ("dp", "in", "out")


def dot(a, b):
    return jnp.dot(a, b, preferred_element_type=F32)


def dot_nt(a, b):
    return lax.dot_general(a, b, (((1,), (1,)), ((), ())), preferred_element_type=F32)


def dot_tn(a, b):
    return lax.dot_general(a, b, (((0,), (0,)), ((), ())), preferred_element_type=F32)


def xor_swap(value, axis, size, step):
    return lax.ppermute(value, axis, [(i, i ^ step) for i in range(size)])


def rotary(x, cos, sin_l, sin_r, sign):
    left = pltpu.roll(x, 128 - ROT // 2, 1)
    right = pltpu.roll(x, ROT // 2, 1)
    return x * cos - sign * (left * sin_l) + sign * (right * sin_r)


def pair_up(x, block):
    blocks = [x[i : i + block] for i in range(0, x.shape[0], block)]
    return jnp.concatenate([jnp.concatenate(blocks[i : i + 2], axis=1) for i in range(0, len(blocks), 2)], axis=0)


def unpair(x, block):
    parts = []
    for i in range(0, x.shape[0], block):
        parts += [x[i : i + block, :HEAD], x[i : i + block, HEAD:]]
    return jnp.concatenate(parts, axis=0)


def params(flops, size, exps=0):
    return dict(
        compiler_params=pltpu.CompilerParams(vmem_limit_bytes=60 * 2**20),
        cost_estimate=pl.CostEstimate(flops=flops, bytes_accessed=size, transcendentals=exps),
    )


def row_at(i, z):
    return (i, 0)


def whole_at(i, z):
    return (0, 0)


def piece(size):
    return pl.BlockSpec((size, 2 * HEAD), row_at)


def bf16_rows(rows):
    return jax.ShapeDtypeStruct((rows, 2 * HEAD), BF16)


def normalized(x_ref):
    x = x_ref[...].astype(F32)
    centred = x - jnp.mean(x, axis=-1, keepdims=True)
    return centred * lax.rsqrt(jnp.mean(centred * centred, axis=-1, keepdims=True) + EPS)


def turn(z, parts):
    out = []
    for step in range(len(parts)):
        pick = parts[step]
        for at in range(1, len(parts)):
            pick = jnp.where(z == at, parts[at ^ step], pick)
        out.append(pick)
    return out


def prep_kernel(heads, block, z_ref, x_ref, norm_ref, w_ref, b_ref, cos_ref, sl_ref, sr_ref, n1_ref, n2_ref, *out_refs):
    z = z_ref[0]
    xhat = normalized(x_ref)
    n1 = (xhat * norm_ref[0:1] + norm_ref[1:2]).astype(BF16)
    n1_ref[...] = n1
    n2_ref[...] = (xhat * norm_ref[2:3] + norm_ref[3:4]).astype(BF16)
    joined = dot(n1, w_ref[...]) + b_ref[...]
    cos, sl, sr = cos_ref[...], sl_ref[...], sr_ref[...]
    cols = heads * HEAD
    qk, v = [], []
    for h in range(heads):
        at = h * HEAD
        part = jnp.concatenate([joined[:, at : at + HEAD], joined[:, cols + at : cols + at + HEAD]], axis=1)
        qk.append(rotary(part, cos, sl, sr, 1.0))
        v.append(pair_up(joined[:, 2 * cols + at : 2 * cols + at + HEAD], block))
    for ref, one, two in zip(out_refs, turn(z, qk), turn(z, v)):
        ref[:TILE, :] = one.astype(BF16)
        ref[TILE:, :] = two.astype(BF16)


def prep(z, x, norms, w, bias, cos, sl, sr, block):
    rows, width = x.shape
    heads = w.shape[1] // (3 * HEAD)
    table = pl.BlockSpec((TILE, 2 * HEAD), row_at)
    tile = pl.BlockSpec((TILE, width), row_at)
    norm = jax.ShapeDtypeStruct((rows, width), BF16)
    return pl.pallas_call(
        functools.partial(prep_kernel, heads, block),
        grid_spec=pltpu.PrefetchScalarGridSpec(
            num_scalar_prefetch=1,
            grid=(rows // TILE,),
            in_specs=[
                tile,
                pl.BlockSpec(norms.shape, whole_at),
                pl.BlockSpec(w.shape, whole_at),
                pl.BlockSpec(bias.shape, whole_at),
                table,
                table,
                table,
            ],
            out_specs=[tile, tile] + [piece(JOINT)] * heads,
        ),
        out_shape=[norm, norm] + [bf16_rows(rows // TILE * JOINT)] * heads,
        **params(2 * rows * width * w.shape[1], 12 * 2**20),
    )(z, x, norms, w, bias, cos, sl, sr)


class Rows:
    def __init__(self, n_dp, n_in, n_out, r_w):
        self.n_in, self.n_out, self.r_w = n_in, n_out, r_w
        self.count = n_dp * n_in * n_out
        self.aligned = r_w % 16 == 0

    def place(self, block):
        out = block % self.n_out
        unit = (block // self.n_out) % self.n_in
        return block // (self.n_out * self.n_in) * self.n_out + out, unit * self.r_w


def feed_kernel(
    layout, x_ref, n2_ref, dy_ref, norm_ref, w_ref, b_ref, h_ref, du_ref, y_ref, dx_ref, sums_ref, db_ref, w_in_ref, w_fc2_ref
):
    units = w_in_ref.shape[1]

    @pl.when(pl.program_id(0) == 0)
    def _():
        size = w_ref.shape[1]
        for part in range(w_ref.shape[0]):
            w_fc2_ref[part * size : (part + 1) * size, :] = w_ref[part, :, units:]
            if not layout.aligned:
                w_in_ref[part * size : (part + 1) * size, :] = w_ref[part, :, :units]
        if layout.aligned:
            for at in range(layout.count):
                part, row = layout.place(at)
                w_in_ref[at * layout.r_w : (at + 1) * layout.r_w, :] = w_ref[part, row : row + layout.r_w, :units]

    up = dot(n2_ref[...], w_in_ref[...]) + b_ref[...]
    cdf = 0.5 + 0.5 * lax.erf(up * (0.5**0.5))
    hidden = (up * cdf).astype(BF16)
    slope = cdf + up * (jnp.exp(-0.5 * up * up) * 0.3989422804014327)
    grad_up = (dot_nt(dy_ref[...], w_fc2_ref[...]) * slope).astype(BF16)
    h_ref[...] = hidden
    du_ref[...] = grad_up
    y_ref[...] = dot(hidden, w_fc2_ref[...])
    grad_norm = dot_nt(grad_up, w_in_ref[...])
    dx_ref[...] = grad_norm * norm_ref[2:3]
    gain = jnp.sum(grad_norm * normalized(x_ref), axis=0, keepdims=True)
    shift = jnp.sum(grad_norm, axis=0, keepdims=True)
    bias = jnp.sum(grad_up.astype(F32), axis=0, keepdims=True)

    @pl.when(pl.program_id(0) == 0)
    def _():
        sums_ref[...] = jnp.zeros_like(sums_ref)
        db_ref[...] = jnp.zeros_like(db_ref)

    sums_ref[0:1] += gain
    sums_ref[1:2] += shift
    db_ref[0:1] += bias


def feed(layout, x, n2, dy, norms, w, bias):
    rows, width = x.shape
    units = bias.shape[1]
    row, whole = lambda i: (i, 0), lambda i: (0, 0)
    tile, tile_ff = pl.BlockSpec((TILE, width), row), pl.BlockSpec((TILE, units), row)
    return pl.pallas_call(
        functools.partial(feed_kernel, layout),
        grid=(rows // TILE,),
        in_specs=[
            tile,
            tile,
            tile,
            pl.BlockSpec(norms.shape, whole),
            pl.BlockSpec(w.shape, lambda i: (0, 0, 0)),
            pl.BlockSpec(bias.shape, whole),
        ],
        out_specs=[
            tile_ff,
            tile_ff,
            tile,
            tile,
            pl.BlockSpec((8, width), whole),
            pl.BlockSpec((8, units), whole),
        ],
        out_shape=[
            jax.ShapeDtypeStruct((rows, units), BF16),
            jax.ShapeDtypeStruct((rows, units), BF16),
            jax.ShapeDtypeStruct((rows, width), F32),
            jax.ShapeDtypeStruct((rows, width), F32),
            jax.ShapeDtypeStruct((8, width), F32),
            jax.ShapeDtypeStruct((8, units), F32),
        ],
        scratch_shapes=[pltpu.VMEM((width, units), BF16), pltpu.VMEM((units, width), BF16)],
        **params(8 * rows * width * units, 24 * 2**20, 2 * rows * units),
    )(x, n2, dy, norms, w, bias)


def feed_grads_kernel(layout, n2_ref, du_ref, h_ref, dy_ref, o_ref, out_ref):
    step = pl.program_id(0)
    size = out_ref.shape[1] // 9 * 4
    grad = dot_tn(n2_ref[...], du_ref[...]).astype(BF16)
    for b in range(TILE // layout.r_w):
        part, row = layout.place(step * (TILE // layout.r_w) + b)
        out_ref[part, pl.ds(pl.multiple_of(row, 16), layout.r_w), :] = grad[b * layout.r_w : (b + 1) * layout.r_w]
    grad = dot_tn(h_ref[...], dy_ref[...]).astype(BF16)
    for b in range(TILE // size):
        out_ref[step * (TILE // size) + b, size : 2 * size, :] = grad[b * size : (b + 1) * size]

    @pl.when(step == 0)
    def _():
        grad = dot_tn(o_ref[...], dy_ref[...]).astype(BF16)
        for part in range(out_ref.shape[0]):
            out_ref[part, 2 * size :, :] = grad[part * layout.r_w : (part + 1) * layout.r_w]


def feed_grads(layout, n2, du, h, dy, o):
    rows, width = n2.shape
    units = h.shape[1]
    parts = layout.count // layout.n_in
    shape = (parts, units // parts + layout.n_in * layout.r_w + layout.r_w, width)
    columns = pl.BlockSpec((rows, TILE), lambda i: (0, i))
    whole = lambda i: (0, 0)
    return pl.pallas_call(
        functools.partial(feed_grads_kernel, layout),
        grid=(width // TILE,),
        in_specs=[
            columns,
            pl.BlockSpec(du.shape, whole),
            columns,
            pl.BlockSpec(dy.shape, whole),
            pl.BlockSpec(o.shape, whole),
        ],
        out_specs=pl.BlockSpec(shape, lambda i: (0, 0, 0)),
        out_shape=jax.ShapeDtypeStruct(shape, BF16),
        **params(4 * rows * width * units, 14 * 2**20),
    )(n2, du, h, dy, o)


def qkv_grads_kernel(layout, n1_ref, da_ref, vec_ref, out_ref):
    step = pl.program_id(0)
    cols = da_ref.shape[1]
    grad = dot_tn(n1_ref[...], da_ref[...]).astype(BF16)
    for b in range(TILE // layout.r_w):
        part, row = layout.place(step * (TILE // layout.r_w) + b)
        out_ref[part, pl.ds(pl.multiple_of(row, 16), layout.r_w), :cols] = grad[b * layout.r_w : (b + 1) * layout.r_w]

    @pl.when(step == 0)
    def _():
        out_ref[:, :, cols:] = vec_ref[...]


def qkv_grads(layout, n1, da, vec):
    rows, width = n1.shape
    shape = (vec.shape[0], vec.shape[1], da.shape[1] + vec.shape[2])
    return pl.pallas_call(
        functools.partial(qkv_grads_kernel, layout),
        grid=(width // TILE,),
        in_specs=[
            pl.BlockSpec((rows, TILE), lambda i: (0, i)),
            pl.BlockSpec(da.shape, lambda i: (0, 0)),
            pl.BlockSpec(vec.shape, lambda i: (0, 0, 0)),
        ],
        out_specs=pl.BlockSpec(shape, lambda i: (0, 0, 0)),
        out_shape=jax.ShapeDtypeStruct(shape, BF16),
        **params(2 * rows * width * da.shape[1], 6 * 2**20),
    )(n1, da, vec)


def grad_att_kernel(heads, block, z_ref, dy_ref, wo_ref, *out_refs):
    grad = dot_nt(dy_ref[...], wo_ref[...])
    parts = [pair_up(grad[:, h * HEAD : (h + 1) * HEAD], block) for h in range(heads)]
    for ref, part in zip(out_refs, turn(z_ref[0], parts)):
        ref[...] = part.astype(BF16)


def grad_att(z, dy, wo, block):
    rows, width = dy.shape
    heads = wo.shape[0] // HEAD
    return pl.pallas_call(
        functools.partial(grad_att_kernel, heads, block),
        grid_spec=pltpu.PrefetchScalarGridSpec(
            num_scalar_prefetch=1,
            grid=(rows // TILE,),
            in_specs=[pl.BlockSpec((TILE, width), row_at), pl.BlockSpec(wo.shape, whole_at)],
            out_specs=[piece(TILE // 2)] * heads,
        ),
        out_shape=[bf16_rows(rows // 2)] * heads,
        **params(2 * rows * width * wo.shape[0], 4 * 2**20),
    )(z, dy, wo)


def project_kernel(heads, block, z_ref, y_ref, wo_ref, *refs):
    parts = turn(z_ref[0], [unpair(ref[...].astype(F32), block) for ref in refs[:heads]])
    o_ref, out_ref = refs[heads:]
    for h in range(0, heads, 2):
        o_ref[:, h * HEAD : (h + 2) * HEAD] = jnp.concatenate(parts[h : h + 2], axis=1).astype(BF16)
    out_ref[...] = (y_ref[...] + dot(o_ref[...], wo_ref[...])).astype(BF16)


def project(z, parts, y, wo, block):
    heads = len(parts)
    rows, width = y.shape
    tile = pl.BlockSpec((TILE, width), row_at)
    return pl.pallas_call(
        functools.partial(project_kernel, heads, block),
        grid_spec=pltpu.PrefetchScalarGridSpec(
            num_scalar_prefetch=1,
            grid=(rows // TILE,),
            in_specs=[tile, pl.BlockSpec(wo.shape, whole_at)] + [piece(TILE // 2)] * heads,
            out_specs=[pl.BlockSpec((TILE, heads * HEAD), row_at), tile],
        ),
        out_shape=[
            jax.ShapeDtypeStruct((rows, heads * HEAD), BF16),
            jax.ShapeDtypeStruct((rows, width), BF16),
        ],
        **params(2 * rows * width * wo.shape[0], 8 * 2**20),
    )(z, y, wo, *parts)


def post_kernel(
    heads, block, z_ref, x_ref, dx_ref, norm_ref, w_ref, cos_ref, sl_ref, sr_ref, *refs
):
    z = z_ref[0]
    dqk = turn(z, [ref[:TILE, :].astype(F32) for ref in refs[:heads]])
    dv = turn(z, [unpair(ref[TILE:, :].astype(F32), block) for ref in refs[:heads]])
    da_ref, sum_ref, sums_ref, db_ref = refs[heads:]
    cos, sl, sr = cos_ref[...], sl_ref[...], sr_ref[...]
    cols = heads * HEAD
    for h in range(0, heads, 2):
        at = h * HEAD
        one = rotary(dqk[h], cos, sl, sr, -1.0)
        two = rotary(dqk[h + 1], cos, sl, sr, -1.0)
        da_ref[:, at : at + 2 * HEAD] = jnp.concatenate([one[:, :HEAD], two[:, :HEAD]], axis=1).astype(BF16)
        da_ref[:, cols + at : cols + at + 2 * HEAD] = jnp.concatenate([one[:, HEAD:], two[:, HEAD:]], axis=1).astype(BF16)
        da_ref[:, 2 * cols + at : 2 * cols + at + 2 * HEAD] = jnp.concatenate(dv[h : h + 2], axis=1).astype(BF16)
    grad = da_ref[...]
    grad_norm = dot_nt(grad, w_ref[...])
    sum_ref[...] = (dx_ref[...] + grad_norm * norm_ref[0:1]).astype(BF16)
    gain = jnp.sum(grad_norm * normalized(x_ref), axis=0, keepdims=True)
    shift = jnp.sum(grad_norm, axis=0, keepdims=True)
    bias = jnp.sum(grad.astype(F32), axis=0, keepdims=True)

    @pl.when(pl.program_id(0) == 0)
    def _():
        sums_ref[...] = jnp.zeros_like(sums_ref)
        db_ref[...] = jnp.zeros_like(db_ref)

    sums_ref[0:1] += gain
    sums_ref[1:2] += shift
    db_ref[0:1] += bias


def post(z, grads, x, dx, norms, w, cos, sl, sr, block):
    heads = len(grads)
    rows, width = x.shape
    three = heads * 3 * HEAD
    table = pl.BlockSpec((TILE, 2 * HEAD), row_at)
    tile = pl.BlockSpec((TILE, width), row_at)
    return pl.pallas_call(
        functools.partial(post_kernel, heads, block),
        grid_spec=pltpu.PrefetchScalarGridSpec(
            num_scalar_prefetch=1,
            grid=(rows // TILE,),
            in_specs=[
                tile,
                tile,
                pl.BlockSpec(norms.shape, whole_at),
                pl.BlockSpec(w.shape, whole_at),
                table,
                table,
                table,
            ]
            + [piece(JOINT)] * heads,
            out_specs=[
                pl.BlockSpec((TILE, three), row_at),
                tile,
                pl.BlockSpec((8, width), whole_at),
                pl.BlockSpec((8, three), whole_at),
            ],
        ),
        out_shape=[
            jax.ShapeDtypeStruct((rows, three), BF16),
            jax.ShapeDtypeStruct((rows, width), BF16),
            jax.ShapeDtypeStruct((8, width), F32),
            jax.ShapeDtypeStruct((8, three), F32),
        ],
        **params(2 * rows * width * three, 14 * 2**20),
    )(z, x, dx, norms, w, cos, sl, sr, *grads)


def doc_start(packed, ends_ref, count):
    start = packed * 0
    for d in range(count):
        start = jnp.where(packed >= ends_ref[d], ends_ref[d], start)
    return start


def doc_end(packed, ends_ref, count):
    end = ends_ref[count - 1]
    for d in range(count - 2, -1, -1):
        end = jnp.where(packed < ends_ref[d], ends_ref[d], end)
    return end


def tile_at(i, size=TILE):
    return pl.ds(pl.multiple_of(i * size, size), size)


def load_half(ref, source, block):
    both = ref[pl.ds(pl.multiple_of((source // 2) * block, block), block), :].astype(F32)
    return jnp.where(source % 2 == 0, both[:, :HEAD], both[:, HEAD:])


def masked_scores(k_s, q_t, ends_ref, count, i, j, q_size, k_size):
    s = dot(k_s[tile_at(j, k_size), :], q_t[:HEAD, tile_at(i, q_size)])
    key_at = lax.broadcasted_iota(jnp.int32, (k_size, q_size), 0)
    query_at = lax.broadcasted_iota(jnp.int32, (k_size, q_size), 1)
    query_row = i * q_size + lax.broadcasted_iota(jnp.int32, (1, q_size), 1)
    first = doc_start(query_row, ends_ref, count) - j * k_size
    last = i * q_size - j * k_size + query_at
    return jnp.where((key_at >= first) & (key_at <= last), s, NEG)


def lay_out(pieces, whole):
    size = pieces[0].shape[0]
    for i, ref in enumerate(pieces):
        whole[i * size : (i + 1) * size, :] = ref[...]


def lay_out_joint(pieces, qk, v):
    at = 0
    for ref in pieces:
        for i in range(0, ref.shape[0], JOINT):
            qk[at : at + TILE, :] = ref[i : i + TILE, :]
            v[at // 2 : (at + TILE) // 2, :] = ref[i + TILE : i + JOINT, :]
            at += TILE


def forward_kernel(block, count, source_ref, packed_ref, ends_ref, *refs):
    pieces = (len(refs) - 8) // 2
    qkv_in, o_out = refs[:pieces], refs[pieces : 2 * pieces]
    o_t, lse_ref, k_s, q_t, v_t, o_s, qk_ref, v_ref = refs[2 * pieces :]
    rows = qk_ref.shape[0]
    lay_out_joint(qkv_in, qk_ref, v_ref)
    tiles = rows // TILE
    per = TILE // block
    scale = HEAD ** (-0.5)

    def gather(i, carry):
        qk, v = [], []
        for b in range(per):
            src = source_ref[i * per + b]
            qk.append(qk_ref[pl.ds(pl.multiple_of(src * block, block), block), :].astype(F32))
            v.append(load_half(v_ref, src, block))
        qk, v = jnp.concatenate(qk, axis=0), jnp.concatenate(v, axis=0)
        k_s[tile_at(i), :] = qk[:, HEAD:].astype(BF16)
        q_t[:, tile_at(i)] = (qk.T[:HEAD] * scale).astype(BF16)
        v_t[:, tile_at(i)] = v.T.astype(BF16)
        return carry

    lax.fori_loop(0, tiles, gather, 0)

    def forward(i, carry):
        here = tile_at(i, FQ)

        def step(j, state):
            top, total, acc = state
            s = masked_scores(k_s, q_t, ends_ref, count, i, j, FQ, FK)
            new_top = jnp.maximum(top, jnp.max(s, axis=0, keepdims=True))
            p = jnp.exp(s - new_top)
            fade = jnp.exp(top - new_top)
            total = total * fade + jnp.sum(p, axis=0, keepdims=True)
            acc = acc * fade + dot(v_t[:, tile_at(j, FK)], p.astype(BF16))
            return new_top, total, acc

        low = doc_start(i * FQ, ends_ref, count) // FK
        high = (i * FQ + FQ - 1) // FK
        top, total, acc = lax.fori_loop(
            low, high + 1, step, (jnp.full((1, FQ), NEG, F32), jnp.zeros((1, FQ), F32), jnp.zeros((HEAD, FQ), F32))
        )
        out = acc / total
        lse_ref[:, here] = top + jnp.log(total)
        o_t[:, here] = out
        o_s[here, :] = out.T
        return carry

    lax.fori_loop(0, rows // FQ, forward, 0)

    send_pairs(o_s, o_out, packed_ref, block)


def load_pair(whole, row, packed_ref, block):
    both = [whole[pl.ds(pl.multiple_of(packed_ref[row + b] * block, block), block), :] for b in range(2)]
    return jnp.concatenate(both, axis=1).astype(BF16)


def send_pairs(whole, out_refs, packed_ref, block):
    per = out_refs[0].shape[0] // block
    for at, ref in enumerate(out_refs):

        def one(i, carry):
            ref[pl.ds(pl.multiple_of(i * block, block), block), :] = load_pair(whole, 2 * (at * per + i), packed_ref, block)
            return carry

        lax.fori_loop(0, per, one, 0)


def backward_kernel(block, count, source_ref, packed_ref, ends_ref, *refs):
    pieces = (len(refs) - 16) // 3
    qkv_in, do_in = refs[:pieces], refs[pieces : 2 * pieces]
    o_t, lse_ref = refs[2 * pieces : 2 * pieces + 2]
    grads_out = refs[2 * pieces + 2 : 3 * pieces + 2]
    q_s, k_s, v_s, do_s, qk_t, do_t, dq_t, delta_s, dk_s, dv_s, qk_ref, v_ref, do_ref, dqk_ref = refs[3 * pieces + 2 :]
    rows = qk_ref.shape[0]
    lay_out_joint(qkv_in, qk_ref, v_ref)
    lay_out(do_in, do_ref)
    tiles = rows // TILE
    per = TILE // block
    scale = HEAD ** (-0.5)

    def gather(i, carry):
        qk, v, do = [], [], []
        for b in range(per):
            src = source_ref[i * per + b]
            qk.append(qk_ref[pl.ds(pl.multiple_of(src * block, block), block), :].astype(F32))
            v.append(load_half(v_ref, src, block))
            do.append(load_half(do_ref, src, block))
        qk, v, do = jnp.concatenate(qk, axis=0), jnp.concatenate(v, axis=0), jnp.concatenate(do, axis=0)
        here = tile_at(i)
        q_s[here, :] = (qk[:, :HEAD] * scale).astype(BF16)
        k_s[here, :] = qk[:, HEAD:].astype(BF16)
        turned = qk.T
        qk_t[:HEAD, here] = (turned[:HEAD] * scale).astype(BF16)
        qk_t[HEAD:, here] = turned[HEAD:].astype(BF16)
        v_s[here, :] = v.astype(BF16)
        do_s[here, :] = do.astype(BF16)
        do_turned = do.T
        do_t[:, here] = do_turned.astype(BF16)
        dq_t[:, here] = jnp.zeros((HEAD, TILE), F32)
        delta_s[:, here] = jnp.sum(o_t[:, here] * do_turned, axis=0, keepdims=True)
        return carry

    lax.fori_loop(0, tiles, gather, 0)

    def backward(j, carry):
        keys = tile_at(j, BK)

        def step(i, state):
            dk, dv = state
            here = tile_at(i, BQ)
            p = jnp.exp(masked_scores(k_s, qk_t, ends_ref, count, i, j, BQ, BK) - lse_ref[:, here])
            dp = dot(v_s[keys, :], do_t[:, here])
            ds = (p * (dp - delta_s[:, here])).astype(BF16)
            dv = dv + dot(p.astype(BF16), do_s[here, :])
            dk = dk + dot(ds, q_s[here, :])
            dq_t[:, here] += dot(qk_t[HEAD:, keys], ds)
            return dk, dv

        high = (doc_end(j * BK + BK - 1, ends_ref, count) - 1) // BQ
        zero = jnp.zeros((BK, HEAD), F32)
        dk, dv = lax.fori_loop(j * BK // BQ, high + 1, step, (zero, zero))
        dk_s[keys, :] = dk
        dv_s[keys, :] = dv
        return carry

    lax.fori_loop(0, rows // BK, backward, 0)

    def scatter(i, carry):
        here = tile_at(i)
        dq = (dq_t[:, here] * scale).T
        dqk = jnp.concatenate([dq, dk_s[here, :]], axis=1).astype(BF16)
        for b in range(per):
            dst = pl.ds(pl.multiple_of(source_ref[i * per + b] * block, block), block)
            dqk_ref[dst, :] = dqk[b * block : (b + 1) * block, :]
        return carry

    lax.fori_loop(0, tiles, scatter, 0)

    per_piece = rows // pieces // TILE
    for at, ref in enumerate(grads_out):

        def one(i, carry):
            start = at * per_piece + i
            out = pl.multiple_of(i * JOINT, JOINT)
            ref[pl.ds(out, TILE), :] = dqk_ref[tile_at(start), :]
            for b in range(0, per, 2):
                row = pl.multiple_of(out + TILE + b // 2 * block, block)
                ref[pl.ds(row, block), :] = load_pair(dv_s, start * per + b, packed_ref, block)
            return carry

        lax.fori_loop(0, per_piece, one, 0)


IN_VMEM = pl.BlockSpec(memory_space=pltpu.VMEM)
IN_SMEM = pl.BlockSpec(memory_space=pltpu.SMEM)


def attend_forward(source, packed, ends, qkv, block):
    pieces = len(qkv)
    rows = pieces * (qkv[0].shape[0] // JOINT * TILE)
    turned = pltpu.VMEM((HEAD, rows), BF16)
    return pl.pallas_call(
        functools.partial(forward_kernel, block, ends.shape[0]),
        in_specs=[IN_SMEM] * 3 + [IN_VMEM] * pieces,
        out_specs=[IN_VMEM] * (pieces + 2),
        out_shape=[bf16_rows(rows // (2 * pieces))] * pieces
        + [
            jax.ShapeDtypeStruct((HEAD, rows), F32),
            jax.ShapeDtypeStruct((1, rows), F32),
        ],
        scratch_shapes=[
            pltpu.VMEM((rows, HEAD), BF16),
            turned,
            turned,
            pltpu.VMEM((rows, HEAD), F32),
            pltpu.VMEM((rows, 2 * HEAD), BF16),
            pltpu.VMEM((rows // 2, 2 * HEAD), BF16),
        ],
        **params(rows * rows * HEAD * 40, 6 * rows * HEAD * 2, rows * rows),
    )(source, packed, ends, *qkv)


def attend_backward(source, packed, ends, qkv, do, o_t, lse, block):
    pieces = len(qkv)
    rows = pieces * (qkv[0].shape[0] // JOINT * TILE)
    half = pltpu.VMEM((rows, HEAD), BF16)
    wide = pltpu.VMEM((rows, HEAD), F32)
    pairs = pltpu.VMEM((rows // 2, 2 * HEAD), BF16)
    whole = pltpu.VMEM((rows, 2 * HEAD), BF16)
    return pl.pallas_call(
        functools.partial(backward_kernel, block, ends.shape[0]),
        in_specs=[IN_SMEM] * 3 + [IN_VMEM] * (2 * pieces + 2),
        out_specs=[IN_VMEM] * pieces,
        out_shape=[bf16_rows(qkv[0].shape[0])] * pieces,
        scratch_shapes=[
            half,
            half,
            half,
            half,
            pltpu.VMEM((2 * HEAD, rows), BF16),
            pltpu.VMEM((HEAD, rows), BF16),
            pltpu.VMEM((HEAD, rows), F32),
            pltpu.VMEM((1, rows), F32),
            wide,
            wide,
            whole,
            pairs,
            pairs,
            whole,
        ],
        **params(rows * rows * HEAD * 40, 12 * rows * HEAD * 2, rows * rows),
    )(source, packed, ends, *qkv, *do, o_t, lse)


def join_in(value, far, near):
    return jnp.concatenate([value, near[0], far, near[1]])


def halves(parts):
    cut = parts.shape[-1] // 2
    return [parts[..., :cut], parts[..., cut:]]


def near_in(parts):
    return xor_swap(jnp.stack([parts[1], parts[3]]), "in", GROUP_IN, 1)


def far_in(parts, near):
    far = xor_swap((parts[2].astype(F32) + near[1].astype(F32)).astype(BF16), "in", GROUP_IN, 2)
    return parts[0].astype(F32) + near[0].astype(F32) + far.astype(F32)


def exchange_in(parts, t):
    here = [lax.dynamic_index_in_dim(parts, t ^ s, 0, keepdims=False) for s in range(GROUP_IN)]
    there = [here[0]] + [xor_swap(here[s], "in", GROUP_IN, s) for s in range(1, GROUP_IN)]
    stacked = jnp.stack(there)
    return jnp.stack([lax.dynamic_index_in_dim(stacked, t ^ u, 0, keepdims=False) for u in range(GROUP_IN)])


def exchange_out(parts):
    size = len(parts)
    return [parts[0]] + [xor_swap(parts[s], "out", size, s) for s in range(1, size)]


def body(
    tokens,
    seq_lengths,
    dealing,
    ln1_gain,
    ln1_bias,
    ln2_gain,
    ln2_bias,
    w_qkv,
    b_qkv,
    w_out,
    w_in,
    b_in,
    w_fc2,
    b_out,
    cotangent,
):
    n_dp, n_out, n_in = lax.axis_size("dp"), lax.axis_size("out"), lax.axis_size("in")
    n_g = n_dp * n_out
    n_all = n_g * n_in
    rows_dev, width = tokens.shape
    ff = w_in.shape[1]
    ff_in = ff // n_in
    r_w = w_in.shape[0]
    r_ff = w_fc2.shape[0]
    block = LONGEST // (2 * n_out * n_in)
    slots_dev = rows_dev // block
    heads = width // HEAD
    h_in = heads // n_in
    cols = h_in * HEAD
    rows = rows_dev * n_in
    layout = Rows(n_dp, n_in, n_out, r_w)
    z, t = lax.axis_index("out"), lax.axis_index("in")
    z_arr = z[None].astype(jnp.int32)
    lengths, order = seq_lengths[0], dealing[0]
    ends = jnp.cumsum(lengths)

    slots = order.shape[0]
    ids = jnp.arange(slots, dtype=jnp.int32)
    slot_of = jnp.sum(jnp.where(order[None, :] == ids[:, None], ids[None, :], 0), axis=1)
    chunk = slot_of // slots_dev
    source = (((chunk % n_out) ^ z) * n_in + ((chunk // n_out) ^ t)) * slots_dev + slot_of % slots_dev
    source = source.astype(jnp.int32)
    lies = ids // slots_dev
    slot_here = (((lies % n_in) ^ t) * n_out + ((lies // n_in) ^ z)) * slots_dev + ids % slots_dev
    packed_of = jnp.sum(jnp.where(slot_here[:, None] == ids[None, :], order[None, :], 0), axis=1).astype(jnp.int32)

    part = jnp.arange(rows, dtype=jnp.int32)
    packed = packed_of[: rows // block].reshape(-1, 1) * block + jnp.arange(block, dtype=jnp.int32)[None, :]
    packed = packed.reshape(rows)
    starts = jnp.max(jnp.where(packed[:, None] >= ends[None, :], ends[None, :], 0), axis=1)
    position = (packed - starts).astype(F32)
    lane = jnp.arange(2 * HEAD, dtype=jnp.int32) % HEAD
    half = ROT // 2
    freq = 10000.0 ** (-2.0 * (lane % half).astype(F32) / ROT)
    phase = position[:, None] * freq[None, :]
    cos = jnp.where(lane < ROT, jnp.cos(phase), 1.0)
    sine = jnp.sin(phase)
    sin_l = jnp.where(lane < half, sine, 0.0)
    sin_r = jnp.where((lane >= half) & (lane < ROT), sine, 0.0)

    vectors = [ln1_gain, ln1_bias, ln2_gain, ln2_bias, b_qkv, b_out, b_in]
    sizes = [v.shape[0] for v in vectors]
    per_row = -(-len(vectors) // r_w)
    lanes = 128 // per_row
    qkv_cols = jnp.transpose(w_qkv.reshape(r_w, 3, n_in, cols), (2, 0, 1, 3)).reshape(n_in, r_w, 3 * cols)
    in_cols = jnp.transpose(w_in.reshape(r_w, n_dp, n_in, n_out, r_ff), (2, 0, 1, 3, 4)).reshape(n_in, r_w, ff_in)
    vec = jnp.stack([jnp.pad(v, (0, lanes - v.shape[0])) for v in vectors])
    vec = jnp.pad(vec, ((0, r_w * per_row - len(vectors)), (0, 0))).reshape(r_w, 128)
    vec = jnp.broadcast_to(vec[None], (n_in, r_w, 128))
    joined_cols = exchange_in(jnp.concatenate([qkv_cols, vec, in_cols], axis=2), t).reshape(n_in * r_w, -1)
    home = []
    for b in range(n_all):
        t_to, g_to = b // n_g, b % n_g
        home.append((b, ((g_to // n_out) * n_in + t_to) * n_out + g_to % n_out))
    out_rows = lax.ppermute(w_out, ALL_AXES, home).reshape(n_in * r_w, cols)
    first = jnp.concatenate([joined_cols[:, : 3 * cols + 128], out_rows], axis=1)
    first, to_send = lax.optimization_barrier((first, tokens))
    x_far = xor_swap(to_send, "in", n_in, 2)
    first = lax.all_gather(first, G_AXES, axis=0, tiled=False)
    second = jnp.concatenate([joined_cols[:, 3 * cols + 128 :], w_fc2], axis=1)
    second = lax.all_gather(second, G_AXES, axis=0, tiled=False)

    def natural(value):
        value = value.reshape(n_dp, n_out, n_in, r_w, -1)
        return jnp.transpose(value, (0, 2, 1, 3, 4)).reshape(n_all * r_w, -1)

    def by_owner(value):
        value = value.reshape(n_dp, n_in, n_out, r_w, -1)
        return jnp.transpose(value, (0, 2, 1, 3, 4)).reshape(n_g, n_in * r_w, -1)

    weight_qkv = natural(first[:, :, : 3 * cols])
    weight_out = first[:, :, 3 * cols + 128 :].reshape(cols, width)
    if not layout.aligned:
        in_rows = natural(second[:, :, :ff_in]).reshape(n_g, n_in * r_w, ff_in)
        second = jnp.concatenate([in_rows, second[:, :, ff_in:]], axis=2)
    vec_all = first[:, :, 3 * cols : 3 * cols + 128].reshape(n_dp, n_out, n_in, r_w * per_row, lanes)
    vec_all = jnp.transpose(vec_all[:, :, :, : len(vectors)], (3, 0, 2, 1, 4)).astype(F32)
    spans = [vec_all[i, ..., :size] for i, size in enumerate(sizes)]
    gain_one, shift_one, gain_two, shift_two = [s.reshape(width) for s in spans[:4]]
    bias_out = spans[5].reshape(width)
    bias_in = lax.dynamic_index_in_dim(spans[6], t, 1, keepdims=False).reshape(ff_in)
    bias_qkv = lax.dynamic_index_in_dim(spans[4].reshape(3, n_in, cols), t, 1, keepdims=False).reshape(-1)
    norms = jnp.concatenate([jnp.stack([gain_one, shift_one, gain_two, shift_two]), jnp.zeros((4, width), F32)])

    x_near = xor_swap(jnp.stack([tokens, x_far]), "in", n_in, 1)
    x_near, weight_qkv, norms, bias_qkv = lax.optimization_barrier((x_near, weight_qkv, norms, bias_qkv))
    x_all = join_in(tokens, x_far, x_near)
    x_all, to_send = lax.optimization_barrier((x_all, cotangent))
    dy_far = xor_swap(to_send, "in", n_in, 2)

    n1, n2, *qkv = prep(z_arr, x_all, norms, weight_qkv, bias_qkv[None], cos, sin_l, sin_r, block)
    qkv = exchange_out(qkv)
    qkv, dy_far = lax.optimization_barrier((qkv, dy_far))
    dy_near = xor_swap(jnp.stack([cotangent, dy_far]), "in", n_in, 1)
    *o, o_t, lse = attend_forward(source, packed_of, ends, qkv, block)
    o, dy_near = lax.optimization_barrier((o, dy_near))
    dy_all = join_in(cotangent, dy_far, dy_near)
    o = exchange_out(o)
    do = exchange_out(grad_att(z_arr, dy_all, weight_out, block))

    hidden, grad_up, y_ff, dx_ff, sums_two, grad_b_in = feed(
        layout, x_all, n2, dy_all, norms, second, bias_in[None]
    )
    o, y_ff = lax.optimization_barrier((o, y_ff))
    o, y_part = project(z_arr, o, y_ff, weight_out, block)
    y_part = y_part.reshape(n_in, rows_dev, width)
    if layout.aligned:
        second_grads = feed_grads(layout, n2, grad_up, hidden, dy_all, o)
    else:
        second_grads = jnp.concatenate(
            [
                by_owner(dot_tn(n2, grad_up).astype(BF16)),
                dot_tn(hidden, dy_all).astype(BF16).reshape(n_g, r_ff, width),
                dot_tn(o, dy_all).astype(BF16).reshape(n_g, r_w, width),
            ],
            axis=1,
        )

    do, second_grads, y_part = lax.optimization_barrier((do, second_grads, y_part))
    second_grads = lax.psum_scatter(second_grads, G_AXES, scatter_dimension=0, tiled=False)
    y_near = near_in(y_part)
    own = tokens.astype(F32)
    parts = attend_backward(source, packed_of, ends, qkv, do, o_t, lse, block)
    parts, y_near = lax.optimization_barrier((parts, y_near))
    parts = exchange_out(parts)
    y_far = xor_swap((y_part[2].astype(F32) + y_near[1].astype(F32)).astype(BF16), "in", n_in, 2)
    parts, y_far = lax.optimization_barrier((parts, y_far))
    y_sum = y_part[0].astype(F32) + y_near[0].astype(F32) + y_far.astype(F32)
    mixed = (own + y_sum + bias_out).astype(BF16)
    da, w_parts, sums_one, grad_b_qkv = post(
        z_arr, parts, x_all, dx_ff, norms, weight_qkv, cos, sin_l, sin_r, block
    )
    w_parts, da, mixed, second_grads = lax.optimization_barrier((w_parts, da, mixed, second_grads))
    in_part = exchange_in(second_grads[: n_in * r_w].reshape(n_in, r_w, ff_in), t)
    w_parts = halves(w_parts.reshape(n_in, rows_dev, width))
    near = near_in(w_parts[0])
    near, w_next = lax.optimization_barrier((near, w_parts[1]))
    w_sum = jnp.concatenate([far_in(w_parts[0], near), far_in(w_next, near_in(w_next))], axis=1)

    def placed(vector, axis):
        spread = jnp.expand_dims(vector, axis)
        mask = (jnp.arange(n_in) == t).reshape([-1 if a == axis else 1 for a in range(spread.ndim)])
        return jnp.where(mask, spread, 0.0).reshape(-1)

    grad_own = cotangent.astype(F32)
    vec_grads = [
        sums_one[0],
        sums_one[1],
        sums_two[0],
        sums_two[1],
        placed(grad_b_qkv[0].reshape(3, cols), 1),
        jnp.sum(grad_own, axis=0),
        placed(grad_b_in[0].reshape(n_dp, n_out, r_ff), 1),
    ]
    vec_grads = [v.astype(BF16).reshape(n_dp, n_in, n_out, -1) for v in vec_grads]
    vec_grads = jnp.stack([jnp.pad(v, ((0, 0), (0, 0), (0, 0), (0, lanes - v.shape[-1]))) for v in vec_grads], axis=3)
    spare = r_w * per_row - len(vectors)
    vec_grads = jnp.pad(vec_grads, ((0, 0), (0, 0), (0, 0), (0, spare), (0, 0)))
    vec_grads = jnp.transpose(vec_grads, (0, 2, 1, 3, 4)).reshape(n_g, n_in * r_w, 128)
    if layout.aligned:
        first_grads = qkv_grads(layout, n1, da, vec_grads)
    else:
        first_grads = jnp.concatenate([by_owner(dot_tn(n1, da).astype(BF16)), vec_grads], axis=2)
    first_grads = lax.psum_scatter(first_grads, G_AXES, scatter_dimension=0, tiled=False)

    in_part = in_part.reshape(n_in, r_w, n_dp, n_out, r_ff)
    grad_w_in = jnp.transpose(in_part, (1, 2, 0, 3, 4)).reshape(r_w, ff).astype(F32)
    grad_w_fc2 = second_grads[n_in * r_w : n_in * r_w + r_ff].astype(F32)
    back_home = [(b, a) for a, b in home]
    out_part = second_grads[n_in * r_w + r_ff :]
    grad_w_out = lax.ppermute(out_part, ALL_AXES, back_home).astype(F32)
    qkv_part = exchange_in(first_grads.reshape(n_in, r_w, 3 * cols + 128), t)
    qkv_grad = jnp.transpose(qkv_part[:, :, : 3 * cols].reshape(n_in, r_w, 3, cols), (1, 2, 0, 3))
    grad_w_qkv = qkv_grad.reshape(r_w, 3 * width).astype(F32)
    vec_part = jnp.sum(qkv_part[:, :, 3 * cols :].astype(F32), axis=0).reshape(r_w * per_row, lanes)
    vec_out = [vec_part[i, :size] for i, size in enumerate(sizes)]

    centred = own - jnp.mean(own, axis=-1, keepdims=True)
    own_rstd = lax.rsqrt(jnp.mean(centred * centred, axis=-1, keepdims=True) + EPS)
    own_hat = centred * own_rstd
    mean_w = jnp.mean(w_sum, axis=-1, keepdims=True)
    mean_wx = jnp.mean(w_sum * own_hat, axis=-1, keepdims=True)
    grad_tokens = grad_own + own_rstd * (w_sum - mean_w - own_hat * mean_wx)
    return (
        mixed,
        grad_tokens,
        vec_out[0],
        vec_out[1],
        vec_out[2],
        vec_out[3],
        grad_w_qkv,
        vec_out[4],
        grad_w_out,
        grad_w_in,
        vec_out[6],
        grad_w_fc2,
        vec_out[5],
    )


def solution(mesh):
    n_dp, n_ctx = mesh.shape["dp"], mesh.shape["ctx"]
    split = Mesh(mesh.devices.reshape(n_dp, GROUP_IN, n_ctx // GROUP_IN), ALL_AXES)
    mat, vec, group = P(ALL_AXES, None), P(ALL_AXES), P("dp", None)
    return jax.shard_map(
        body,
        mesh=split,
        in_specs=(mat, group, group, vec, vec, vec, vec, mat, vec, mat, mat, vec, mat, vec, mat),
        out_specs=(mat, mat, vec, vec, vec, vec, mat, vec, mat, mat, vec, mat, vec),
        check_vma=False,
    )
```

```python
import functools

import jax
import jax.numpy as jnp
from jax import lax
from jax.experimental import pallas as pl
from jax.experimental.pallas import tpu as pltpu
from jax.sharding import Mesh
from jax.sharding import PartitionSpec as P

HEAD = 64
ROT = 16
LONGEST = 2048
GROUP_IN = 4
TILE = 256
JOINT = TILE + TILE // 2
FQ, FK = 512, 512
BQ, BK = 512, 256
EPS = 1e-05
NEG = -1e30
F32 = jnp.float32
BF16 = jnp.bfloat16
G_AXES = ("dp", "out")
ALL_AXES = ("dp", "in", "out")


def dot(a, b):
    return jnp.dot(a, b, preferred_element_type=F32)


def dot_nt(a, b):
    return lax.dot_general(a, b, (((1,), (1,)), ((), ())), preferred_element_type=F32)


def dot_tn(a, b):
    return lax.dot_general(a, b, (((0,), (0,)), ((), ())), preferred_element_type=F32)


def xor_swap(value, axis, size, step):
    return lax.ppermute(value, axis, [(i, i ^ step) for i in range(size)])


def rotary(x, cos, sin_l, sin_r, sign):
    left = pltpu.roll(x, 128 - ROT // 2, 1)
    right = pltpu.roll(x, ROT // 2, 1)
    return x * cos - sign * (left * sin_l) + sign * (right * sin_r)


def pair_up(x, block):
    blocks = [x[i : i + block] for i in range(0, x.shape[0], block)]
    return jnp.concatenate([jnp.concatenate(blocks[i : i + 2], axis=1) for i in range(0, len(blocks), 2)], axis=0)


def unpair(x, block):
    parts = []
    for i in range(0, x.shape[0], block):
        parts += [x[i : i + block, :HEAD], x[i : i + block, HEAD:]]
    return jnp.concatenate(parts, axis=0)


def params(flops, size, exps=0):
    return dict(
        compiler_params=pltpu.CompilerParams(vmem_limit_bytes=60 * 2**20),
        cost_estimate=pl.CostEstimate(flops=flops, bytes_accessed=size, transcendentals=exps),
    )


def row_at(i, z):
    return (i, 0)


def whole_at(i, z):
    return (0, 0)


def piece(size):
    return pl.BlockSpec((size, 2 * HEAD), row_at)


def bf16_rows(rows):
    return jax.ShapeDtypeStruct((rows, 2 * HEAD), BF16)


def normalized(x_ref):
    x = x_ref[...].astype(F32)
    centred = x - jnp.mean(x, axis=-1, keepdims=True)
    return centred * lax.rsqrt(jnp.mean(centred * centred, axis=-1, keepdims=True) + EPS)


def turn(z, parts):
    out = []
    for step in range(len(parts)):
        pick = parts[step]
        for at in range(1, len(parts)):
            pick = jnp.where(z == at, parts[at ^ step], pick)
        out.append(pick)
    return out


def prep_kernel(heads, block, z_ref, x_ref, norm_ref, w_ref, b_ref, cos_ref, sl_ref, sr_ref, n1_ref, n2_ref, *out_refs):
    z = z_ref[0]
    xhat = normalized(x_ref)
    n1 = (xhat * norm_ref[0:1] + norm_ref[1:2]).astype(BF16)
    n1_ref[...] = n1
    n2_ref[...] = (xhat * norm_ref[2:3] + norm_ref[3:4]).astype(BF16)
    joined = dot(n1, w_ref[...]) + b_ref[...]
    cos, sl, sr = cos_ref[...], sl_ref[...], sr_ref[...]
    cols = heads * HEAD
    qk, v = [], []
    for h in range(heads):
        at = h * HEAD
        part = jnp.concatenate([joined[:, at : at + HEAD], joined[:, cols + at : cols + at + HEAD]], axis=1)
        qk.append(rotary(part, cos, sl, sr, 1.0))
        v.append(pair_up(joined[:, 2 * cols + at : 2 * cols + at + HEAD], block))
    for ref, one, two in zip(out_refs, turn(z, qk), turn(z, v)):
        ref[:TILE, :] = one.astype(BF16)
        ref[TILE:, :] = two.astype(BF16)


def prep(z, x, norms, w, bias, cos, sl, sr, block):
    rows, width = x.shape
    heads = w.shape[1] // (3 * HEAD)
    table = pl.BlockSpec((TILE, 2 * HEAD), row_at)
    tile = pl.BlockSpec((TILE, width), row_at)
    norm = jax.ShapeDtypeStruct((rows, width), BF16)
    return pl.pallas_call(
        functools.partial(prep_kernel, heads, block),
        grid_spec=pltpu.PrefetchScalarGridSpec(
            num_scalar_prefetch=1,
            grid=(rows // TILE,),
            in_specs=[
                tile,
                pl.BlockSpec(norms.shape, whole_at),
                pl.BlockSpec(w.shape, whole_at),
                pl.BlockSpec(bias.shape, whole_at),
                table,
                table,
                table,
            ],
            out_specs=[tile, tile] + [piece(JOINT)] * heads,
        ),
        out_shape=[norm, norm] + [bf16_rows(rows // TILE * JOINT)] * heads,
        **params(2 * rows * width * w.shape[1], 12 * 2**20),
    )(z, x, norms, w, bias, cos, sl, sr)


class Rows:
    def __init__(self, n_dp, n_in, n_out, r_w):
        self.n_in, self.n_out, self.r_w = n_in, n_out, r_w
        self.count = n_dp * n_in * n_out
        self.aligned = r_w % 16 == 0

    def place(self, block):
        out = block % self.n_out
        unit = (block // self.n_out) % self.n_in
        return block // (self.n_out * self.n_in) * self.n_out + out, unit * self.r_w


def feed_kernel(
    layout, x_ref, n2_ref, dy_ref, norm_ref, w_ref, b_ref, h_ref, du_ref, y_ref, dx_ref, sums_ref, db_ref, w_in_ref, w_fc2_ref
):
    units = w_in_ref.shape[1]

    @pl.when(pl.program_id(0) == 0)
    def _():
        size = w_ref.shape[1]
        for part in range(w_ref.shape[0]):
            w_fc2_ref[part * size : (part + 1) * size, :] = w_ref[part, :, units:]
            if not layout.aligned:
                w_in_ref[part * size : (part + 1) * size, :] = w_ref[part, :, :units]
        if layout.aligned:
            for at in range(layout.count):
                part, row = layout.place(at)
                w_in_ref[at * layout.r_w : (at + 1) * layout.r_w, :] = w_ref[part, row : row + layout.r_w, :units]

    up = dot(n2_ref[...], w_in_ref[...]) + b_ref[...]
    cdf = 0.5 + 0.5 * lax.erf(up * (0.5**0.5))
    hidden = (up * cdf).astype(BF16)
    slope = cdf + up * (jnp.exp(-0.5 * up * up) * 0.3989422804014327)
    grad_up = (dot_nt(dy_ref[...], w_fc2_ref[...]) * slope).astype(BF16)
    h_ref[...] = hidden
    du_ref[...] = grad_up
    y_ref[...] = dot(hidden, w_fc2_ref[...])
    grad_norm = dot_nt(grad_up, w_in_ref[...])
    dx_ref[...] = grad_norm * norm_ref[2:3]
    gain = jnp.sum(grad_norm * normalized(x_ref), axis=0, keepdims=True)
    shift = jnp.sum(grad_norm, axis=0, keepdims=True)
    bias = jnp.sum(grad_up.astype(F32), axis=0, keepdims=True)

    @pl.when(pl.program_id(0) == 0)
    def _():
        sums_ref[...] = jnp.zeros_like(sums_ref)
        db_ref[...] = jnp.zeros_like(db_ref)

    sums_ref[0:1] += gain
    sums_ref[1:2] += shift
    db_ref[0:1] += bias


def feed(layout, x, n2, dy, norms, w, bias):
    rows, width = x.shape
    units = bias.shape[1]
    row, whole = lambda i: (i, 0), lambda i: (0, 0)
    tile, tile_ff = pl.BlockSpec((TILE, width), row), pl.BlockSpec((TILE, units), row)
    return pl.pallas_call(
        functools.partial(feed_kernel, layout),
        grid=(rows // TILE,),
        in_specs=[
            tile,
            tile,
            tile,
            pl.BlockSpec(norms.shape, whole),
            pl.BlockSpec(w.shape, lambda i: (0, 0, 0)),
            pl.BlockSpec(bias.shape, whole),
        ],
        out_specs=[
            tile_ff,
            tile_ff,
            tile,
            tile,
            pl.BlockSpec((8, width), whole),
            pl.BlockSpec((8, units), whole),
        ],
        out_shape=[
            jax.ShapeDtypeStruct((rows, units), BF16),
            jax.ShapeDtypeStruct((rows, units), BF16),
            jax.ShapeDtypeStruct((rows, width), F32),
            jax.ShapeDtypeStruct((rows, width), F32),
            jax.ShapeDtypeStruct((8, width), F32),
            jax.ShapeDtypeStruct((8, units), F32),
        ],
        scratch_shapes=[pltpu.VMEM((width, units), BF16), pltpu.VMEM((units, width), BF16)],
        **params(8 * rows * width * units, 24 * 2**20, 2 * rows * units),
    )(x, n2, dy, norms, w, bias)


def feed_grads_kernel(layout, n2_ref, du_ref, h_ref, dy_ref, o_ref, out_ref):
    step = pl.program_id(0)
    size = out_ref.shape[1] // 9 * 4
    grad = dot_tn(n2_ref[...], du_ref[...]).astype(BF16)
    for b in range(TILE // layout.r_w):
        part, row = layout.place(step * (TILE // layout.r_w) + b)
        out_ref[part, pl.ds(pl.multiple_of(row, 16), layout.r_w), :] = grad[b * layout.r_w : (b + 1) * layout.r_w]
    grad = dot_tn(h_ref[...], dy_ref[...]).astype(BF16)
    for b in range(TILE // size):
        out_ref[step * (TILE // size) + b, size : 2 * size, :] = grad[b * size : (b + 1) * size]

    @pl.when(step == 0)
    def _():
        grad = dot_tn(o_ref[...], dy_ref[...]).astype(BF16)
        for part in range(out_ref.shape[0]):
            out_ref[part, 2 * size :, :] = grad[part * layout.r_w : (part + 1) * layout.r_w]


def feed_grads(layout, n2, du, h, dy, o):
    rows, width = n2.shape
    units = h.shape[1]
    parts = layout.count // layout.n_in
    shape = (parts, units // parts + layout.n_in * layout.r_w + layout.r_w, width)
    columns = pl.BlockSpec((rows, TILE), lambda i: (0, i))
    whole = lambda i: (0, 0)
    return pl.pallas_call(
        functools.partial(feed_grads_kernel, layout),
        grid=(width // TILE,),
        in_specs=[
            columns,
            pl.BlockSpec(du.shape, whole),
            columns,
            pl.BlockSpec(dy.shape, whole),
            pl.BlockSpec(o.shape, whole),
        ],
        out_specs=pl.BlockSpec(shape, lambda i: (0, 0, 0)),
        out_shape=jax.ShapeDtypeStruct(shape, BF16),
        **params(4 * rows * width * units, 14 * 2**20),
    )(n2, du, h, dy, o)


def qkv_grads_kernel(layout, n1_ref, da_ref, vec_ref, out_ref):
    step = pl.program_id(0)
    cols = da_ref.shape[1]
    grad = dot_tn(n1_ref[...], da_ref[...]).astype(BF16)
    for b in range(TILE // layout.r_w):
        part, row = layout.place(step * (TILE // layout.r_w) + b)
        out_ref[part, pl.ds(pl.multiple_of(row, 16), layout.r_w), :cols] = grad[b * layout.r_w : (b + 1) * layout.r_w]

    @pl.when(step == 0)
    def _():
        out_ref[:, :, cols:] = vec_ref[...]


def qkv_grads(layout, n1, da, vec):
    rows, width = n1.shape
    shape = (vec.shape[0], vec.shape[1], da.shape[1] + vec.shape[2])
    return pl.pallas_call(
        functools.partial(qkv_grads_kernel, layout),
        grid=(width // TILE,),
        in_specs=[
            pl.BlockSpec((rows, TILE), lambda i: (0, i)),
            pl.BlockSpec(da.shape, lambda i: (0, 0)),
            pl.BlockSpec(vec.shape, lambda i: (0, 0, 0)),
        ],
        out_specs=pl.BlockSpec(shape, lambda i: (0, 0, 0)),
        out_shape=jax.ShapeDtypeStruct(shape, BF16),
        **params(2 * rows * width * da.shape[1], 6 * 2**20),
    )(n1, da, vec)


def grad_att_kernel(heads, block, z_ref, dy_ref, wo_ref, *out_refs):
    grad = dot_nt(dy_ref[...], wo_ref[...])
    parts = [pair_up(grad[:, h * HEAD : (h + 1) * HEAD], block) for h in range(heads)]
    for ref, part in zip(out_refs, turn(z_ref[0], parts)):
        ref[...] = part.astype(BF16)


def grad_att(z, dy, wo, block):
    rows, width = dy.shape
    heads = wo.shape[0] // HEAD
    return pl.pallas_call(
        functools.partial(grad_att_kernel, heads, block),
        grid_spec=pltpu.PrefetchScalarGridSpec(
            num_scalar_prefetch=1,
            grid=(rows // TILE,),
            in_specs=[pl.BlockSpec((TILE, width), row_at), pl.BlockSpec(wo.shape, whole_at)],
            out_specs=[piece(TILE // 2)] * heads,
        ),
        out_shape=[bf16_rows(rows // 2)] * heads,
        **params(2 * rows * width * wo.shape[0], 4 * 2**20),
    )(z, dy, wo)


def split_parts(step, total, keep_refs, near_refs):
    low = total.astype(BF16)
    half = total.shape[1] // 2

    @pl.when(step % 2 == 0)
    def _():
        for at, ref in enumerate(keep_refs):
            ref[...] = low[:, at * half : (at + 1) * half]

    @pl.when(step % 2 == 1)
    def _():
        for at, ref in enumerate(near_refs):
            ref[...] = low[:, at * half : (at + 1) * half]


def half_tile(width):
    return pl.BlockSpec((TILE, width // 2), lambda i, z: (i // 2, 0))


def half_parts(rows, width):
    return jax.ShapeDtypeStruct((rows // 2, width // 2), BF16)


def project_kernel(heads, block, z_ref, y_ref, wo_ref, *refs):
    parts = turn(z_ref[0], [unpair(ref[...].astype(F32), block) for ref in refs[:heads]])
    o_ref = refs[heads]
    for h in range(0, heads, 2):
        o_ref[:, h * HEAD : (h + 2) * HEAD] = jnp.concatenate(parts[h : h + 2], axis=1).astype(BF16)
    total = y_ref[...] + dot(o_ref[...], wo_ref[...])
    split_parts(pl.program_id(0), total, refs[heads + 1 : heads + 3], refs[heads + 3 :])


def project(z, parts, y, wo, block):
    heads = len(parts)
    rows, width = y.shape
    tile = pl.BlockSpec((TILE, width), row_at)
    return pl.pallas_call(
        functools.partial(project_kernel, heads, block),
        grid_spec=pltpu.PrefetchScalarGridSpec(
            num_scalar_prefetch=1,
            grid=(rows // TILE,),
            in_specs=[tile, pl.BlockSpec(wo.shape, whole_at)] + [piece(TILE // 2)] * heads,
            out_specs=[pl.BlockSpec((TILE, heads * HEAD), row_at)] + [half_tile(width)] * 4,
        ),
        out_shape=[jax.ShapeDtypeStruct((rows, heads * HEAD), BF16)] + [half_parts(rows, width)] * 4,
        **params(2 * rows * width * wo.shape[0], 8 * 2**20),
    )(z, y, wo, *parts)


def post_kernel(
    heads, block, z_ref, x_ref, dx_ref, norm_ref, w_ref, cos_ref, sl_ref, sr_ref, *refs
):
    z = z_ref[0]
    dqk = turn(z, [ref[:TILE, :].astype(F32) for ref in refs[:heads]])
    dv = turn(z, [unpair(ref[TILE:, :].astype(F32), block) for ref in refs[:heads]])
    da_ref, sums_ref, db_ref = refs[heads : heads + 3]
    cos, sl, sr = cos_ref[...], sl_ref[...], sr_ref[...]
    cols = heads * HEAD
    for h in range(0, heads, 2):
        at = h * HEAD
        one = rotary(dqk[h], cos, sl, sr, -1.0)
        two = rotary(dqk[h + 1], cos, sl, sr, -1.0)
        da_ref[:, at : at + 2 * HEAD] = jnp.concatenate([one[:, :HEAD], two[:, :HEAD]], axis=1).astype(BF16)
        da_ref[:, cols + at : cols + at + 2 * HEAD] = jnp.concatenate([one[:, HEAD:], two[:, HEAD:]], axis=1).astype(BF16)
        da_ref[:, 2 * cols + at : 2 * cols + at + 2 * HEAD] = jnp.concatenate(dv[h : h + 2], axis=1).astype(BF16)
    grad = da_ref[...]
    grad_norm = dot_nt(grad, w_ref[...])
    total = dx_ref[...] + grad_norm * norm_ref[0:1]
    split_parts(pl.program_id(0), total, refs[heads + 3 : heads + 5], refs[heads + 5 :])
    gain = jnp.sum(grad_norm * normalized(x_ref), axis=0, keepdims=True)
    shift = jnp.sum(grad_norm, axis=0, keepdims=True)
    bias = jnp.sum(grad.astype(F32), axis=0, keepdims=True)

    @pl.when(pl.program_id(0) == 0)
    def _():
        sums_ref[...] = jnp.zeros_like(sums_ref)
        db_ref[...] = jnp.zeros_like(db_ref)

    sums_ref[0:1] += gain
    sums_ref[1:2] += shift
    db_ref[0:1] += bias


def post(z, grads, x, dx, norms, w, cos, sl, sr, block):
    heads = len(grads)
    rows, width = x.shape
    three = heads * 3 * HEAD
    table = pl.BlockSpec((TILE, 2 * HEAD), row_at)
    tile = pl.BlockSpec((TILE, width), row_at)
    return pl.pallas_call(
        functools.partial(post_kernel, heads, block),
        grid_spec=pltpu.PrefetchScalarGridSpec(
            num_scalar_prefetch=1,
            grid=(rows // TILE,),
            in_specs=[
                tile,
                tile,
                pl.BlockSpec(norms.shape, whole_at),
                pl.BlockSpec(w.shape, whole_at),
                table,
                table,
                table,
            ]
            + [piece(JOINT)] * heads,
            out_specs=[
                pl.BlockSpec((TILE, three), row_at),
                pl.BlockSpec((8, width), whole_at),
                pl.BlockSpec((8, three), whole_at),
            ]
            + [half_tile(width)] * 4,
        ),
        out_shape=[
            jax.ShapeDtypeStruct((rows, three), BF16),
            jax.ShapeDtypeStruct((8, width), F32),
            jax.ShapeDtypeStruct((8, three), F32),
        ]
        + [half_parts(rows, width)] * 4,
        **params(2 * rows * width * three, 14 * 2**20),
    )(z, x, dx, norms, w, cos, sl, sr, *grads)


def doc_start(packed, ends_ref, count):
    start = packed * 0
    for d in range(count):
        start = jnp.where(packed >= ends_ref[d], ends_ref[d], start)
    return start


def doc_end(packed, ends_ref, count):
    end = ends_ref[count - 1]
    for d in range(count - 2, -1, -1):
        end = jnp.where(packed < ends_ref[d], ends_ref[d], end)
    return end


def tile_at(i, size=TILE):
    return pl.ds(pl.multiple_of(i * size, size), size)


def load_half(ref, source, block):
    both = ref[pl.ds(pl.multiple_of((source // 2) * block, block), block), :].astype(F32)
    return jnp.where(source % 2 == 0, both[:, :HEAD], both[:, HEAD:])


def scores(masked, k_s, q_t, ends_ref, count, i, j, q_size, k_size):
    s = dot(k_s[tile_at(j, k_size), :], q_t[:HEAD, tile_at(i, q_size)])
    if not masked:
        return s
    key_at = lax.broadcasted_iota(jnp.int32, (k_size, q_size), 0)
    query_at = lax.broadcasted_iota(jnp.int32, (k_size, q_size), 1)
    query_row = i * q_size + lax.broadcasted_iota(jnp.int32, (1, q_size), 1)
    first = doc_start(query_row, ends_ref, count) - j * k_size
    last = i * q_size - j * k_size + query_at
    return jnp.where((key_at >= first) & (key_at <= last), s, NEG)


def lay_out(pieces, whole):
    size = pieces[0].shape[0]
    for i, ref in enumerate(pieces):
        whole[i * size : (i + 1) * size, :] = ref[...]


def lay_out_joint(pieces, qk, v):
    at = 0
    for ref in pieces:
        for i in range(0, ref.shape[0], JOINT):
            qk[at : at + TILE, :] = ref[i : i + TILE, :]
            v[at // 2 : (at + TILE) // 2, :] = ref[i + TILE : i + JOINT, :]
            at += TILE


def forward_kernel(block, count, source_ref, packed_ref, ends_ref, *refs):
    pieces = (len(refs) - 8) // 2
    qkv_in, o_out = refs[:pieces], refs[pieces : 2 * pieces]
    o_t, lse_ref, k_s, q_t, v_t, o_s, qk_ref, v_ref = refs[2 * pieces :]
    rows = qk_ref.shape[0]
    lay_out_joint(qkv_in, qk_ref, v_ref)
    tiles = rows // TILE
    per = TILE // block
    scale = HEAD ** (-0.5)

    def gather(i, carry):
        qk, v = [], []
        for b in range(per):
            src = source_ref[i * per + b]
            qk.append(qk_ref[pl.ds(pl.multiple_of(src * block, block), block), :].astype(F32))
            v.append(load_half(v_ref, src, block))
        qk, v = jnp.concatenate(qk, axis=0), jnp.concatenate(v, axis=0)
        k_s[tile_at(i), :] = qk[:, HEAD:].astype(BF16)
        q_t[:, tile_at(i)] = (qk.T[:HEAD] * scale).astype(BF16)
        v_t[:, tile_at(i)] = v.T.astype(BF16)
        return carry

    lax.fori_loop(0, tiles, gather, 0, unroll=4)

    def forward(i, carry):
        here = tile_at(i, FQ)

        def step(masked, j, state):
            top, total, acc = state
            s = scores(masked, k_s, q_t, ends_ref, count, i, j, FQ, FK)
            new_top = jnp.maximum(top, jnp.max(s, axis=0, keepdims=True))
            p = jnp.exp(s - new_top)
            fade = jnp.exp(top - new_top)
            total = total * fade + jnp.sum(p, axis=0, keepdims=True)
            acc = acc * fade + dot(v_t[:, tile_at(j, FK)], p.astype(BF16))
            return new_top, total, acc

        low = doc_start(i * FQ, ends_ref, count) // FK
        high = (i * FQ + FQ - 1) // FK + 1
        inner_low = (doc_start(i * FQ + FQ - 1, ends_ref, count) + FK - 1) // FK
        inner_high = jnp.maximum((i * FQ + 1) // FK, low)
        inner_low = jnp.clip(inner_low, low, inner_high)
        state = (jnp.full((1, FQ), NEG, F32), jnp.zeros((1, FQ), F32), jnp.zeros((HEAD, FQ), F32))
        state = lax.fori_loop(low, inner_low, functools.partial(step, True), state)
        state = lax.fori_loop(inner_low, inner_high, functools.partial(step, False), state)
        top, total, acc = lax.fori_loop(inner_high, high, functools.partial(step, True), state)
        out = acc / total
        lse_ref[:, here] = top + jnp.log(total)
        o_t[:, here] = out
        o_s[here, :] = out.T
        return carry

    lax.fori_loop(0, rows // FQ, forward, 0)

    send_pairs(o_s, o_out, packed_ref, block)


def load_pair(whole, row, packed_ref, block):
    both = [whole[pl.ds(pl.multiple_of(packed_ref[row + b] * block, block), block), :] for b in range(2)]
    return jnp.concatenate(both, axis=1).astype(BF16)


def send_pairs(whole, out_refs, packed_ref, block):
    per = out_refs[0].shape[0] // block
    for at, ref in enumerate(out_refs):

        def one(i, carry):
            ref[pl.ds(pl.multiple_of(i * block, block), block), :] = load_pair(whole, 2 * (at * per + i), packed_ref, block)
            return carry

        lax.fori_loop(0, per, one, 0, unroll=4)


def backward_kernel(block, count, source_ref, packed_ref, ends_ref, *refs):
    pieces = (len(refs) - 16) // 3
    qkv_in, do_in = refs[:pieces], refs[pieces : 2 * pieces]
    o_t, lse_ref = refs[2 * pieces : 2 * pieces + 2]
    grads_out = refs[2 * pieces + 2 : 3 * pieces + 2]
    q_s, k_s, v_s, do_s, qk_t, do_t, dq_t, delta_s, dk_s, dv_s, qk_ref, v_ref, do_ref, dqk_ref = refs[3 * pieces + 2 :]
    rows = qk_ref.shape[0]
    lay_out_joint(qkv_in, qk_ref, v_ref)
    lay_out(do_in, do_ref)
    tiles = rows // TILE
    per = TILE // block
    scale = HEAD ** (-0.5)

    def gather(i, carry):
        qk, v, do = [], [], []
        for b in range(per):
            src = source_ref[i * per + b]
            qk.append(qk_ref[pl.ds(pl.multiple_of(src * block, block), block), :].astype(F32))
            v.append(load_half(v_ref, src, block))
            do.append(load_half(do_ref, src, block))
        qk, v, do = jnp.concatenate(qk, axis=0), jnp.concatenate(v, axis=0), jnp.concatenate(do, axis=0)
        here = tile_at(i)
        q_s[here, :] = (qk[:, :HEAD] * scale).astype(BF16)
        k_s[here, :] = qk[:, HEAD:].astype(BF16)
        turned = qk.T
        qk_t[:HEAD, here] = (turned[:HEAD] * scale).astype(BF16)
        qk_t[HEAD:, here] = turned[HEAD:].astype(BF16)
        v_s[here, :] = v.astype(BF16)
        do_s[here, :] = do.astype(BF16)
        do_turned = do.T
        do_t[:, here] = do_turned.astype(BF16)
        dq_t[:, here] = jnp.zeros((HEAD, TILE), F32)
        delta_s[:, here] = jnp.sum(o_t[:, here] * do_turned, axis=0, keepdims=True)
        return carry

    lax.fori_loop(0, tiles, gather, 0, unroll=4)

    def backward(j, carry):
        keys = tile_at(j, BK)

        def step(masked, i, state):
            dk, dv = state
            here = tile_at(i, BQ)
            p = jnp.exp(scores(masked, k_s, qk_t, ends_ref, count, i, j, BQ, BK) - lse_ref[:, here])
            dp = dot(v_s[keys, :], do_t[:, here])
            ds = (p * (dp - delta_s[:, here])).astype(BF16)
            dv = dv + dot(p.astype(BF16), do_s[here, :])
            dk = dk + dot(ds, q_s[here, :])
            dq_t[:, here] += dot(qk_t[HEAD:, keys], ds)
            return dk, dv

        low = j * BK // BQ
        high = (doc_end(j * BK + BK - 1, ends_ref, count) - 1) // BQ + 1
        inner_low = jnp.minimum((j * BK + BK - 1 + BQ - 1) // BQ, high)
        inner_high = jnp.clip(doc_end(j * BK, ends_ref, count) // BQ, inner_low, high)
        zero = jnp.zeros((BK, HEAD), F32)
        state = lax.fori_loop(low, inner_low, functools.partial(step, True), (zero, zero))
        state = lax.fori_loop(inner_low, inner_high, functools.partial(step, False), state)
        dk, dv = lax.fori_loop(inner_high, high, functools.partial(step, True), state)
        dk_s[keys, :] = dk
        dv_s[keys, :] = dv
        return carry

    lax.fori_loop(0, rows // BK, backward, 0)

    def scatter(i, carry):
        here = tile_at(i)
        dq = (dq_t[:, here] * scale).T
        dqk = jnp.concatenate([dq, dk_s[here, :]], axis=1).astype(BF16)
        for b in range(per):
            dst = pl.ds(pl.multiple_of(source_ref[i * per + b] * block, block), block)
            dqk_ref[dst, :] = dqk[b * block : (b + 1) * block, :]
        return carry

    lax.fori_loop(0, tiles, scatter, 0, unroll=4)

    per_piece = rows // pieces // TILE
    for at, ref in enumerate(grads_out):

        def one(i, carry):
            start = at * per_piece + i
            out = pl.multiple_of(i * JOINT, JOINT)
            ref[pl.ds(out, TILE), :] = dqk_ref[tile_at(start), :]
            for b in range(0, per, 2):
                row = pl.multiple_of(out + TILE + b // 2 * block, block)
                ref[pl.ds(row, block), :] = load_pair(dv_s, start * per + b, packed_ref, block)
            return carry

        lax.fori_loop(0, per_piece, one, 0, unroll=2)


IN_VMEM = pl.BlockSpec(memory_space=pltpu.VMEM)
IN_SMEM = pl.BlockSpec(memory_space=pltpu.SMEM)


def attend_forward(source, packed, ends, qkv, block):
    pieces = len(qkv)
    rows = pieces * (qkv[0].shape[0] // JOINT * TILE)
    turned = pltpu.VMEM((HEAD, rows), BF16)
    return pl.pallas_call(
        functools.partial(forward_kernel, block, ends.shape[0]),
        in_specs=[IN_SMEM] * 3 + [IN_VMEM] * pieces,
        out_specs=[IN_VMEM] * (pieces + 2),
        out_shape=[bf16_rows(rows // (2 * pieces))] * pieces
        + [
            jax.ShapeDtypeStruct((HEAD, rows), F32),
            jax.ShapeDtypeStruct((1, rows), F32),
        ],
        scratch_shapes=[
            pltpu.VMEM((rows, HEAD), BF16),
            turned,
            turned,
            pltpu.VMEM((rows, HEAD), F32),
            pltpu.VMEM((rows, 2 * HEAD), BF16),
            pltpu.VMEM((rows // 2, 2 * HEAD), BF16),
        ],
        **params(rows * rows * HEAD * 40, 6 * rows * HEAD * 2, rows * rows),
    )(source, packed, ends, *qkv)


def attend_backward(source, packed, ends, qkv, do, o_t, lse, block):
    pieces = len(qkv)
    rows = pieces * (qkv[0].shape[0] // JOINT * TILE)
    half = pltpu.VMEM((rows, HEAD), BF16)
    wide = pltpu.VMEM((rows, HEAD), F32)
    pairs = pltpu.VMEM((rows // 2, 2 * HEAD), BF16)
    whole = pltpu.VMEM((rows, 2 * HEAD), BF16)
    return pl.pallas_call(
        functools.partial(backward_kernel, block, ends.shape[0]),
        in_specs=[IN_SMEM] * 3 + [IN_VMEM] * (2 * pieces + 2),
        out_specs=[IN_VMEM] * pieces,
        out_shape=[bf16_rows(qkv[0].shape[0])] * pieces,
        scratch_shapes=[
            half,
            half,
            half,
            half,
            pltpu.VMEM((2 * HEAD, rows), BF16),
            pltpu.VMEM((HEAD, rows), BF16),
            pltpu.VMEM((HEAD, rows), F32),
            pltpu.VMEM((1, rows), F32),
            wide,
            wide,
            whole,
            pairs,
            pairs,
            whole,
        ],
        **params(rows * rows * HEAD * 40, 12 * rows * HEAD * 2, rows * rows),
    )(source, packed, ends, *qkv, *do, o_t, lse)


def join_in(value, far, near):
    return jnp.concatenate([value, near[0], far, near[1]])


def near_in(near):
    return xor_swap(near, "in", GROUP_IN, 1)


def far_in(keep, near):
    size = keep.shape[0] // 2
    return xor_swap((keep[size:].astype(F32) + near[size:].astype(F32)).astype(BF16), "in", GROUP_IN, 2)


def total(keep, near, far):
    size = far[0].shape[0]
    parts = [k[:size].astype(F32) + n[:size].astype(F32) + f.astype(F32) for k, n, f in zip(keep, near, far)]
    return jnp.concatenate(parts, axis=1)


def exchange_in(parts, t):
    here = [lax.dynamic_index_in_dim(parts, t ^ s, 0, keepdims=False) for s in range(GROUP_IN)]
    there = [here[0]] + [xor_swap(here[s], "in", GROUP_IN, s) for s in range(1, GROUP_IN)]
    stacked = jnp.stack(there)
    return jnp.stack([lax.dynamic_index_in_dim(stacked, t ^ u, 0, keepdims=False) for u in range(GROUP_IN)])


def exchange_out(parts):
    size = len(parts)
    return [parts[0]] + [xor_swap(parts[s], "out", size, s) for s in range(1, size)]


def body(
    tokens,
    seq_lengths,
    dealing,
    ln1_gain,
    ln1_bias,
    ln2_gain,
    ln2_bias,
    w_qkv,
    b_qkv,
    w_out,
    w_in,
    b_in,
    w_fc2,
    b_out,
    cotangent,
):
    n_dp, n_out, n_in = lax.axis_size("dp"), lax.axis_size("out"), lax.axis_size("in")
    n_g = n_dp * n_out
    n_all = n_g * n_in
    rows_dev, width = tokens.shape
    ff = w_in.shape[1]
    ff_in = ff // n_in
    r_w = w_in.shape[0]
    r_ff = w_fc2.shape[0]
    block = LONGEST // (2 * n_out * n_in)
    slots_dev = rows_dev // block
    heads = width // HEAD
    h_in = heads // n_in
    cols = h_in * HEAD
    rows = rows_dev * n_in
    layout = Rows(n_dp, n_in, n_out, r_w)
    z, t = lax.axis_index("out"), lax.axis_index("in")
    z_arr = z[None].astype(jnp.int32)
    lengths, order = seq_lengths[0], dealing[0]
    ends = jnp.cumsum(lengths)

    slots = order.shape[0]
    ids = jnp.arange(slots, dtype=jnp.int32)
    slot_of = jnp.sum(jnp.where(order[None, :] == ids[:, None], ids[None, :], 0), axis=1)
    chunk = slot_of // slots_dev
    source = (((chunk % n_out) ^ z) * n_in + ((chunk // n_out) ^ t)) * slots_dev + slot_of % slots_dev
    source = source.astype(jnp.int32)
    lies = ids // slots_dev
    slot_here = (((lies % n_in) ^ t) * n_out + ((lies // n_in) ^ z)) * slots_dev + ids % slots_dev
    packed_of = jnp.sum(jnp.where(slot_here[:, None] == ids[None, :], order[None, :], 0), axis=1).astype(jnp.int32)

    part = jnp.arange(rows, dtype=jnp.int32)
    packed = packed_of[: rows // block].reshape(-1, 1) * block + jnp.arange(block, dtype=jnp.int32)[None, :]
    packed = packed.reshape(rows)
    starts = jnp.max(jnp.where(packed[:, None] >= ends[None, :], ends[None, :], 0), axis=1)
    position = (packed - starts).astype(F32)
    vectors = [ln1_gain, ln1_bias, ln2_gain, ln2_bias, b_qkv, b_out, b_in]
    sizes = [v.shape[0] for v in vectors]
    per_row = -(-len(vectors) // r_w)
    lanes = 128 // per_row
    qkv_cols = jnp.transpose(w_qkv.reshape(r_w, 3, n_in, cols), (2, 0, 1, 3)).reshape(n_in, r_w, 3 * cols)
    in_cols = jnp.transpose(w_in.reshape(r_w, n_dp, n_in, n_out, r_ff), (2, 0, 1, 3, 4)).reshape(n_in, r_w, ff_in)
    vec = jnp.stack([jnp.pad(v, (0, lanes - v.shape[0])) for v in vectors])
    vec = jnp.pad(vec, ((0, r_w * per_row - len(vectors)), (0, 0))).reshape(r_w, 128)
    vec = jnp.broadcast_to(vec[None], (n_in, r_w, 128))
    joined_cols = exchange_in(jnp.concatenate([qkv_cols, vec, in_cols], axis=2), t).reshape(n_in * r_w, -1)
    home = []
    for b in range(n_all):
        t_to, g_to = b // n_g, b % n_g
        home.append((b, ((g_to // n_out) * n_in + t_to) * n_out + g_to % n_out))
    out_rows = lax.ppermute(w_out, ALL_AXES, home).reshape(n_in * r_w, cols)
    first = jnp.concatenate([joined_cols[:, : 3 * cols + 128], out_rows], axis=1)
    first, to_send = lax.optimization_barrier((first, tokens))
    x_far = xor_swap(to_send, "in", n_in, 2)
    first, position = lax.optimization_barrier((lax.all_gather(first, G_AXES, axis=0, tiled=False), position))
    second = jnp.concatenate([joined_cols[:, 3 * cols + 128 :], w_fc2], axis=1)
    second = lax.all_gather(second, G_AXES, axis=0, tiled=False)

    def natural(value):
        value = value.reshape(n_dp, n_out, n_in, r_w, -1)
        return jnp.transpose(value, (0, 2, 1, 3, 4)).reshape(n_all * r_w, -1)

    def by_owner(value):
        value = value.reshape(n_dp, n_in, n_out, r_w, -1)
        return jnp.transpose(value, (0, 2, 1, 3, 4)).reshape(n_g, n_in * r_w, -1)

    weight_qkv = natural(first[:, :, : 3 * cols])
    weight_out = first[:, :, 3 * cols + 128 :].reshape(cols, width)
    if not layout.aligned:
        in_rows = natural(second[:, :, :ff_in]).reshape(n_g, n_in * r_w, ff_in)
        second = jnp.concatenate([in_rows, second[:, :, ff_in:]], axis=2)
    vec_all = first[:, :, 3 * cols : 3 * cols + 128].reshape(n_dp, n_out, n_in, r_w * per_row, lanes)
    vec_all = jnp.transpose(vec_all[:, :, :, : len(vectors)], (3, 0, 2, 1, 4)).astype(F32)
    spans = [vec_all[i, ..., :size] for i, size in enumerate(sizes)]
    gain_one, shift_one, gain_two, shift_two = [s.reshape(width) for s in spans[:4]]
    bias_out = spans[5].reshape(width)
    bias_in = lax.dynamic_index_in_dim(spans[6], t, 1, keepdims=False).reshape(ff_in)
    bias_qkv = lax.dynamic_index_in_dim(spans[4].reshape(3, n_in, cols), t, 1, keepdims=False).reshape(-1)
    norms = jnp.concatenate([jnp.stack([gain_one, shift_one, gain_two, shift_two]), jnp.zeros((4, width), F32)])

    lane = jnp.arange(2 * HEAD, dtype=jnp.int32) % HEAD
    half = ROT // 2
    freq = 10000.0 ** (-2.0 * (lane % half).astype(F32) / ROT)
    phase = position[:, None] * freq[None, :]
    cos = jnp.where(lane < ROT, jnp.cos(phase), 1.0)
    sine = jnp.sin(phase)
    sin_l = jnp.where(lane < half, sine, 0.0)
    sin_r = jnp.where((lane >= half) & (lane < ROT), sine, 0.0)

    x_near = xor_swap(jnp.stack([tokens, x_far]), "in", n_in, 1)
    x_near, weight_qkv, norms, bias_qkv, cos, sin_l, sin_r = lax.optimization_barrier(
        (x_near, weight_qkv, norms, bias_qkv, cos, sin_l, sin_r)
    )
    x_all = join_in(tokens, x_far, x_near)
    x_all, to_send = lax.optimization_barrier((x_all, cotangent))
    dy_far = xor_swap(to_send, "in", n_in, 2)

    n1, n2, *qkv = prep(z_arr, x_all, norms, weight_qkv, bias_qkv[None], cos, sin_l, sin_r, block)
    qkv = exchange_out(qkv)
    qkv, dy_far = lax.optimization_barrier((qkv, dy_far))
    dy_near = xor_swap(jnp.stack([cotangent, dy_far]), "in", n_in, 1)
    *o, o_t, lse = attend_forward(source, packed_of, ends, qkv, block)
    o, dy_near = lax.optimization_barrier((o, dy_near))
    dy_all = join_in(cotangent, dy_far, dy_near)
    o = exchange_out(o)
    do = exchange_out(grad_att(z_arr, dy_all, weight_out, block))

    hidden, grad_up, y_ff, dx_ff, sums_two, grad_b_in = feed(
        layout, x_all, n2, dy_all, norms, second, bias_in[None]
    )
    o, y_ff = lax.optimization_barrier((o, y_ff))
    o, *y_parts = project(z_arr, o, y_ff, weight_out, block)
    if layout.aligned:
        second_grads = feed_grads(layout, n2, grad_up, hidden, dy_all, o)
    else:
        second_grads = jnp.concatenate(
            [
                by_owner(dot_tn(n2, grad_up).astype(BF16)),
                dot_tn(hidden, dy_all).astype(BF16).reshape(n_g, r_ff, width),
                dot_tn(o, dy_all).astype(BF16).reshape(n_g, r_w, width),
            ],
            axis=1,
        )

    do, second_grads, y_parts = lax.optimization_barrier((do, second_grads, y_parts))
    second_grads = lax.psum_scatter(second_grads, G_AXES, scatter_dimension=0, tiled=False)
    y_keep, y_near = y_parts[:2], [near_in(p) for p in y_parts[2:]]
    own = tokens.astype(F32)
    parts = attend_backward(source, packed_of, ends, qkv, do, o_t, lse, block)
    parts, y_near = lax.optimization_barrier((parts, y_near))
    parts = exchange_out(parts)
    y_far = [far_in(k, n) for k, n in zip(y_keep, y_near)]
    parts, y_far = lax.optimization_barrier((parts, y_far))
    da, sums_one, grad_b_qkv, *w_parts = post(
        z_arr, parts, x_all, dx_ff, norms, weight_qkv, cos, sin_l, sin_r, block
    )
    w_parts, da, second_grads = lax.optimization_barrier((w_parts, da, second_grads))
    w_keep, w_near = w_parts[:2], [near_in(w_parts[2])]
    w_near[0], w_next, tokens, y_far = lax.optimization_barrier((w_near[0], w_parts[3], tokens, y_far))
    own = tokens.astype(F32)
    mixed = (own + total(y_keep, y_near, y_far) + bias_out).astype(BF16)
    w_near.append(near_in(w_next))
    w_far = [far_in(w_keep[0], w_near[0])]
    w_near[1], second_grads = lax.optimization_barrier((w_near[1], second_grads))
    w_far.append(far_in(w_keep[1], w_near[1]))
    w_sum = total(w_keep, w_near, w_far)

    def placed(vector, axis):
        spread = jnp.expand_dims(vector, axis)
        mask = (jnp.arange(n_in) == t).reshape([-1 if a == axis else 1 for a in range(spread.ndim)])
        return jnp.where(mask, spread, 0.0).reshape(-1)

    grad_own = cotangent.astype(F32)
    vec_grads = [
        sums_one[0],
        sums_one[1],
        sums_two[0],
        sums_two[1],
        placed(grad_b_qkv[0].reshape(3, cols), 1),
        jnp.sum(grad_own, axis=0),
        placed(grad_b_in[0].reshape(n_dp, n_out, r_ff), 1),
    ]
    vec_grads = [v.astype(BF16).reshape(n_dp, n_in, n_out, -1) for v in vec_grads]
    vec_grads = jnp.stack([jnp.pad(v, ((0, 0), (0, 0), (0, 0), (0, lanes - v.shape[-1]))) for v in vec_grads], axis=3)
    spare = r_w * per_row - len(vectors)
    vec_grads = jnp.pad(vec_grads, ((0, 0), (0, 0), (0, 0), (0, spare), (0, 0)))
    vec_grads = jnp.transpose(vec_grads, (0, 2, 1, 3, 4)).reshape(n_g, n_in * r_w, 128)
    if layout.aligned:
        first_grads = qkv_grads(layout, n1, da, vec_grads)
    else:
        first_grads = jnp.concatenate([by_owner(dot_tn(n1, da).astype(BF16)), vec_grads], axis=2)
    first_grads = lax.psum_scatter(first_grads, G_AXES, scatter_dimension=0, tiled=False)

    last = [first_grads.reshape(n_in, r_w, -1), second_grads[: n_in * r_w].reshape(n_in, r_w, ff_in)]
    last = exchange_in(jnp.concatenate(last, axis=2), t)
    qkv_part, in_part = last[:, :, : 3 * cols + 128], last[:, :, 3 * cols + 128 :]
    in_part = in_part.reshape(n_in, r_w, n_dp, n_out, r_ff)
    grad_w_in = jnp.transpose(in_part, (1, 2, 0, 3, 4)).reshape(r_w, ff).astype(F32)
    grad_w_fc2 = second_grads[n_in * r_w : n_in * r_w + r_ff].astype(F32)
    back_home = [(b, a) for a, b in home]
    out_part = second_grads[n_in * r_w + r_ff :]
    grad_w_out = lax.ppermute(out_part, ALL_AXES, back_home).astype(F32)
    qkv_grad = jnp.transpose(qkv_part[:, :, : 3 * cols].reshape(n_in, r_w, 3, cols), (1, 2, 0, 3))
    grad_w_qkv = qkv_grad.reshape(r_w, 3 * width).astype(F32)
    vec_part = jnp.sum(qkv_part[:, :, 3 * cols :].astype(F32), axis=0).reshape(r_w * per_row, lanes)
    vec_out = [vec_part[i, :size] for i, size in enumerate(sizes)]

    centred = own - jnp.mean(own, axis=-1, keepdims=True)
    own_rstd = lax.rsqrt(jnp.mean(centred * centred, axis=-1, keepdims=True) + EPS)
    own_hat = centred * own_rstd
    mean_w = jnp.mean(w_sum, axis=-1, keepdims=True)
    mean_wx = jnp.mean(w_sum * own_hat, axis=-1, keepdims=True)
    grad_tokens = grad_own + own_rstd * (w_sum - mean_w - own_hat * mean_wx)
    return (
        mixed,
        grad_tokens,
        vec_out[0],
        vec_out[1],
        vec_out[2],
        vec_out[3],
        grad_w_qkv,
        vec_out[4],
        grad_w_out,
        grad_w_in,
        vec_out[6],
        grad_w_fc2,
        vec_out[5],
    )


def solution(mesh):
    n_dp, n_ctx = mesh.shape["dp"], mesh.shape["ctx"]
    split = Mesh(mesh.devices.reshape(n_dp, GROUP_IN, n_ctx // GROUP_IN), ALL_AXES)
    mat, vec, group = P(ALL_AXES, None), P(ALL_AXES), P("dp", None)
    return jax.shard_map(
        body,
        mesh=split,
        in_specs=(mat, group, group, vec, vec, vec, vec, mat, vec, mat, mat, vec, mat, vec, mat),
        out_specs=(mat, mat, vec, vec, vec, vec, mat, vec, mat, mat, vec, mat, vec),
        check_vma=False,
    )
```

```python
import functools

import jax
import jax.numpy as jnp
from jax import lax
from jax.experimental import pallas as pl
from jax.experimental.pallas import tpu as pltpu
from jax.sharding import Mesh
from jax.sharding import PartitionSpec as P

HEAD = 64
ROT = 16
LONGEST = 2048
GROUP_IN = 4
TILE = 256
JOINT = TILE + TILE // 2
FQ, FK = 512, 512
BQ, BK = 512, 256
EPS = 1e-05
NEG = -1e30
F32 = jnp.float32
BF16 = jnp.bfloat16
G_AXES = ("dp", "out")
ALL_AXES = ("dp", "in", "out")


def dot(a, b):
    return jnp.dot(a, b, preferred_element_type=F32)


def dot_nt(a, b):
    return lax.dot_general(a, b, (((1,), (1,)), ((), ())), preferred_element_type=F32)


def dot_tn(a, b):
    return lax.dot_general(a, b, (((0,), (0,)), ((), ())), preferred_element_type=F32)


def xor_swap(value, axis, size, step):
    return lax.ppermute(value, axis, [(i, i ^ step) for i in range(size)])


def rotary(x, cos, sin_l, sin_r, sign):
    left = pltpu.roll(x, 128 - ROT // 2, 1)
    right = pltpu.roll(x, ROT // 2, 1)
    return x * cos - sign * (left * sin_l) + sign * (right * sin_r)


def pair_up(x, block):
    blocks = [x[i : i + block] for i in range(0, x.shape[0], block)]
    return jnp.concatenate([jnp.concatenate(blocks[i : i + 2], axis=1) for i in range(0, len(blocks), 2)], axis=0)


def unpair(x, block):
    parts = []
    for i in range(0, x.shape[0], block):
        parts += [x[i : i + block, :HEAD], x[i : i + block, HEAD:]]
    return jnp.concatenate(parts, axis=0)


def params(flops, size, exps=0):
    return dict(
        compiler_params=pltpu.CompilerParams(vmem_limit_bytes=60 * 2**20),
        cost_estimate=pl.CostEstimate(flops=flops, bytes_accessed=size, transcendentals=exps),
    )


def row_at(i, z):
    return (i, 0)


def whole_at(i, z):
    return (0, 0)


def piece(size):
    return pl.BlockSpec((size, 2 * HEAD), row_at)


def bf16_rows(rows):
    return jax.ShapeDtypeStruct((rows, 2 * HEAD), BF16)


def normalized(x_ref):
    x = x_ref[...].astype(F32)
    centred = x - jnp.mean(x, axis=-1, keepdims=True)
    return centred * lax.rsqrt(jnp.mean(centred * centred, axis=-1, keepdims=True) + EPS)


def turn(z, parts):
    out = []
    for step in range(len(parts)):
        pick = parts[step]
        for at in range(1, len(parts)):
            pick = jnp.where(z == at, parts[at ^ step], pick)
        out.append(pick)
    return out


def prep_kernel(heads, block, z_ref, x_ref, norm_ref, w_ref, b_ref, cos_ref, sl_ref, sr_ref, n1_ref, n2_ref, *out_refs):
    z = z_ref[0]
    xhat = normalized(x_ref)
    n1 = (xhat * norm_ref[0:1] + norm_ref[1:2]).astype(BF16)
    n1_ref[...] = n1
    n2_ref[...] = (xhat * norm_ref[2:3] + norm_ref[3:4]).astype(BF16)
    joined = dot(n1, w_ref[...]) + b_ref[...]
    cos, sl, sr = cos_ref[...], sl_ref[...], sr_ref[...]
    cols = heads * HEAD
    qk, v = [], []
    for h in range(heads):
        at = h * HEAD
        part = jnp.concatenate([joined[:, at : at + HEAD], joined[:, cols + at : cols + at + HEAD]], axis=1)
        qk.append(rotary(part, cos, sl, sr, 1.0))
        v.append(pair_up(joined[:, 2 * cols + at : 2 * cols + at + HEAD], block))
    for ref, one, two in zip(out_refs, turn(z, qk), turn(z, v)):
        ref[:TILE, :] = one.astype(BF16)
        ref[TILE:, :] = two.astype(BF16)


def prep(z, x, norms, w, bias, cos, sl, sr, block):
    rows, width = x.shape
    heads = w.shape[1] // (3 * HEAD)
    table = pl.BlockSpec((TILE, 2 * HEAD), row_at)
    tile = pl.BlockSpec((TILE, width), row_at)
    norm = jax.ShapeDtypeStruct((rows, width), BF16)
    return pl.pallas_call(
        functools.partial(prep_kernel, heads, block),
        grid_spec=pltpu.PrefetchScalarGridSpec(
            num_scalar_prefetch=1,
            grid=(rows // TILE,),
            in_specs=[
                tile,
                pl.BlockSpec(norms.shape, whole_at),
                pl.BlockSpec(w.shape, whole_at),
                pl.BlockSpec(bias.shape, whole_at),
                table,
                table,
                table,
            ],
            out_specs=[tile, tile] + [piece(JOINT)] * heads,
        ),
        out_shape=[norm, norm] + [bf16_rows(rows // TILE * JOINT)] * heads,
        **params(2 * rows * width * w.shape[1], 12 * 2**20),
    )(z, x, norms, w, bias, cos, sl, sr)


class Rows:
    def __init__(self, n_dp, n_in, n_out, r_w):
        self.n_in, self.n_out, self.r_w = n_in, n_out, r_w
        self.count = n_dp * n_in * n_out
        self.aligned = r_w % 16 == 0

    def place(self, block):
        out = block % self.n_out
        unit = (block // self.n_out) % self.n_in
        return block // (self.n_out * self.n_in) * self.n_out + out, unit * self.r_w


def feed_kernel(
    layout, x_ref, n2_ref, dy_ref, norm_ref, w_ref, b_ref, h_ref, du_ref, y_ref, dx_ref, sums_ref, db_ref, w_in_ref, w_fc2_ref
):
    units = w_in_ref.shape[1]

    @pl.when(pl.program_id(0) == 0)
    def _():
        size = w_ref.shape[1]
        for part in range(w_ref.shape[0]):
            w_fc2_ref[part * size : (part + 1) * size, :] = w_ref[part, :, units:]
            if not layout.aligned:
                w_in_ref[part * size : (part + 1) * size, :] = w_ref[part, :, :units]
        if layout.aligned:
            for at in range(layout.count):
                part, row = layout.place(at)
                w_in_ref[at * layout.r_w : (at + 1) * layout.r_w, :] = w_ref[part, row : row + layout.r_w, :units]

    up = dot(n2_ref[...], w_in_ref[...]) + b_ref[...]
    cdf = 0.5 + 0.5 * lax.erf(up * (0.5**0.5))
    hidden = (up * cdf).astype(BF16)
    slope = cdf + up * (jnp.exp(-0.5 * up * up) * 0.3989422804014327)
    grad_up = (dot_nt(dy_ref[...], w_fc2_ref[...]) * slope).astype(BF16)
    h_ref[...] = hidden
    du_ref[...] = grad_up
    y_ref[...] = dot(hidden, w_fc2_ref[...])
    grad_norm = dot_nt(grad_up, w_in_ref[...])
    dx_ref[...] = grad_norm * norm_ref[2:3]
    gain = jnp.sum(grad_norm * normalized(x_ref), axis=0, keepdims=True)
    shift = jnp.sum(grad_norm, axis=0, keepdims=True)
    bias = jnp.sum(grad_up.astype(F32), axis=0, keepdims=True)

    @pl.when(pl.program_id(0) == 0)
    def _():
        sums_ref[...] = jnp.zeros_like(sums_ref)
        db_ref[...] = jnp.zeros_like(db_ref)

    sums_ref[0:1] += gain
    sums_ref[1:2] += shift
    db_ref[0:1] += bias


def feed(layout, x, n2, dy, norms, w, bias):
    rows, width = x.shape
    units = bias.shape[1]
    row, whole = lambda i: (i, 0), lambda i: (0, 0)
    tile, tile_ff = pl.BlockSpec((TILE, width), row), pl.BlockSpec((TILE, units), row)
    return pl.pallas_call(
        functools.partial(feed_kernel, layout),
        grid=(rows // TILE,),
        in_specs=[
            tile,
            tile,
            tile,
            pl.BlockSpec(norms.shape, whole),
            pl.BlockSpec(w.shape, lambda i: (0, 0, 0)),
            pl.BlockSpec(bias.shape, whole),
        ],
        out_specs=[
            tile_ff,
            tile_ff,
            tile,
            tile,
            pl.BlockSpec((8, width), whole),
            pl.BlockSpec((8, units), whole),
        ],
        out_shape=[
            jax.ShapeDtypeStruct((rows, units), BF16),
            jax.ShapeDtypeStruct((rows, units), BF16),
            jax.ShapeDtypeStruct((rows, width), F32),
            jax.ShapeDtypeStruct((rows, width), F32),
            jax.ShapeDtypeStruct((8, width), F32),
            jax.ShapeDtypeStruct((8, units), F32),
        ],
        scratch_shapes=[pltpu.VMEM((width, units), BF16), pltpu.VMEM((units, width), BF16)],
        **params(8 * rows * width * units, 24 * 2**20, 2 * rows * units),
    )(x, n2, dy, norms, w, bias)


def feed_grads_kernel(layout, n2_ref, du_ref, h_ref, dy_ref, o_ref, out_ref):
    step = pl.program_id(0)
    size = out_ref.shape[1] // 9 * 4
    grad = dot_tn(n2_ref[...], du_ref[...]).astype(BF16)
    for b in range(TILE // layout.r_w):
        part, row = layout.place(step * (TILE // layout.r_w) + b)
        out_ref[part, pl.ds(pl.multiple_of(row, 16), layout.r_w), :] = grad[b * layout.r_w : (b + 1) * layout.r_w]
    grad = dot_tn(h_ref[...], dy_ref[...]).astype(BF16)
    for b in range(TILE // size):
        out_ref[step * (TILE // size) + b, size : 2 * size, :] = grad[b * size : (b + 1) * size]

    @pl.when(step == 0)
    def _():
        grad = dot_tn(o_ref[...], dy_ref[...]).astype(BF16)
        for part in range(out_ref.shape[0]):
            out_ref[part, 2 * size :, :] = grad[part * layout.r_w : (part + 1) * layout.r_w]


def feed_grads(layout, n2, du, h, dy, o):
    rows, width = n2.shape
    units = h.shape[1]
    parts = layout.count // layout.n_in
    shape = (parts, units // parts + layout.n_in * layout.r_w + layout.r_w, width)
    columns = pl.BlockSpec((rows, TILE), lambda i: (0, i))
    whole = lambda i: (0, 0)
    return pl.pallas_call(
        functools.partial(feed_grads_kernel, layout),
        grid=(width // TILE,),
        in_specs=[
            columns,
            pl.BlockSpec(du.shape, whole),
            columns,
            pl.BlockSpec(dy.shape, whole),
            pl.BlockSpec(o.shape, whole),
        ],
        out_specs=pl.BlockSpec(shape, lambda i: (0, 0, 0)),
        out_shape=jax.ShapeDtypeStruct(shape, BF16),
        **params(4 * rows * width * units, 14 * 2**20),
    )(n2, du, h, dy, o)


def qkv_grads_kernel(layout, n1_ref, da_ref, vec_ref, out_ref):
    step = pl.program_id(0)
    cols = da_ref.shape[1]
    grad = dot_tn(n1_ref[...], da_ref[...]).astype(BF16)
    for b in range(TILE // layout.r_w):
        part, row = layout.place(step * (TILE // layout.r_w) + b)
        out_ref[part, pl.ds(pl.multiple_of(row, 16), layout.r_w), :cols] = grad[b * layout.r_w : (b + 1) * layout.r_w]

    @pl.when(step == 0)
    def _():
        out_ref[:, :, cols:] = vec_ref[...]


def qkv_grads(layout, n1, da, vec):
    rows, width = n1.shape
    shape = (vec.shape[0], vec.shape[1], da.shape[1] + vec.shape[2])
    return pl.pallas_call(
        functools.partial(qkv_grads_kernel, layout),
        grid=(width // TILE,),
        in_specs=[
            pl.BlockSpec((rows, TILE), lambda i: (0, i)),
            pl.BlockSpec(da.shape, lambda i: (0, 0)),
            pl.BlockSpec(vec.shape, lambda i: (0, 0, 0)),
        ],
        out_specs=pl.BlockSpec(shape, lambda i: (0, 0, 0)),
        out_shape=jax.ShapeDtypeStruct(shape, BF16),
        **params(2 * rows * width * da.shape[1], 6 * 2**20),
    )(n1, da, vec)


def grad_att_kernel(heads, block, z_ref, dy_ref, wo_ref, *out_refs):
    grad = dot_nt(dy_ref[...], wo_ref[...])
    parts = [pair_up(grad[:, h * HEAD : (h + 1) * HEAD], block) for h in range(heads)]
    for ref, part in zip(out_refs, turn(z_ref[0], parts)):
        ref[...] = part.astype(BF16)


def grad_att(z, dy, wo, block):
    rows, width = dy.shape
    heads = wo.shape[0] // HEAD
    return pl.pallas_call(
        functools.partial(grad_att_kernel, heads, block),
        grid_spec=pltpu.PrefetchScalarGridSpec(
            num_scalar_prefetch=1,
            grid=(rows // TILE,),
            in_specs=[pl.BlockSpec((TILE, width), row_at), pl.BlockSpec(wo.shape, whole_at)],
            out_specs=[piece(TILE // 2)] * heads,
        ),
        out_shape=[bf16_rows(rows // 2)] * heads,
        **params(2 * rows * width * wo.shape[0], 4 * 2**20),
    )(z, dy, wo)


def split_parts(step, total, refs):
    low = total.astype(BF16)
    for at, ref in enumerate(refs):

        @pl.when(step == at)
        def _(ref=ref):
            ref[...] = low


def project_kernel(heads, block, z_ref, y_ref, wo_ref, *refs):
    parts = turn(z_ref[0], [unpair(ref[...].astype(F32), block) for ref in refs[:heads]])
    o_ref = refs[heads]
    for h in range(0, heads, 2):
        o_ref[:, h * HEAD : (h + 2) * HEAD] = jnp.concatenate(parts[h : h + 2], axis=1).astype(BF16)
    total = y_ref[...] + dot(o_ref[...], wo_ref[...])
    split_parts(pl.program_id(0), total, refs[heads + 1 :])


def project(z, parts, y, wo, block):
    heads = len(parts)
    rows, width = y.shape
    tile = pl.BlockSpec((TILE, width), row_at)
    return pl.pallas_call(
        functools.partial(project_kernel, heads, block),
        grid_spec=pltpu.PrefetchScalarGridSpec(
            num_scalar_prefetch=1,
            grid=(rows // TILE,),
            in_specs=[tile, pl.BlockSpec(wo.shape, whole_at)] + [piece(TILE // 2)] * heads,
            out_specs=[pl.BlockSpec((TILE, heads * HEAD), row_at)] + [pl.BlockSpec((TILE, width), whole_at)] * GROUP_IN,
        ),
        out_shape=[jax.ShapeDtypeStruct((rows, heads * HEAD), BF16)] + [jax.ShapeDtypeStruct((TILE, width), BF16)] * GROUP_IN,
        **params(2 * rows * width * wo.shape[0], 8 * 2**20),
    )(z, y, wo, *parts)


def post_kernel(
    heads, block, z_ref, x_ref, dx_ref, norm_ref, w_ref, cos_ref, sl_ref, sr_ref, *refs
):
    z = z_ref[0]
    dqk = turn(z, [ref[:TILE, :].astype(F32) for ref in refs[:heads]])
    dv = turn(z, [unpair(ref[TILE:, :].astype(F32), block) for ref in refs[:heads]])
    da_ref, sums_ref, db_ref = refs[heads : heads + 3]
    cos, sl, sr = cos_ref[...], sl_ref[...], sr_ref[...]
    cols = heads * HEAD
    for h in range(0, heads, 2):
        at = h * HEAD
        one = rotary(dqk[h], cos, sl, sr, -1.0)
        two = rotary(dqk[h + 1], cos, sl, sr, -1.0)
        da_ref[:, at : at + 2 * HEAD] = jnp.concatenate([one[:, :HEAD], two[:, :HEAD]], axis=1).astype(BF16)
        da_ref[:, cols + at : cols + at + 2 * HEAD] = jnp.concatenate([one[:, HEAD:], two[:, HEAD:]], axis=1).astype(BF16)
        da_ref[:, 2 * cols + at : 2 * cols + at + 2 * HEAD] = jnp.concatenate(dv[h : h + 2], axis=1).astype(BF16)
    grad = da_ref[...]
    grad_norm = dot_nt(grad, w_ref[...])
    total = dx_ref[...] + grad_norm * norm_ref[0:1]
    split_parts(pl.program_id(0), total, refs[heads + 3 :])
    gain = jnp.sum(grad_norm * normalized(x_ref), axis=0, keepdims=True)
    shift = jnp.sum(grad_norm, axis=0, keepdims=True)
    bias = jnp.sum(grad.astype(F32), axis=0, keepdims=True)

    @pl.when(pl.program_id(0) == 0)
    def _():
        sums_ref[...] = jnp.zeros_like(sums_ref)
        db_ref[...] = jnp.zeros_like(db_ref)

    sums_ref[0:1] += gain
    sums_ref[1:2] += shift
    db_ref[0:1] += bias


def post(z, grads, x, dx, norms, w, cos, sl, sr, block):
    heads = len(grads)
    rows, width = x.shape
    three = heads * 3 * HEAD
    table = pl.BlockSpec((TILE, 2 * HEAD), row_at)
    tile = pl.BlockSpec((TILE, width), row_at)
    return pl.pallas_call(
        functools.partial(post_kernel, heads, block),
        grid_spec=pltpu.PrefetchScalarGridSpec(
            num_scalar_prefetch=1,
            grid=(rows // TILE,),
            in_specs=[
                tile,
                tile,
                pl.BlockSpec(norms.shape, whole_at),
                pl.BlockSpec(w.shape, whole_at),
                table,
                table,
                table,
            ]
            + [piece(JOINT)] * heads,
            out_specs=[
                pl.BlockSpec((TILE, three), row_at),
                pl.BlockSpec((8, width), whole_at),
                pl.BlockSpec((8, three), whole_at),
            ]
            + [pl.BlockSpec((TILE, width), whole_at)] * GROUP_IN,
        ),
        out_shape=[
            jax.ShapeDtypeStruct((rows, three), BF16),
            jax.ShapeDtypeStruct((8, width), F32),
            jax.ShapeDtypeStruct((8, three), F32),
        ]
        + [jax.ShapeDtypeStruct((TILE, width), BF16)] * GROUP_IN,
        **params(2 * rows * width * three, 14 * 2**20),
    )(z, x, dx, norms, w, cos, sl, sr, *grads)


def doc_start(packed, ends_ref, count):
    start = packed * 0
    for d in range(count):
        start = jnp.where(packed >= ends_ref[d], ends_ref[d], start)
    return start


def doc_end(packed, ends_ref, count):
    end = ends_ref[count - 1]
    for d in range(count - 2, -1, -1):
        end = jnp.where(packed < ends_ref[d], ends_ref[d], end)
    return end


def tile_at(i, size=TILE):
    return pl.ds(pl.multiple_of(i * size, size), size)


def load_half(ref, source, block):
    both = ref[pl.ds(pl.multiple_of((source // 2) * block, block), block), :].astype(F32)
    return jnp.where(source % 2 == 0, both[:, :HEAD], both[:, HEAD:])


def scores(masked, k_s, q_t, ends_ref, count, i, j, q_size, k_size):
    s = dot(k_s[tile_at(j, k_size), :], q_t[:HEAD, tile_at(i, q_size)])
    if not masked:
        return s
    key_at = lax.broadcasted_iota(jnp.int32, (k_size, q_size), 0)
    query_at = lax.broadcasted_iota(jnp.int32, (k_size, q_size), 1)
    query_row = i * q_size + lax.broadcasted_iota(jnp.int32, (1, q_size), 1)
    first = doc_start(query_row, ends_ref, count) - j * k_size
    last = i * q_size - j * k_size + query_at
    return jnp.where((key_at >= first) & (key_at <= last), s, NEG)


def lay_out(pieces, whole):
    size = pieces[0].shape[0]
    for i, ref in enumerate(pieces):
        whole[i * size : (i + 1) * size, :] = ref[...]


def lay_out_joint(pieces, qk, v):
    at = 0
    for ref in pieces:
        for i in range(0, ref.shape[0], JOINT):
            qk[at : at + TILE, :] = ref[i : i + TILE, :]
            v[at // 2 : (at + TILE) // 2, :] = ref[i + TILE : i + JOINT, :]
            at += TILE


def forward_kernel(block, count, source_ref, packed_ref, ends_ref, *refs):
    pieces = (len(refs) - 8) // 2
    qkv_in, o_out = refs[:pieces], refs[pieces : 2 * pieces]
    o_t, lse_ref, k_s, q_t, v_t, o_s, qk_ref, v_ref = refs[2 * pieces :]
    rows = qk_ref.shape[0]
    lay_out_joint(qkv_in, qk_ref, v_ref)
    tiles = rows // TILE
    per = TILE // block
    scale = HEAD ** (-0.5)

    def gather(i, carry):
        qk, v = [], []
        for b in range(per):
            src = source_ref[i * per + b]
            qk.append(qk_ref[pl.ds(pl.multiple_of(src * block, block), block), :].astype(F32))
            v.append(load_half(v_ref, src, block))
        qk, v = jnp.concatenate(qk, axis=0), jnp.concatenate(v, axis=0)
        k_s[tile_at(i), :] = qk[:, HEAD:].astype(BF16)
        q_t[:, tile_at(i)] = (qk.T[:HEAD] * scale).astype(BF16)
        v_t[:, tile_at(i)] = v.T.astype(BF16)
        return carry

    lax.fori_loop(0, tiles, gather, 0, unroll=4)

    def forward(i, carry):
        here = tile_at(i, FQ)

        def step(masked, j, state):
            top, total, acc = state
            s = scores(masked, k_s, q_t, ends_ref, count, i, j, FQ, FK)
            new_top = jnp.maximum(top, jnp.max(s, axis=0, keepdims=True))
            p = jnp.exp(s - new_top)
            fade = jnp.exp(top - new_top)
            total = total * fade + jnp.sum(p, axis=0, keepdims=True)
            acc = acc * fade + dot(v_t[:, tile_at(j, FK)], p.astype(BF16))
            return new_top, total, acc

        low = doc_start(i * FQ, ends_ref, count) // FK
        high = (i * FQ + FQ - 1) // FK + 1
        inner_low = (doc_start(i * FQ + FQ - 1, ends_ref, count) + FK - 1) // FK
        inner_high = jnp.maximum((i * FQ + 1) // FK, low)
        inner_low = jnp.clip(inner_low, low, inner_high)
        state = (jnp.full((1, FQ), NEG, F32), jnp.zeros((1, FQ), F32), jnp.zeros((HEAD, FQ), F32))
        state = lax.fori_loop(low, inner_low, functools.partial(step, True), state)
        state = lax.fori_loop(inner_low, inner_high, functools.partial(step, False), state)
        top, total, acc = lax.fori_loop(inner_high, high, functools.partial(step, True), state)
        out = acc / total
        lse_ref[:, here] = top + jnp.log(total)
        o_t[:, here] = out
        o_s[here, :] = out.T
        return carry

    lax.fori_loop(0, rows // FQ, forward, 0)

    send_pairs(o_s, o_out, packed_ref, block)


def load_pair(whole, row, packed_ref, block):
    both = [whole[pl.ds(pl.multiple_of(packed_ref[row + b] * block, block), block), :] for b in range(2)]
    return jnp.concatenate(both, axis=1).astype(BF16)


def send_pairs(whole, out_refs, packed_ref, block):
    per = out_refs[0].shape[0] // block
    for at, ref in enumerate(out_refs):

        def one(i, carry):
            ref[pl.ds(pl.multiple_of(i * block, block), block), :] = load_pair(whole, 2 * (at * per + i), packed_ref, block)
            return carry

        lax.fori_loop(0, per, one, 0, unroll=4)


def backward_kernel(block, count, source_ref, packed_ref, ends_ref, *refs):
    pieces = (len(refs) - 16) // 3
    qkv_in, do_in = refs[:pieces], refs[pieces : 2 * pieces]
    o_t, lse_ref = refs[2 * pieces : 2 * pieces + 2]
    grads_out = refs[2 * pieces + 2 : 3 * pieces + 2]
    q_s, k_s, v_s, do_s, qk_t, do_t, dq_t, delta_s, dk_s, dv_s, qk_ref, v_ref, do_ref, dqk_ref = refs[3 * pieces + 2 :]
    rows = qk_ref.shape[0]
    lay_out_joint(qkv_in, qk_ref, v_ref)
    lay_out(do_in, do_ref)
    tiles = rows // TILE
    per = TILE // block
    scale = HEAD ** (-0.5)

    def gather(i, carry):
        qk, v, do = [], [], []
        for b in range(per):
            src = source_ref[i * per + b]
            qk.append(qk_ref[pl.ds(pl.multiple_of(src * block, block), block), :].astype(F32))
            v.append(load_half(v_ref, src, block))
            do.append(load_half(do_ref, src, block))
        qk, v, do = jnp.concatenate(qk, axis=0), jnp.concatenate(v, axis=0), jnp.concatenate(do, axis=0)
        here = tile_at(i)
        q_s[here, :] = (qk[:, :HEAD] * scale).astype(BF16)
        k_s[here, :] = qk[:, HEAD:].astype(BF16)
        turned = qk.T
        qk_t[:HEAD, here] = (turned[:HEAD] * scale).astype(BF16)
        qk_t[HEAD:, here] = turned[HEAD:].astype(BF16)
        v_s[here, :] = v.astype(BF16)
        do_s[here, :] = do.astype(BF16)
        do_turned = do.T
        do_t[:, here] = do_turned.astype(BF16)
        dq_t[:, here] = jnp.zeros((HEAD, TILE), F32)
        delta_s[:, here] = jnp.sum(o_t[:, here] * do_turned, axis=0, keepdims=True)
        return carry

    lax.fori_loop(0, tiles, gather, 0, unroll=4)

    def backward(j, carry):
        keys = tile_at(j, BK)

        def step(masked, i, state):
            dk, dv = state
            here = tile_at(i, BQ)
            p = jnp.exp(scores(masked, k_s, qk_t, ends_ref, count, i, j, BQ, BK) - lse_ref[:, here])
            dp = dot(v_s[keys, :], do_t[:, here])
            ds = (p * (dp - delta_s[:, here])).astype(BF16)
            dv = dv + dot(p.astype(BF16), do_s[here, :])
            dk = dk + dot(ds, q_s[here, :])
            dq_t[:, here] += dot(qk_t[HEAD:, keys], ds)
            return dk, dv

        low = j * BK // BQ
        high = (doc_end(j * BK + BK - 1, ends_ref, count) - 1) // BQ + 1
        inner_low = jnp.minimum((j * BK + BK - 1 + BQ - 1) // BQ, high)
        inner_high = jnp.clip(doc_end(j * BK, ends_ref, count) // BQ, inner_low, high)
        zero = jnp.zeros((BK, HEAD), F32)
        state = lax.fori_loop(low, inner_low, functools.partial(step, True), (zero, zero))
        state = lax.fori_loop(inner_low, inner_high, functools.partial(step, False), state)
        dk, dv = lax.fori_loop(inner_high, high, functools.partial(step, True), state)
        dk_s[keys, :] = dk
        dv_s[keys, :] = dv
        return carry

    lax.fori_loop(0, rows // BK, backward, 0)

    def scatter(i, carry):
        here = tile_at(i)
        dq = (dq_t[:, here] * scale).T
        dqk = jnp.concatenate([dq, dk_s[here, :]], axis=1).astype(BF16)
        for b in range(per):
            dst = pl.ds(pl.multiple_of(source_ref[i * per + b] * block, block), block)
            dqk_ref[dst, :] = dqk[b * block : (b + 1) * block, :]
        return carry

    lax.fori_loop(0, tiles, scatter, 0, unroll=4)

    per_piece = rows // pieces // TILE
    for at, ref in enumerate(grads_out):

        def one(i, carry):
            start = at * per_piece + i
            out = pl.multiple_of(i * JOINT, JOINT)
            ref[pl.ds(out, TILE), :] = dqk_ref[tile_at(start), :]
            for b in range(0, per, 2):
                row = pl.multiple_of(out + TILE + b // 2 * block, block)
                ref[pl.ds(row, block), :] = load_pair(dv_s, start * per + b, packed_ref, block)
            return carry

        lax.fori_loop(0, per_piece, one, 0, unroll=2)


IN_VMEM = pl.BlockSpec(memory_space=pltpu.VMEM)
IN_SMEM = pl.BlockSpec(memory_space=pltpu.SMEM)


def attend_forward(source, packed, ends, qkv, block):
    pieces = len(qkv)
    rows = pieces * (qkv[0].shape[0] // JOINT * TILE)
    turned = pltpu.VMEM((HEAD, rows), BF16)
    return pl.pallas_call(
        functools.partial(forward_kernel, block, ends.shape[0]),
        in_specs=[IN_SMEM] * 3 + [IN_VMEM] * pieces,
        out_specs=[IN_VMEM] * (pieces + 2),
        out_shape=[bf16_rows(rows // (2 * pieces))] * pieces
        + [
            jax.ShapeDtypeStruct((HEAD, rows), F32),
            jax.ShapeDtypeStruct((1, rows), F32),
        ],
        scratch_shapes=[
            pltpu.VMEM((rows, HEAD), BF16),
            turned,
            turned,
            pltpu.VMEM((rows, HEAD), F32),
            pltpu.VMEM((rows, 2 * HEAD), BF16),
            pltpu.VMEM((rows // 2, 2 * HEAD), BF16),
        ],
        **params(rows * rows * HEAD * 40, 6 * rows * HEAD * 2, rows * rows),
    )(source, packed, ends, *qkv)


def attend_backward(source, packed, ends, qkv, do, o_t, lse, block):
    pieces = len(qkv)
    rows = pieces * (qkv[0].shape[0] // JOINT * TILE)
    half = pltpu.VMEM((rows, HEAD), BF16)
    wide = pltpu.VMEM((rows, HEAD), F32)
    pairs = pltpu.VMEM((rows // 2, 2 * HEAD), BF16)
    whole = pltpu.VMEM((rows, 2 * HEAD), BF16)
    return pl.pallas_call(
        functools.partial(backward_kernel, block, ends.shape[0]),
        in_specs=[IN_SMEM] * 3 + [IN_VMEM] * (2 * pieces + 2),
        out_specs=[IN_VMEM] * pieces,
        out_shape=[bf16_rows(qkv[0].shape[0])] * pieces,
        scratch_shapes=[
            half,
            half,
            half,
            half,
            pltpu.VMEM((2 * HEAD, rows), BF16),
            pltpu.VMEM((HEAD, rows), BF16),
            pltpu.VMEM((HEAD, rows), F32),
            pltpu.VMEM((1, rows), F32),
            wide,
            wide,
            whole,
            pairs,
            pairs,
            whole,
        ],
        **params(rows * rows * HEAD * 40, 12 * rows * HEAD * 2, rows * rows),
    )(source, packed, ends, *qkv, *do, o_t, lse)


def total(*parts):
    return sum((p.astype(F32) for p in parts[1:]), parts[0].astype(F32))


def exchange_in(parts, t):
    here = [lax.dynamic_index_in_dim(parts, t ^ s, 0, keepdims=False) for s in range(GROUP_IN)]
    there = [here[0]] + [xor_swap(here[s], "in", GROUP_IN, s) for s in range(1, GROUP_IN)]
    stacked = jnp.stack(there)
    return jnp.stack([lax.dynamic_index_in_dim(stacked, t ^ u, 0, keepdims=False) for u in range(GROUP_IN)])


def exchange_out(parts):
    size = len(parts)
    return [parts[0]] + [xor_swap(parts[s], "out", size, s) for s in range(1, size)]


def body(
    tokens,
    seq_lengths,
    dealing,
    ln1_gain,
    ln1_bias,
    ln2_gain,
    ln2_bias,
    w_qkv,
    b_qkv,
    w_out,
    w_in,
    b_in,
    w_fc2,
    b_out,
    cotangent,
):
    n_dp, n_out, n_in = lax.axis_size("dp"), lax.axis_size("out"), lax.axis_size("in")
    n_g = n_dp * n_out
    n_all = n_g * n_in
    rows_dev, width = tokens.shape
    ff = w_in.shape[1]
    ff_in = ff // n_in
    r_w = w_in.shape[0]
    r_ff = w_fc2.shape[0]
    block = LONGEST // (2 * n_out * n_in)
    slots_dev = rows_dev // block
    heads = width // HEAD
    h_in = heads // n_in
    cols = h_in * HEAD
    rows = rows_dev * n_in
    layout = Rows(n_dp, n_in, n_out, r_w)
    z, t = lax.axis_index("out"), lax.axis_index("in")
    z_arr = z[None].astype(jnp.int32)
    lengths, order = seq_lengths[0], dealing[0]
    ends = jnp.cumsum(lengths)

    slots = order.shape[0]
    ids = jnp.arange(slots, dtype=jnp.int32)
    slot_of = jnp.sum(jnp.where(order[None, :] == ids[:, None], ids[None, :], 0), axis=1)
    chunk = slot_of // slots_dev
    source = (((chunk % n_out) ^ z) * n_in + ((chunk // n_out) ^ t)) * slots_dev + slot_of % slots_dev
    source = source.astype(jnp.int32)
    lies = ids // slots_dev
    slot_here = (((lies % n_in) ^ t) * n_out + ((lies // n_in) ^ z)) * slots_dev + ids % slots_dev
    packed_of = jnp.sum(jnp.where(slot_here[:, None] == ids[None, :], order[None, :], 0), axis=1).astype(jnp.int32)

    part = jnp.arange(rows, dtype=jnp.int32)
    packed = packed_of[: rows // block].reshape(-1, 1) * block + jnp.arange(block, dtype=jnp.int32)[None, :]
    packed = packed.reshape(rows)
    starts = jnp.max(jnp.where(packed[:, None] >= ends[None, :], ends[None, :], 0), axis=1)
    position = (packed - starts).astype(F32)
    vectors = [ln1_gain, ln1_bias, ln2_gain, ln2_bias, b_qkv, b_out, b_in]
    sizes = [v.shape[0] for v in vectors]
    per_row = -(-len(vectors) // r_w)
    lanes = 128 // per_row
    qkv_cols = jnp.transpose(w_qkv.reshape(r_w, 3, n_in, cols), (2, 0, 1, 3)).reshape(n_in, r_w, 3 * cols)
    in_cols = jnp.transpose(w_in.reshape(r_w, n_dp, n_in, n_out, r_ff), (2, 0, 1, 3, 4)).reshape(n_in, r_w, ff_in)
    vec = jnp.stack([jnp.pad(v, (0, lanes - v.shape[0])) for v in vectors])
    vec = jnp.pad(vec, ((0, r_w * per_row - len(vectors)), (0, 0))).reshape(r_w, 128)
    vec = jnp.broadcast_to(vec[None], (n_in, r_w, 128))
    joined_cols = exchange_in(jnp.concatenate([qkv_cols, vec, in_cols], axis=2), t).reshape(n_in * r_w, -1)
    home = []
    for b in range(n_all):
        t_to, g_to = b // n_g, b % n_g
        home.append((b, ((g_to // n_out) * n_in + t_to) * n_out + g_to % n_out))
    out_rows = lax.ppermute(w_out, ALL_AXES, home).reshape(n_in * r_w, cols)
    first = jnp.concatenate([joined_cols[:, : 3 * cols + 128], out_rows], axis=1)
    first, to_send = lax.optimization_barrier((first, tokens))
    x_near = xor_swap(to_send, "in", n_in, 1)
    x_far, x_near = lax.optimization_barrier((xor_swap(to_send, "in", n_in, 2), x_near))
    first, position = lax.optimization_barrier((lax.all_gather(first, G_AXES, axis=0, tiled=False), position))
    second = jnp.concatenate([joined_cols[:, 3 * cols + 128 :], w_fc2], axis=1)

    def natural(value):
        value = value.reshape(n_dp, n_out, n_in, r_w, -1)
        return jnp.transpose(value, (0, 2, 1, 3, 4)).reshape(n_all * r_w, -1)

    def by_owner(value):
        value = value.reshape(n_dp, n_in, n_out, r_w, -1)
        return jnp.transpose(value, (0, 2, 1, 3, 4)).reshape(n_g, n_in * r_w, -1)

    weight_qkv = natural(first[:, :, : 3 * cols])
    weight_out = first[:, :, 3 * cols + 128 :].reshape(cols, width)
    vec_all = first[:, :, 3 * cols : 3 * cols + 128].reshape(n_dp, n_out, n_in, r_w * per_row, lanes)
    vec_all = jnp.transpose(vec_all[:, :, :, : len(vectors)], (3, 0, 2, 1, 4)).astype(F32)
    spans = [vec_all[i, ..., :size] for i, size in enumerate(sizes)]
    gain_one, shift_one, gain_two, shift_two = [s.reshape(width) for s in spans[:4]]
    bias_out = spans[5].reshape(width)
    bias_in = lax.dynamic_index_in_dim(spans[6], t, 1, keepdims=False).reshape(ff_in)
    bias_qkv = lax.dynamic_index_in_dim(spans[4].reshape(3, n_in, cols), t, 1, keepdims=False).reshape(-1)
    norms = jnp.concatenate([jnp.stack([gain_one, shift_one, gain_two, shift_two]), jnp.zeros((4, width), F32)])

    lane = jnp.arange(2 * HEAD, dtype=jnp.int32) % HEAD
    half = ROT // 2
    freq = 10000.0 ** (-2.0 * (lane % half).astype(F32) / ROT)
    phase = position[:, None] * freq[None, :]
    cos = jnp.where(lane < ROT, jnp.cos(phase), 1.0)
    sine = jnp.sin(phase)
    sin_l = jnp.where(lane < half, sine, 0.0)
    sin_r = jnp.where((lane >= half) & (lane < ROT), sine, 0.0)

    x_both = xor_swap(x_far, "in", n_in, 1)
    x_both, weight_qkv, norms, bias_qkv, cos, sin_l, sin_r = lax.optimization_barrier(
        (x_both, weight_qkv, norms, bias_qkv, cos, sin_l, sin_r)
    )
    x_all = jnp.concatenate([tokens, x_near, x_far, x_both])
    x_all, to_send = lax.optimization_barrier((x_all, cotangent))
    dy_near, dy_far = [xor_swap(to_send, "in", n_in, step) for step in (1, 2)]

    n1, n2, *qkv = prep(z_arr, x_all, norms, weight_qkv, bias_qkv[None], cos, sin_l, sin_r, block)
    qkv = exchange_out(qkv)
    qkv, dy_far, dy_near, second = lax.optimization_barrier((qkv, dy_far, dy_near, second))
    second = lax.all_gather(second, G_AXES, axis=0, tiled=False)
    if not layout.aligned:
        in_rows = natural(second[:, :, :ff_in]).reshape(n_g, n_in * r_w, ff_in)
        second = jnp.concatenate([in_rows, second[:, :, ff_in:]], axis=2)
    dy_both = xor_swap(dy_far, "in", n_in, 1)
    *o, o_t, lse = attend_forward(source, packed_of, ends, qkv, block)
    o, dy_both = lax.optimization_barrier((o, dy_both))
    dy_all = jnp.concatenate([cotangent, dy_near, dy_far, dy_both])
    o = exchange_out(o)
    do = exchange_out(grad_att(z_arr, dy_all, weight_out, block))

    hidden, grad_up, y_ff, dx_ff, sums_two, grad_b_in = feed(
        layout, x_all, n2, dy_all, norms, second, bias_in[None]
    )
    o, y_ff = lax.optimization_barrier((o, y_ff))
    o, *y_parts = project(z_arr, o, y_ff, weight_out, block)
    if layout.aligned:
        second_grads = feed_grads(layout, n2, grad_up, hidden, dy_all, o)
    else:
        second_grads = jnp.concatenate(
            [
                by_owner(dot_tn(n2, grad_up).astype(BF16)),
                dot_tn(hidden, dy_all).astype(BF16).reshape(n_g, r_ff, width),
                dot_tn(o, dy_all).astype(BF16).reshape(n_g, r_w, width),
            ],
            axis=1,
        )

    do, second_grads, y_parts = lax.optimization_barrier((do, second_grads, y_parts))
    second_grads = lax.psum_scatter(second_grads, G_AXES, scatter_dimension=0, tiled=False)
    y_hop = xor_swap(y_parts[3], "in", n_in, 1)
    own = tokens.astype(F32)
    parts = attend_backward(source, packed_of, ends, qkv, do, o_t, lse, block)
    parts, y_hop, y_parts = lax.optimization_barrier((parts, y_hop, y_parts))
    parts = exchange_out(parts)
    y_near = xor_swap(y_parts[1], "in", n_in, 1)
    y_far = xor_swap(total(y_parts[2], y_hop).astype(BF16), "in", n_in, 2)
    parts, y_far, y_near = lax.optimization_barrier((parts, y_far, y_near))
    da, sums_one, grad_b_qkv, *w_parts = post(
        z_arr, parts, x_all, dx_ff, norms, weight_qkv, cos, sin_l, sin_r, block
    )
    w_parts, da, second_grads = lax.optimization_barrier((w_parts, da, second_grads))
    w_hop = xor_swap(w_parts[3], "in", n_in, 1)
    w_hop, w_near, tokens, y_far, second_grads = lax.optimization_barrier(
        (w_hop, w_parts[1], tokens, y_far, second_grads)
    )
    w_far = xor_swap(total(w_parts[2], w_hop).astype(BF16), "in", n_in, 2)
    w_near = xor_swap(w_near, "in", n_in, 1)
    own = tokens.astype(F32)
    mixed = (own + total(y_parts[0], y_near, y_far) + bias_out).astype(BF16)
    w_far, w_near, in_part = lax.optimization_barrier((w_far, w_near, second_grads[: n_in * r_w]))
    in_part = exchange_in(in_part.reshape(n_in, r_w, ff_in), t)
    w_sum = total(w_parts[0], w_near, w_far)

    def placed(vector, axis):
        spread = jnp.expand_dims(vector, axis)
        mask = (jnp.arange(n_in) == t).reshape([-1 if a == axis else 1 for a in range(spread.ndim)])
        return jnp.where(mask, spread, 0.0).reshape(-1)

    grad_own = cotangent.astype(F32)
    vec_grads = [
        sums_one[0],
        sums_one[1],
        sums_two[0],
        sums_two[1],
        placed(grad_b_qkv[0].reshape(3, cols), 1),
        jnp.sum(grad_own, axis=0),
        placed(grad_b_in[0].reshape(n_dp, n_out, r_ff), 1),
    ]
    vec_grads = [v.astype(BF16).reshape(n_dp, n_in, n_out, -1) for v in vec_grads]
    vec_grads = jnp.stack([jnp.pad(v, ((0, 0), (0, 0), (0, 0), (0, lanes - v.shape[-1]))) for v in vec_grads], axis=3)
    spare = r_w * per_row - len(vectors)
    vec_grads = jnp.pad(vec_grads, ((0, 0), (0, 0), (0, 0), (0, spare), (0, 0)))
    vec_grads = jnp.transpose(vec_grads, (0, 2, 1, 3, 4)).reshape(n_g, n_in * r_w, 128)
    if layout.aligned:
        first_grads = qkv_grads(layout, n1, da, vec_grads)
    else:
        first_grads = jnp.concatenate([by_owner(dot_tn(n1, da).astype(BF16)), vec_grads], axis=2)
    first_grads = lax.psum_scatter(first_grads, G_AXES, scatter_dimension=0, tiled=False)

    qkv_part = exchange_in(first_grads.reshape(n_in, r_w, 3 * cols + 128), t)
    in_part = in_part.reshape(n_in, r_w, n_dp, n_out, r_ff)
    grad_w_in = jnp.transpose(in_part, (1, 2, 0, 3, 4)).reshape(r_w, ff).astype(F32)
    grad_w_fc2 = second_grads[n_in * r_w : n_in * r_w + r_ff].astype(F32)
    back_home = [(b, a) for a, b in home]
    out_part = second_grads[n_in * r_w + r_ff :]
    grad_w_out = lax.ppermute(out_part, ALL_AXES, back_home).astype(F32)
    qkv_grad = jnp.transpose(qkv_part[:, :, : 3 * cols].reshape(n_in, r_w, 3, cols), (1, 2, 0, 3))
    grad_w_qkv = qkv_grad.reshape(r_w, 3 * width).astype(F32)
    vec_part = jnp.sum(qkv_part[:, :, 3 * cols :].astype(F32), axis=0).reshape(r_w * per_row, lanes)
    vec_out = [vec_part[i, :size] for i, size in enumerate(sizes)]

    centred = own - jnp.mean(own, axis=-1, keepdims=True)
    own_rstd = lax.rsqrt(jnp.mean(centred * centred, axis=-1, keepdims=True) + EPS)
    own_hat = centred * own_rstd
    mean_w = jnp.mean(w_sum, axis=-1, keepdims=True)
    mean_wx = jnp.mean(w_sum * own_hat, axis=-1, keepdims=True)
    grad_tokens = grad_own + own_rstd * (w_sum - mean_w - own_hat * mean_wx)
    return (
        mixed,
        grad_tokens,
        vec_out[0],
        vec_out[1],
        vec_out[2],
        vec_out[3],
        grad_w_qkv,
        vec_out[4],
        grad_w_out,
        grad_w_in,
        vec_out[6],
        grad_w_fc2,
        vec_out[5],
    )


def solution(mesh):
    n_dp, n_ctx = mesh.shape["dp"], mesh.shape["ctx"]
    split = Mesh(mesh.devices.reshape(n_dp, GROUP_IN, n_ctx // GROUP_IN), ALL_AXES)
    mat, vec, group = P(ALL_AXES, None), P(ALL_AXES), P("dp", None)
    return jax.shard_map(
        body,
        mesh=split,
        in_specs=(mat, group, group, vec, vec, vec, vec, mat, vec, mat, mat, vec, mat, vec, mat),
        out_specs=(mat, mat, vec, vec, vec, vec, mat, vec, mat, mat, vec, mat, vec),
        check_vma=False,
    )
```

```python
import functools

import jax
import jax.numpy as jnp
from jax import lax
from jax.experimental import pallas as pl
from jax.experimental.pallas import tpu as pltpu
from jax.sharding import Mesh
from jax.sharding import PartitionSpec as P

HEAD = 64
ROT = 16
LONGEST = 2048
GROUP_IN = 4
TILE = 256
JOINT = TILE + TILE // 2
FQ, FK = 512, 512
BQ, BK = 512, 256
EPS = 1e-05
NEG = -1e30
F32 = jnp.float32
BF16 = jnp.bfloat16
G_AXES = ("dp", "out")
ALL_AXES = ("dp", "in", "out")


def dot(a, b):
    return jnp.dot(a, b, preferred_element_type=F32)


def dot_nt(a, b):
    return lax.dot_general(a, b, (((1,), (1,)), ((), ())), preferred_element_type=F32)


def dot_tn(a, b):
    return lax.dot_general(a, b, (((0,), (0,)), ((), ())), preferred_element_type=F32)


def xor_swap(value, axis, size, step):
    return lax.ppermute(value, axis, [(i, i ^ step) for i in range(size)])


def rotary(x, cos, sin_l, sin_r, sign):
    left = pltpu.roll(x, 128 - ROT // 2, 1)
    right = pltpu.roll(x, ROT // 2, 1)
    return x * cos - sign * (left * sin_l) + sign * (right * sin_r)


def pair_up(x, block):
    blocks = [x[i : i + block] for i in range(0, x.shape[0], block)]
    return jnp.concatenate([jnp.concatenate(blocks[i : i + 2], axis=1) for i in range(0, len(blocks), 2)], axis=0)


def unpair(x, block):
    parts = []
    for i in range(0, x.shape[0], block):
        parts += [x[i : i + block, :HEAD], x[i : i + block, HEAD:]]
    return jnp.concatenate(parts, axis=0)


def params(flops, size, exps=0):
    return dict(
        compiler_params=pltpu.CompilerParams(vmem_limit_bytes=60 * 2**20),
        cost_estimate=pl.CostEstimate(flops=flops, bytes_accessed=size, transcendentals=exps),
    )


def row_at(i, z):
    return (i, 0)


def whole_at(i, z):
    return (0, 0)


def piece(size):
    return pl.BlockSpec((size, 2 * HEAD), row_at)


def bf16_rows(rows):
    return jax.ShapeDtypeStruct((rows, 2 * HEAD), BF16)


def normalized(x_ref):
    x = x_ref[...].astype(F32)
    centred = x - jnp.mean(x, axis=-1, keepdims=True)
    return centred * lax.rsqrt(jnp.mean(centred * centred, axis=-1, keepdims=True) + EPS)


def turn(z, parts):
    out = []
    for step in range(len(parts)):
        pick = parts[step]
        for at in range(1, len(parts)):
            pick = jnp.where(z == at, parts[at ^ step], pick)
        out.append(pick)
    return out


def prep_kernel(heads, block, z_ref, x_ref, norm_ref, w_ref, b_ref, cos_ref, sl_ref, sr_ref, n1_ref, n2_ref, *out_refs):
    z = z_ref[0]
    xhat = normalized(x_ref)
    n1 = (xhat * norm_ref[0:1] + norm_ref[1:2]).astype(BF16)
    n1_ref[...] = n1
    n2_ref[...] = (xhat * norm_ref[2:3] + norm_ref[3:4]).astype(BF16)
    joined = dot(n1, w_ref[...]) + b_ref[...]
    cos, sl, sr = cos_ref[...], sl_ref[...], sr_ref[...]
    cols = heads * HEAD
    qk, v = [], []
    for h in range(heads):
        at = h * HEAD
        part = jnp.concatenate([joined[:, at : at + HEAD], joined[:, cols + at : cols + at + HEAD]], axis=1)
        qk.append(rotary(part, cos, sl, sr, 1.0))
        v.append(pair_up(joined[:, 2 * cols + at : 2 * cols + at + HEAD], block))
    for ref, one, two in zip(out_refs, turn(z, qk), turn(z, v)):
        ref[:TILE, :] = one.astype(BF16)
        ref[TILE:, :] = two.astype(BF16)


def prep(z, x, norms, w, bias, cos, sl, sr, block):
    rows, width = x.shape
    heads = w.shape[1] // (3 * HEAD)
    table = pl.BlockSpec((TILE, 2 * HEAD), row_at)
    tile = pl.BlockSpec((TILE, width), row_at)
    norm = jax.ShapeDtypeStruct((rows, width), BF16)
    return pl.pallas_call(
        functools.partial(prep_kernel, heads, block),
        grid_spec=pltpu.PrefetchScalarGridSpec(
            num_scalar_prefetch=1,
            grid=(rows // TILE,),
            in_specs=[
                tile,
                pl.BlockSpec(norms.shape, whole_at),
                pl.BlockSpec(w.shape, whole_at),
                pl.BlockSpec(bias.shape, whole_at),
                table,
                table,
                table,
            ],
            out_specs=[tile, tile] + [piece(JOINT)] * heads,
        ),
        out_shape=[norm, norm] + [bf16_rows(rows // TILE * JOINT)] * heads,
        **params(2 * rows * width * w.shape[1], 12 * 2**20),
    )(z, x, norms, w, bias, cos, sl, sr)


class Rows:
    def __init__(self, n_dp, n_in, n_out, r_w):
        self.n_in, self.n_out, self.r_w = n_in, n_out, r_w
        self.count = n_dp * n_in * n_out
        self.aligned = r_w % 16 == 0

    def place(self, block):
        out = block % self.n_out
        unit = (block // self.n_out) % self.n_in
        return block // (self.n_out * self.n_in) * self.n_out + out, unit * self.r_w


def feed_kernel(
    layout, x_ref, n2_ref, dy_ref, norm_ref, w_ref, b_ref, h_ref, du_ref, y_ref, dx_ref, sums_ref, db_ref, w_in_ref, w_fc2_ref
):
    units = w_in_ref.shape[1]

    @pl.when(pl.program_id(0) == 0)
    def _():
        size = w_ref.shape[1]
        for part in range(w_ref.shape[0]):
            w_fc2_ref[part * size : (part + 1) * size, :] = w_ref[part, :, units:]
            if not layout.aligned:
                w_in_ref[part * size : (part + 1) * size, :] = w_ref[part, :, :units]
        if layout.aligned:
            for at in range(layout.count):
                part, row = layout.place(at)
                w_in_ref[at * layout.r_w : (at + 1) * layout.r_w, :] = w_ref[part, row : row + layout.r_w, :units]

    up = dot(n2_ref[...], w_in_ref[...]) + b_ref[...]
    cdf = 0.5 + 0.5 * lax.erf(up * (0.5**0.5))
    hidden = (up * cdf).astype(BF16)
    slope = cdf + up * (jnp.exp(-0.5 * up * up) * 0.3989422804014327)
    grad_up = (dot_nt(dy_ref[...], w_fc2_ref[...]) * slope).astype(BF16)
    h_ref[...] = hidden
    du_ref[...] = grad_up
    y_ref[...] = dot(hidden, w_fc2_ref[...])
    grad_norm = dot_nt(grad_up, w_in_ref[...])
    dx_ref[...] = grad_norm * norm_ref[2:3]
    gain = jnp.sum(grad_norm * normalized(x_ref), axis=0, keepdims=True)
    shift = jnp.sum(grad_norm, axis=0, keepdims=True)
    bias = jnp.sum(grad_up.astype(F32), axis=0, keepdims=True)

    @pl.when(pl.program_id(0) == 0)
    def _():
        sums_ref[...] = jnp.zeros_like(sums_ref)
        db_ref[...] = jnp.zeros_like(db_ref)

    sums_ref[0:1] += gain
    sums_ref[1:2] += shift
    db_ref[0:1] += bias


def feed(layout, x, n2, dy, norms, w, bias):
    rows, width = x.shape
    units = bias.shape[1]
    row, whole = lambda i: (i, 0), lambda i: (0, 0)
    tile, tile_ff = pl.BlockSpec((TILE, width), row), pl.BlockSpec((TILE, units), row)
    return pl.pallas_call(
        functools.partial(feed_kernel, layout),
        grid=(rows // TILE,),
        in_specs=[
            tile,
            tile,
            tile,
            pl.BlockSpec(norms.shape, whole),
            pl.BlockSpec(w.shape, lambda i: (0, 0, 0)),
            pl.BlockSpec(bias.shape, whole),
        ],
        out_specs=[
            tile_ff,
            tile_ff,
            tile,
            tile,
            pl.BlockSpec((8, width), whole),
            pl.BlockSpec((8, units), whole),
        ],
        out_shape=[
            jax.ShapeDtypeStruct((rows, units), BF16),
            jax.ShapeDtypeStruct((rows, units), BF16),
            jax.ShapeDtypeStruct((rows, width), F32),
            jax.ShapeDtypeStruct((rows, width), F32),
            jax.ShapeDtypeStruct((8, width), F32),
            jax.ShapeDtypeStruct((8, units), F32),
        ],
        scratch_shapes=[pltpu.VMEM((width, units), BF16), pltpu.VMEM((units, width), BF16)],
        **params(8 * rows * width * units, 24 * 2**20, 2 * rows * units),
    )(x, n2, dy, norms, w, bias)


def feed_grads_kernel(layout, n2_ref, du_ref, h_ref, dy_ref, o_ref, out_ref):
    step = pl.program_id(0)
    size = out_ref.shape[1] // 9 * 4
    grad = dot_tn(n2_ref[...], du_ref[...]).astype(BF16)
    for b in range(TILE // layout.r_w):
        part, row = layout.place(step * (TILE // layout.r_w) + b)
        out_ref[part, pl.ds(pl.multiple_of(row, 16), layout.r_w), :] = grad[b * layout.r_w : (b + 1) * layout.r_w]
    grad = dot_tn(h_ref[...], dy_ref[...]).astype(BF16)
    for b in range(TILE // size):
        out_ref[step * (TILE // size) + b, size : 2 * size, :] = grad[b * size : (b + 1) * size]

    @pl.when(step == 0)
    def _():
        grad = dot_tn(o_ref[...], dy_ref[...]).astype(BF16)
        for part in range(out_ref.shape[0]):
            out_ref[part, 2 * size :, :] = grad[part * layout.r_w : (part + 1) * layout.r_w]


def feed_grads(layout, n2, du, h, dy, o):
    rows, width = n2.shape
    units = h.shape[1]
    parts = layout.count // layout.n_in
    shape = (parts, units // parts + layout.n_in * layout.r_w + layout.r_w, width)
    columns = pl.BlockSpec((rows, TILE), lambda i: (0, i))
    whole = lambda i: (0, 0)
    return pl.pallas_call(
        functools.partial(feed_grads_kernel, layout),
        grid=(width // TILE,),
        in_specs=[
            columns,
            pl.BlockSpec(du.shape, whole),
            columns,
            pl.BlockSpec(dy.shape, whole),
            pl.BlockSpec(o.shape, whole),
        ],
        out_specs=pl.BlockSpec(shape, lambda i: (0, 0, 0)),
        out_shape=jax.ShapeDtypeStruct(shape, BF16),
        **params(4 * rows * width * units, 14 * 2**20),
    )(n2, du, h, dy, o)


def qkv_grads_kernel(layout, n1_ref, da_ref, vec_ref, out_ref):
    step = pl.program_id(0)
    cols = da_ref.shape[1]
    grad = dot_tn(n1_ref[...], da_ref[...]).astype(BF16)
    for b in range(TILE // layout.r_w):
        part, row = layout.place(step * (TILE // layout.r_w) + b)
        out_ref[part, pl.ds(pl.multiple_of(row, 16), layout.r_w), :cols] = grad[b * layout.r_w : (b + 1) * layout.r_w]

    @pl.when(step == 0)
    def _():
        out_ref[:, :, cols:] = vec_ref[...]


def qkv_grads(layout, n1, da, vec):
    rows, width = n1.shape
    shape = (vec.shape[0], vec.shape[1], da.shape[1] + vec.shape[2])
    return pl.pallas_call(
        functools.partial(qkv_grads_kernel, layout),
        grid=(width // TILE,),
        in_specs=[
            pl.BlockSpec((rows, TILE), lambda i: (0, i)),
            pl.BlockSpec(da.shape, lambda i: (0, 0)),
            pl.BlockSpec(vec.shape, lambda i: (0, 0, 0)),
        ],
        out_specs=pl.BlockSpec(shape, lambda i: (0, 0, 0)),
        out_shape=jax.ShapeDtypeStruct(shape, BF16),
        **params(2 * rows * width * da.shape[1], 6 * 2**20),
    )(n1, da, vec)


def grad_att_kernel(heads, block, z_ref, dy_ref, wo_ref, *out_refs):
    grad = dot_nt(dy_ref[...], wo_ref[...])
    parts = [pair_up(grad[:, h * HEAD : (h + 1) * HEAD], block) for h in range(heads)]
    for ref, part in zip(out_refs, turn(z_ref[0], parts)):
        ref[...] = part.astype(BF16)


def grad_att(z, dy, wo, block):
    rows, width = dy.shape
    heads = wo.shape[0] // HEAD
    return pl.pallas_call(
        functools.partial(grad_att_kernel, heads, block),
        grid_spec=pltpu.PrefetchScalarGridSpec(
            num_scalar_prefetch=1,
            grid=(rows // TILE,),
            in_specs=[pl.BlockSpec((TILE, width), row_at), pl.BlockSpec(wo.shape, whole_at)],
            out_specs=[piece(TILE // 2)] * heads,
        ),
        out_shape=[bf16_rows(rows // 2)] * heads,
        **params(2 * rows * width * wo.shape[0], 4 * 2**20),
    )(z, dy, wo)


def split_parts(step, total, refs):
    low = total.astype(BF16)
    for at, ref in enumerate(refs):

        @pl.when(step == at)
        def _(ref=ref):
            ref[...] = low


def project_kernel(heads, block, z_ref, y_ref, wo_ref, *refs):
    parts = turn(z_ref[0], [unpair(ref[...].astype(F32), block) for ref in refs[:heads]])
    o_ref = refs[heads]
    for h in range(0, heads, 2):
        o_ref[:, h * HEAD : (h + 2) * HEAD] = jnp.concatenate(parts[h : h + 2], axis=1).astype(BF16)
    total = y_ref[...] + dot(o_ref[...], wo_ref[...])
    split_parts(pl.program_id(0), total, refs[heads + 1 :])


def project(z, parts, y, wo, block):
    heads = len(parts)
    rows, width = y.shape
    tile = pl.BlockSpec((TILE, width), row_at)
    return pl.pallas_call(
        functools.partial(project_kernel, heads, block),
        grid_spec=pltpu.PrefetchScalarGridSpec(
            num_scalar_prefetch=1,
            grid=(rows // TILE,),
            in_specs=[tile, pl.BlockSpec(wo.shape, whole_at)] + [piece(TILE // 2)] * heads,
            out_specs=[pl.BlockSpec((TILE, heads * HEAD), row_at)] + [pl.BlockSpec((TILE, width), whole_at)] * GROUP_IN,
        ),
        out_shape=[jax.ShapeDtypeStruct((rows, heads * HEAD), BF16)] + [jax.ShapeDtypeStruct((TILE, width), BF16)] * GROUP_IN,
        **params(2 * rows * width * wo.shape[0], 8 * 2**20),
    )(z, y, wo, *parts)


def post_kernel(
    heads, block, z_ref, x_ref, dx_ref, norm_ref, w_ref, cos_ref, sl_ref, sr_ref, *refs
):
    z = z_ref[0]
    dqk = turn(z, [ref[:TILE, :].astype(F32) for ref in refs[:heads]])
    dv = turn(z, [unpair(ref[TILE:, :].astype(F32), block) for ref in refs[:heads]])
    da_ref, sums_ref, db_ref = refs[heads : heads + 3]
    cos, sl, sr = cos_ref[...], sl_ref[...], sr_ref[...]
    cols = heads * HEAD
    for h in range(0, heads, 2):
        at = h * HEAD
        one = rotary(dqk[h], cos, sl, sr, -1.0)
        two = rotary(dqk[h + 1], cos, sl, sr, -1.0)
        da_ref[:, at : at + 2 * HEAD] = jnp.concatenate([one[:, :HEAD], two[:, :HEAD]], axis=1).astype(BF16)
        da_ref[:, cols + at : cols + at + 2 * HEAD] = jnp.concatenate([one[:, HEAD:], two[:, HEAD:]], axis=1).astype(BF16)
        da_ref[:, 2 * cols + at : 2 * cols + at + 2 * HEAD] = jnp.concatenate(dv[h : h + 2], axis=1).astype(BF16)
    grad = da_ref[...]
    grad_norm = dot_nt(grad, w_ref[...])
    total = dx_ref[...] + grad_norm * norm_ref[0:1]
    split_parts(pl.program_id(0), total, refs[heads + 3 :])
    gain = jnp.sum(grad_norm * normalized(x_ref), axis=0, keepdims=True)
    shift = jnp.sum(grad_norm, axis=0, keepdims=True)
    bias = jnp.sum(grad.astype(F32), axis=0, keepdims=True)

    @pl.when(pl.program_id(0) == 0)
    def _():
        sums_ref[...] = jnp.zeros_like(sums_ref)
        db_ref[...] = jnp.zeros_like(db_ref)

    sums_ref[0:1] += gain
    sums_ref[1:2] += shift
    db_ref[0:1] += bias


def post(z, grads, x, dx, norms, w, cos, sl, sr, block):
    heads = len(grads)
    rows, width = x.shape
    three = heads * 3 * HEAD
    table = pl.BlockSpec((TILE, 2 * HEAD), row_at)
    tile = pl.BlockSpec((TILE, width), row_at)
    return pl.pallas_call(
        functools.partial(post_kernel, heads, block),
        grid_spec=pltpu.PrefetchScalarGridSpec(
            num_scalar_prefetch=1,
            grid=(rows // TILE,),
            in_specs=[
                tile,
                tile,
                pl.BlockSpec(norms.shape, whole_at),
                pl.BlockSpec(w.shape, whole_at),
                table,
                table,
                table,
            ]
            + [piece(JOINT)] * heads,
            out_specs=[
                pl.BlockSpec((TILE, three), row_at),
                pl.BlockSpec((8, width), whole_at),
                pl.BlockSpec((8, three), whole_at),
            ]
            + [pl.BlockSpec((TILE, width), whole_at)] * GROUP_IN,
        ),
        out_shape=[
            jax.ShapeDtypeStruct((rows, three), BF16),
            jax.ShapeDtypeStruct((8, width), F32),
            jax.ShapeDtypeStruct((8, three), F32),
        ]
        + [jax.ShapeDtypeStruct((TILE, width), BF16)] * GROUP_IN,
        **params(2 * rows * width * three, 14 * 2**20),
    )(z, x, dx, norms, w, cos, sl, sr, *grads)


def doc_start(packed, ends_ref, count):
    start = packed * 0
    for d in range(count):
        start = jnp.where(packed >= ends_ref[d], ends_ref[d], start)
    return start


def doc_end(packed, ends_ref, count):
    end = ends_ref[count - 1]
    for d in range(count - 2, -1, -1):
        end = jnp.where(packed < ends_ref[d], ends_ref[d], end)
    return end


def tile_at(i, size=TILE):
    return pl.ds(pl.multiple_of(i * size, size), size)


def load_half(ref, source, block):
    both = ref[pl.ds(pl.multiple_of((source // 2) * block, block), block), :].astype(F32)
    return jnp.where(source % 2 == 0, both[:, :HEAD], both[:, HEAD:])


def scores(masked, k_s, q_t, ends_ref, count, i, j, q_size, k_size):
    s = dot(k_s[tile_at(j, k_size), :], q_t[:HEAD, tile_at(i, q_size)])
    if not masked:
        return s
    key_at = lax.broadcasted_iota(jnp.int32, (k_size, q_size), 0)
    query_at = lax.broadcasted_iota(jnp.int32, (k_size, q_size), 1)
    query_row = i * q_size + lax.broadcasted_iota(jnp.int32, (1, q_size), 1)
    first = doc_start(query_row, ends_ref, count) - j * k_size
    last = i * q_size - j * k_size + query_at
    return jnp.where((key_at >= first) & (key_at <= last), s, NEG)


def lay_out(pieces, whole):
    size = pieces[0].shape[0]
    for i, ref in enumerate(pieces):
        whole[i * size : (i + 1) * size, :] = ref[...]


def lay_out_joint(pieces, qk, v):
    at = 0
    for ref in pieces:
        for i in range(0, ref.shape[0], JOINT):
            qk[at : at + TILE, :] = ref[i : i + TILE, :]
            v[at // 2 : (at + TILE) // 2, :] = ref[i + TILE : i + JOINT, :]
            at += TILE


def forward_kernel(block, count, source_ref, packed_ref, ends_ref, *refs):
    pieces = (len(refs) - 8) // 2
    qkv_in, o_out = refs[:pieces], refs[pieces : 2 * pieces]
    o_t, lse_ref, k_s, q_t, v_t, o_s, qk_ref, v_ref = refs[2 * pieces :]
    rows = qk_ref.shape[0]
    lay_out_joint(qkv_in, qk_ref, v_ref)
    tiles = rows // TILE
    per = TILE // block
    scale = HEAD ** (-0.5)

    def gather(i, carry):
        qk, v = [], []
        for b in range(per):
            src = source_ref[i * per + b]
            qk.append(qk_ref[pl.ds(pl.multiple_of(src * block, block), block), :].astype(F32))
            v.append(load_half(v_ref, src, block))
        qk, v = jnp.concatenate(qk, axis=0), jnp.concatenate(v, axis=0)
        k_s[tile_at(i), :] = qk[:, HEAD:].astype(BF16)
        q_t[:, tile_at(i)] = (qk.T[:HEAD] * scale).astype(BF16)
        v_t[:, tile_at(i)] = v.T.astype(BF16)
        return carry

    lax.fori_loop(0, tiles, gather, 0, unroll=4)

    def forward(i, carry):
        here = tile_at(i, FQ)

        def step(masked, j, state):
            top, total, acc = state
            s = scores(masked, k_s, q_t, ends_ref, count, i, j, FQ, FK)
            new_top = jnp.maximum(top, jnp.max(s, axis=0, keepdims=True))
            p = jnp.exp(s - new_top)
            fade = jnp.exp(top - new_top)
            total = total * fade + jnp.sum(p, axis=0, keepdims=True)
            acc = acc * fade + dot(v_t[:, tile_at(j, FK)], p.astype(BF16))
            return new_top, total, acc

        low = doc_start(i * FQ, ends_ref, count) // FK
        high = (i * FQ + FQ - 1) // FK + 1
        inner_low = (doc_start(i * FQ + FQ - 1, ends_ref, count) + FK - 1) // FK
        inner_high = jnp.maximum((i * FQ + 1) // FK, low)
        inner_low = jnp.clip(inner_low, low, inner_high)
        state = (jnp.full((1, FQ), NEG, F32), jnp.zeros((1, FQ), F32), jnp.zeros((HEAD, FQ), F32))
        state = lax.fori_loop(low, inner_low, functools.partial(step, True), state)
        state = lax.fori_loop(inner_low, inner_high, functools.partial(step, False), state)
        top, total, acc = lax.fori_loop(inner_high, high, functools.partial(step, True), state)
        out = acc / total
        lse_ref[:, here] = top + jnp.log(total)
        o_t[:, here] = out
        o_s[here, :] = out.T
        return carry

    lax.fori_loop(0, rows // FQ, forward, 0)

    send_pairs(o_s, o_out, packed_ref, block)


def load_pair(whole, row, packed_ref, block):
    both = [whole[pl.ds(pl.multiple_of(packed_ref[row + b] * block, block), block), :] for b in range(2)]
    return jnp.concatenate(both, axis=1).astype(BF16)


def send_pairs(whole, out_refs, packed_ref, block):
    per = out_refs[0].shape[0] // block
    for at, ref in enumerate(out_refs):

        def one(i, carry):
            ref[pl.ds(pl.multiple_of(i * block, block), block), :] = load_pair(whole, 2 * (at * per + i), packed_ref, block)
            return carry

        lax.fori_loop(0, per, one, 0, unroll=4)


def backward_kernel(block, count, source_ref, packed_ref, ends_ref, *refs):
    pieces = (len(refs) - 16) // 3
    qkv_in, do_in = refs[:pieces], refs[pieces : 2 * pieces]
    o_t, lse_ref = refs[2 * pieces : 2 * pieces + 2]
    grads_out = refs[2 * pieces + 2 : 3 * pieces + 2]
    q_s, k_s, v_s, do_s, qk_t, do_t, dq_t, delta_s, dk_s, dv_s, qk_ref, v_ref, do_ref, dqk_ref = refs[3 * pieces + 2 :]
    rows = qk_ref.shape[0]
    lay_out_joint(qkv_in, qk_ref, v_ref)
    lay_out(do_in, do_ref)
    tiles = rows // TILE
    per = TILE // block
    scale = HEAD ** (-0.5)

    def gather(i, carry):
        qk, v, do = [], [], []
        for b in range(per):
            src = source_ref[i * per + b]
            qk.append(qk_ref[pl.ds(pl.multiple_of(src * block, block), block), :].astype(F32))
            v.append(load_half(v_ref, src, block))
            do.append(load_half(do_ref, src, block))
        qk, v, do = jnp.concatenate(qk, axis=0), jnp.concatenate(v, axis=0), jnp.concatenate(do, axis=0)
        here = tile_at(i)
        q_s[here, :] = (qk[:, :HEAD] * scale).astype(BF16)
        k_s[here, :] = qk[:, HEAD:].astype(BF16)
        turned = qk.T
        qk_t[:HEAD, here] = (turned[:HEAD] * scale).astype(BF16)
        qk_t[HEAD:, here] = turned[HEAD:].astype(BF16)
        v_s[here, :] = v.astype(BF16)
        do_s[here, :] = do.astype(BF16)
        do_turned = do.T
        do_t[:, here] = do_turned.astype(BF16)
        dq_t[:, here] = jnp.zeros((HEAD, TILE), F32)
        delta_s[:, here] = jnp.sum(o_t[:, here] * do_turned, axis=0, keepdims=True)
        return carry

    lax.fori_loop(0, tiles, gather, 0, unroll=4)

    def backward(j, carry):
        keys = tile_at(j, BK)

        def step(masked, i, state):
            dk, dv = state
            here = tile_at(i, BQ)
            p = jnp.exp(scores(masked, k_s, qk_t, ends_ref, count, i, j, BQ, BK) - lse_ref[:, here])
            dp = dot(v_s[keys, :], do_t[:, here])
            ds = (p * (dp - delta_s[:, here])).astype(BF16)
            dv = dv + dot(p.astype(BF16), do_s[here, :])
            dk = dk + dot(ds, q_s[here, :])
            dq_t[:, here] += dot(qk_t[HEAD:, keys], ds)
            return dk, dv

        low = j * BK // BQ
        high = (doc_end(j * BK + BK - 1, ends_ref, count) - 1) // BQ + 1
        inner_low = jnp.minimum((j * BK + BK - 1 + BQ - 1) // BQ, high)
        inner_high = jnp.clip(doc_end(j * BK, ends_ref, count) // BQ, inner_low, high)
        zero = jnp.zeros((BK, HEAD), F32)
        state = lax.fori_loop(low, inner_low, functools.partial(step, True), (zero, zero))
        state = lax.fori_loop(inner_low, inner_high, functools.partial(step, False), state)
        dk, dv = lax.fori_loop(inner_high, high, functools.partial(step, True), state)
        dk_s[keys, :] = dk
        dv_s[keys, :] = dv
        return carry

    lax.fori_loop(0, rows // BK, backward, 0)

    def scatter(i, carry):
        here = tile_at(i)
        dq = (dq_t[:, here] * scale).T
        dqk = jnp.concatenate([dq, dk_s[here, :]], axis=1).astype(BF16)
        for b in range(per):
            dst = pl.ds(pl.multiple_of(source_ref[i * per + b] * block, block), block)
            dqk_ref[dst, :] = dqk[b * block : (b + 1) * block, :]
        return carry

    lax.fori_loop(0, tiles, scatter, 0, unroll=4)

    per_piece = rows // pieces // TILE
    for at, ref in enumerate(grads_out):

        def one(i, carry):
            start = at * per_piece + i
            out = pl.multiple_of(i * JOINT, JOINT)
            ref[pl.ds(out, TILE), :] = dqk_ref[tile_at(start), :]
            for b in range(0, per, 2):
                row = pl.multiple_of(out + TILE + b // 2 * block, block)
                ref[pl.ds(row, block), :] = load_pair(dv_s, start * per + b, packed_ref, block)
            return carry

        lax.fori_loop(0, per_piece, one, 0, unroll=2)


IN_VMEM = pl.BlockSpec(memory_space=pltpu.VMEM)
IN_SMEM = pl.BlockSpec(memory_space=pltpu.SMEM)


def attend_forward(source, packed, ends, qkv, block):
    pieces = len(qkv)
    rows = pieces * (qkv[0].shape[0] // JOINT * TILE)
    turned = pltpu.VMEM((HEAD, rows), BF16)
    return pl.pallas_call(
        functools.partial(forward_kernel, block, ends.shape[0]),
        in_specs=[IN_SMEM] * 3 + [IN_VMEM] * pieces,
        out_specs=[IN_VMEM] * (pieces + 2),
        out_shape=[bf16_rows(rows // (2 * pieces))] * pieces
        + [
            jax.ShapeDtypeStruct((HEAD, rows), F32),
            jax.ShapeDtypeStruct((1, rows), F32),
        ],
        scratch_shapes=[
            pltpu.VMEM((rows, HEAD), BF16),
            turned,
            turned,
            pltpu.VMEM((rows, HEAD), F32),
            pltpu.VMEM((rows, 2 * HEAD), BF16),
            pltpu.VMEM((rows // 2, 2 * HEAD), BF16),
        ],
        **params(rows * rows * HEAD * 40, 6 * rows * HEAD * 2, rows * rows),
    )(source, packed, ends, *qkv)


def attend_backward(source, packed, ends, qkv, do, o_t, lse, block):
    pieces = len(qkv)
    rows = pieces * (qkv[0].shape[0] // JOINT * TILE)
    half = pltpu.VMEM((rows, HEAD), BF16)
    wide = pltpu.VMEM((rows, HEAD), F32)
    pairs = pltpu.VMEM((rows // 2, 2 * HEAD), BF16)
    whole = pltpu.VMEM((rows, 2 * HEAD), BF16)
    return pl.pallas_call(
        functools.partial(backward_kernel, block, ends.shape[0]),
        in_specs=[IN_SMEM] * 3 + [IN_VMEM] * (2 * pieces + 2),
        out_specs=[IN_VMEM] * pieces,
        out_shape=[bf16_rows(qkv[0].shape[0])] * pieces,
        scratch_shapes=[
            half,
            half,
            half,
            half,
            pltpu.VMEM((2 * HEAD, rows), BF16),
            pltpu.VMEM((HEAD, rows), BF16),
            pltpu.VMEM((HEAD, rows), F32),
            pltpu.VMEM((1, rows), F32),
            wide,
            wide,
            whole,
            pairs,
            pairs,
            whole,
        ],
        **params(rows * rows * HEAD * 40, 12 * rows * HEAD * 2, rows * rows),
    )(source, packed, ends, *qkv, *do, o_t, lse)


def total(*parts):
    return sum((p.astype(F32) for p in parts[1:]), parts[0].astype(F32))


def exchange_in(parts, t):
    here = [lax.dynamic_index_in_dim(parts, t ^ s, 0, keepdims=False) for s in range(GROUP_IN)]
    there = [here[0]] + [xor_swap(here[s], "in", GROUP_IN, s) for s in range(1, GROUP_IN)]
    stacked = jnp.stack(there)
    return jnp.stack([lax.dynamic_index_in_dim(stacked, t ^ u, 0, keepdims=False) for u in range(GROUP_IN)])


def exchange_out(parts):
    size = len(parts)
    return [parts[0]] + [xor_swap(parts[s], "out", size, s) for s in range(1, size)]


def body(
    tokens,
    seq_lengths,
    dealing,
    ln1_gain,
    ln1_bias,
    ln2_gain,
    ln2_bias,
    w_qkv,
    b_qkv,
    w_out,
    w_in,
    b_in,
    w_fc2,
    b_out,
    cotangent,
):
    n_dp, n_out, n_in = lax.axis_size("dp"), lax.axis_size("out"), lax.axis_size("in")
    n_g = n_dp * n_out
    n_all = n_g * n_in
    rows_dev, width = tokens.shape
    ff = w_in.shape[1]
    ff_in = ff // n_in
    r_w = w_in.shape[0]
    r_ff = w_fc2.shape[0]
    block = LONGEST // (2 * n_out * n_in)
    slots_dev = rows_dev // block
    heads = width // HEAD
    h_in = heads // n_in
    cols = h_in * HEAD
    rows = rows_dev * n_in
    layout = Rows(n_dp, n_in, n_out, r_w)
    z, t = lax.axis_index("out"), lax.axis_index("in")
    z_arr = z[None].astype(jnp.int32)
    lengths, order = seq_lengths[0], dealing[0]
    ends = jnp.cumsum(lengths)

    slots = order.shape[0]
    ids = jnp.arange(slots, dtype=jnp.int32)
    slot_of = jnp.sum(jnp.where(order[None, :] == ids[:, None], ids[None, :], 0), axis=1)
    chunk = slot_of // slots_dev
    source = (((chunk % n_out) ^ z) * n_in + ((chunk // n_out) ^ t)) * slots_dev + slot_of % slots_dev
    source = source.astype(jnp.int32)
    lies = ids // slots_dev
    slot_here = (((lies % n_in) ^ t) * n_out + ((lies // n_in) ^ z)) * slots_dev + ids % slots_dev
    packed_of = jnp.sum(jnp.where(slot_here[:, None] == ids[None, :], order[None, :], 0), axis=1).astype(jnp.int32)

    part = jnp.arange(rows, dtype=jnp.int32)
    packed = packed_of[: rows // block].reshape(-1, 1) * block + jnp.arange(block, dtype=jnp.int32)[None, :]
    packed = packed.reshape(rows)
    starts = jnp.max(jnp.where(packed[:, None] >= ends[None, :], ends[None, :], 0), axis=1)
    position = (packed - starts).astype(F32)
    vectors = [ln1_gain, ln1_bias, ln2_gain, ln2_bias, b_qkv, b_out, b_in]
    sizes = [v.shape[0] for v in vectors]
    per_row = -(-len(vectors) // r_w)
    lanes = 128 // per_row
    qkv_cols = jnp.transpose(w_qkv.reshape(r_w, 3, n_in, cols), (2, 0, 1, 3)).reshape(n_in, r_w, 3 * cols)
    in_cols = jnp.transpose(w_in.reshape(r_w, n_dp, n_in, n_out, r_ff), (2, 0, 1, 3, 4)).reshape(n_in, r_w, ff_in)
    vec = jnp.stack([jnp.pad(v, (0, lanes - v.shape[0])) for v in vectors])
    vec = jnp.pad(vec, ((0, r_w * per_row - len(vectors)), (0, 0))).reshape(r_w, 128)
    vec = jnp.broadcast_to(vec[None], (n_in, r_w, 128))
    joined_cols = exchange_in(jnp.concatenate([qkv_cols, vec, in_cols], axis=2), t).reshape(n_in * r_w, -1)
    home = []
    for b in range(n_all):
        t_to, g_to = b // n_g, b % n_g
        home.append((b, ((g_to // n_out) * n_in + t_to) * n_out + g_to % n_out))
    out_rows = lax.ppermute(w_out, ALL_AXES, home).reshape(n_in * r_w, cols)
    first = jnp.concatenate([joined_cols[:, : 3 * cols + 128], out_rows], axis=1)
    first, to_send = lax.optimization_barrier((first, tokens))
    x_near = xor_swap(to_send, "in", n_in, 1)
    x_far, x_near = lax.optimization_barrier((xor_swap(to_send, "in", n_in, 2), x_near))
    first, position = lax.optimization_barrier((lax.all_gather(first, G_AXES, axis=0, tiled=False), position))
    second = jnp.concatenate([joined_cols[:, 3 * cols + 128 :], w_fc2], axis=1)

    def natural(value):
        value = value.reshape(n_dp, n_out, n_in, r_w, -1)
        return jnp.transpose(value, (0, 2, 1, 3, 4)).reshape(n_all * r_w, -1)

    def by_owner(value):
        value = value.reshape(n_dp, n_in, n_out, r_w, -1)
        return jnp.transpose(value, (0, 2, 1, 3, 4)).reshape(n_g, n_in * r_w, -1)

    weight_qkv = natural(first[:, :, : 3 * cols])
    weight_out = first[:, :, 3 * cols + 128 :].reshape(cols, width)
    vec_all = first[:, :, 3 * cols : 3 * cols + 128].reshape(n_dp, n_out, n_in, r_w * per_row, lanes)
    vec_all = jnp.transpose(vec_all[:, :, :, : len(vectors)], (3, 0, 2, 1, 4)).astype(F32)
    spans = [vec_all[i, ..., :size] for i, size in enumerate(sizes)]
    gain_one, shift_one, gain_two, shift_two = [s.reshape(width) for s in spans[:4]]
    bias_out = spans[5].reshape(width)
    bias_in = lax.dynamic_index_in_dim(spans[6], t, 1, keepdims=False).reshape(ff_in)
    bias_qkv = lax.dynamic_index_in_dim(spans[4].reshape(3, n_in, cols), t, 1, keepdims=False).reshape(-1)
    norms = jnp.concatenate([jnp.stack([gain_one, shift_one, gain_two, shift_two]), jnp.zeros((4, width), F32)])

    lane = jnp.arange(2 * HEAD, dtype=jnp.int32) % HEAD
    half = ROT // 2
    freq = 10000.0 ** (-2.0 * (lane % half).astype(F32) / ROT)
    phase = position[:, None] * freq[None, :]
    cos = jnp.where(lane < ROT, jnp.cos(phase), 1.0)
    sine = jnp.sin(phase)
    sin_l = jnp.where(lane < half, sine, 0.0)
    sin_r = jnp.where((lane >= half) & (lane < ROT), sine, 0.0)

    x_both = xor_swap(x_far, "in", n_in, 1)
    x_both, weight_qkv, norms, bias_qkv, cos, sin_l, sin_r = lax.optimization_barrier(
        (x_both, weight_qkv, norms, bias_qkv, cos, sin_l, sin_r)
    )
    x_all = jnp.concatenate([tokens, x_near, x_far, x_both])
    x_all, to_send = lax.optimization_barrier((x_all, cotangent))
    dy_near, dy_far = [xor_swap(to_send, "in", n_in, step) for step in (1, 2)]

    n1, n2, *qkv = prep(z_arr, x_all, norms, weight_qkv, bias_qkv[None], cos, sin_l, sin_r, block)
    qkv = exchange_out(qkv)
    qkv, dy_far, dy_near, second = lax.optimization_barrier((qkv, dy_far, dy_near, second))
    second = lax.all_gather(second, G_AXES, axis=0, tiled=False)
    if not layout.aligned:
        in_rows = natural(second[:, :, :ff_in]).reshape(n_g, n_in * r_w, ff_in)
        second = jnp.concatenate([in_rows, second[:, :, ff_in:]], axis=2)
    dy_both = xor_swap(dy_far, "in", n_in, 1)
    *o, o_t, lse = attend_forward(source, packed_of, ends, qkv, block)
    o, dy_both = lax.optimization_barrier((o, dy_both))
    dy_all = jnp.concatenate([cotangent, dy_near, dy_far, dy_both])
    o = exchange_out(o)
    do = exchange_out(grad_att(z_arr, dy_all, weight_out, block))

    hidden, grad_up, y_ff, dx_ff, sums_two, grad_b_in = feed(
        layout, x_all, n2, dy_all, norms, second, bias_in[None]
    )
    o, y_ff = lax.optimization_barrier((o, y_ff))
    o, *y_parts = project(z_arr, o, y_ff, weight_out, block)
    if layout.aligned:
        second_grads = feed_grads(layout, n2, grad_up, hidden, dy_all, o)
    else:
        second_grads = jnp.concatenate(
            [
                by_owner(dot_tn(n2, grad_up).astype(BF16)),
                dot_tn(hidden, dy_all).astype(BF16).reshape(n_g, r_ff, width),
                dot_tn(o, dy_all).astype(BF16).reshape(n_g, r_w, width),
            ],
            axis=1,
        )

    do, second_grads, y_parts = lax.optimization_barrier((do, second_grads, y_parts))
    second_grads = lax.psum_scatter(second_grads, G_AXES, scatter_dimension=0, tiled=False)
    y_hop = xor_swap(y_parts[3], "in", n_in, 1)
    own = tokens.astype(F32)
    parts = attend_backward(source, packed_of, ends, qkv, do, o_t, lse, block)
    parts, y_hop, y_parts = lax.optimization_barrier((parts, y_hop, y_parts))
    parts = exchange_out(parts)
    y_near = xor_swap(y_parts[1], "in", n_in, 1)
    y_far = xor_swap(total(y_parts[2], y_hop).astype(BF16), "in", n_in, 2)
    parts, y_far, y_near = lax.optimization_barrier((parts, y_far, y_near))
    da, sums_one, grad_b_qkv, *w_parts = post(
        z_arr, parts, x_all, dx_ff, norms, weight_qkv, cos, sin_l, sin_r, block
    )
    w_parts, da, second_grads = lax.optimization_barrier((w_parts, da, second_grads))
    w_hop = xor_swap(w_parts[3], "in", n_in, 1)
    w_hop, w_near, tokens, y_far, second_grads = lax.optimization_barrier(
        (w_hop, w_parts[1], tokens, y_far, second_grads)
    )
    w_far = xor_swap(total(w_parts[2], w_hop).astype(BF16), "in", n_in, 2)
    w_near = xor_swap(w_near, "in", n_in, 1)
    own = tokens.astype(F32)
    mixed = (own + total(y_parts[0], y_near, y_far) + bias_out).astype(BF16)
    in_part = exchange_in(second_grads[: n_in * r_w].reshape(n_in, r_w, ff_in), t)
    w_sum = total(w_parts[0], w_near, w_far)

    def placed(vector, axis):
        spread = jnp.expand_dims(vector, axis)
        mask = (jnp.arange(n_in) == t).reshape([-1 if a == axis else 1 for a in range(spread.ndim)])
        return jnp.where(mask, spread, 0.0).reshape(-1)

    grad_own = cotangent.astype(F32)
    vec_grads = [
        sums_one[0],
        sums_one[1],
        sums_two[0],
        sums_two[1],
        placed(grad_b_qkv[0].reshape(3, cols), 1),
        jnp.sum(grad_own, axis=0),
        placed(grad_b_in[0].reshape(n_dp, n_out, r_ff), 1),
    ]
    vec_grads = [v.astype(BF16).reshape(n_dp, n_in, n_out, -1) for v in vec_grads]
    vec_grads = jnp.stack([jnp.pad(v, ((0, 0), (0, 0), (0, 0), (0, lanes - v.shape[-1]))) for v in vec_grads], axis=3)
    spare = r_w * per_row - len(vectors)
    vec_grads = jnp.pad(vec_grads, ((0, 0), (0, 0), (0, 0), (0, spare), (0, 0)))
    vec_grads = jnp.transpose(vec_grads, (0, 2, 1, 3, 4)).reshape(n_g, n_in * r_w, 128)
    if layout.aligned:
        first_grads = qkv_grads(layout, n1, da, vec_grads)
    else:
        first_grads = jnp.concatenate([by_owner(dot_tn(n1, da).astype(BF16)), vec_grads], axis=2)
    first_grads = lax.psum_scatter(first_grads, G_AXES, scatter_dimension=0, tiled=False)

    qkv_part = exchange_in(first_grads.reshape(n_in, r_w, 3 * cols + 128), t)
    in_part = in_part.reshape(n_in, r_w, n_dp, n_out, r_ff)
    grad_w_in = jnp.transpose(in_part, (1, 2, 0, 3, 4)).reshape(r_w, ff).astype(F32)
    grad_w_fc2 = second_grads[n_in * r_w : n_in * r_w + r_ff].astype(F32)
    back_home = [(b, a) for a, b in home]
    out_part = second_grads[n_in * r_w + r_ff :]
    grad_w_out = lax.ppermute(out_part, ALL_AXES, back_home).astype(F32)
    qkv_grad = jnp.transpose(qkv_part[:, :, : 3 * cols].reshape(n_in, r_w, 3, cols), (1, 2, 0, 3))
    grad_w_qkv = qkv_grad.reshape(r_w, 3 * width).astype(F32)
    vec_part = jnp.sum(qkv_part[:, :, 3 * cols :].astype(F32), axis=0).reshape(r_w * per_row, lanes)
    vec_out = [vec_part[i, :size] for i, size in enumerate(sizes)]

    centred = own - jnp.mean(own, axis=-1, keepdims=True)
    own_rstd = lax.rsqrt(jnp.mean(centred * centred, axis=-1, keepdims=True) + EPS)
    own_hat = centred * own_rstd
    mean_w = jnp.mean(w_sum, axis=-1, keepdims=True)
    mean_wx = jnp.mean(w_sum * own_hat, axis=-1, keepdims=True)
    grad_tokens = grad_own + own_rstd * (w_sum - mean_w - own_hat * mean_wx)
    return (
        mixed,
        grad_tokens,
        vec_out[0],
        vec_out[1],
        vec_out[2],
        vec_out[3],
        grad_w_qkv,
        vec_out[4],
        grad_w_out,
        grad_w_in,
        vec_out[6],
        grad_w_fc2,
        vec_out[5],
    )


def solution(mesh):
    n_dp, n_ctx = mesh.shape["dp"], mesh.shape["ctx"]
    split = Mesh(mesh.devices.reshape(n_dp, GROUP_IN, n_ctx // GROUP_IN), ALL_AXES)
    mat, vec, group = P(ALL_AXES, None), P(ALL_AXES), P("dp", None)
    return jax.shard_map(
        body,
        mesh=split,
        in_specs=(mat, group, group, vec, vec, vec, vec, mat, vec, mat, mat, vec, mat, vec, mat),
        out_specs=(mat, mat, vec, vec, vec, vec, mat, vec, mat, mat, vec, mat, vec),
        check_vma=False,
    )
```
